32 devices in a mesh: seq: 8 (over y, x, core), head: 4 (over z).
Axes of the slice: x: 2, y: 2, z: 4, core: 2. Of those that a mesh axis runs over, the one named last changes fastest.
Arguments:
- tokens: bfloat16 [1, 8192, 768], P(None, 'seq'), may hold values from -6 to 6
- starts: int32 [1, 8192], P(None, 'seq'), may hold values from 0 to 1, as said below
- norm_in_gain: float32 [768], replicated, may hold values from 0.1 to 1.9
- inner_weight: bfloat16 [768, 2, 1536], P(None, None, 'head'), may hold values from -0.21875 to 0.21875
- state_weight: bfloat16 [768, 2, 128], P(None, None, 'head'), may hold values from -0.21875 to 0.21875
- step_weight: bfloat16 [768, 24], P(None, 'head'), may hold values from -0.21875 to 0.21875
- conv_inner: bfloat16 [4, 1536], P(None, 'head'), may hold values from -3 to 3
- conv_inner_bias: bfloat16 [1536], P('head'), may hold values from -3 to 3
- conv_state: bfloat16 [4, 2, 128], P(None, None, 'head'), may hold values from -3 to 3
- conv_state_bias: bfloat16 [2, 128], P(None, 'head'), may hold values from -3 to 3
- step_bias: float32 [24], P('head'), may hold values from -7 to -2
- decay_log: float32 [24], P('head'), may hold values from -7 to 0.5
- skip_gain: float32 [24], P('head'), may hold values from 0.5 to 1.5
- norm_out_gain: float32 [1536], P('head'), may hold values from 0.1 to 1.9
- out_weight: bfloat16 [1536, 768], P('head'), may hold values from -0.15625 to 0.15625
- cotangent: bfloat16 [1, 8192, 768], P(None, 'seq'), may hold values from -6 to 6
Outputs:
- output: bfloat16 [1, 8192, 768], P(None, 'seq', 'head')
- grad_tokens: float32 [1, 8192, 768], P(None, 'seq', 'head')
- grad_norm_in_gain: float32 [768], P('head')
- grad_inner_weight: float32 [768, 2, 1536], P(None, None, 'head')
- grad_state_weight: float32 [768, 2, 128], P(None, None, 'head')
- grad_step_weight: float32 [768, 24], P(None, 'head')
- grad_conv_inner: float32 [4, 1536], P(None, 'head')
- grad_conv_inner_bias: float32 [1536], P('head')
- grad_conv_state: float32 [4, 2, 128], P(None, None, 'head')
- grad_conv_state_bias: float32 [2, 128], P(None, 'head')
- grad_step_bias: float32 [24], P('head')
- grad_decay_log: float32 [24], P('head')
- grad_skip_gain: float32 [24], P('head')
- grad_norm_out_gain: float32 [1536], P('head')
- grad_out_weight: float32 [1536, 768], P('head')
The draws below stay inside these ranges and needn't reach their ends.
Inputs may be any that keep to these rules, and one draw needn't show every extreme that they name: `starts`: 1 marks the first token of a document; the first token of every sequence is marked, and in every draw one sequence has marks only within its first 512 and its last 512 positions.
All inputs are finite; a program needn't handle non-finite values.
Results may differ from the reference program's by a relative error of at most 0.0085.
The reference program's roundings to bfloat16 on the way count: a program that leaves them out, or rounds other values in their place, can miss the bound.
Values may be sent and summed in bfloat16 or wider, within the bound.
No kernel may reach another device: no remote copies, remote signals or barrier semaphores. Data moves between devices by JAX's collectives and lax.ppermute only.
A program may use at most 192 MiB of HBM per device.

```python
import jax
import jax.numpy as jnp
from jax import lax

D = 768
H = 24
P_SIZE = 64
N = 128
K = 4
GROUP = 256
SEQ_LEN = 8192
DI = 1536
SEQS = 1
SEG = 1024


def draw_starts(key, part):
    key = jax.random.fold_in(key, 11)
    pick_key, flag_key, edge_key = jax.random.split(key, 3)
    marked = (jax.random.randint(flag_key, (SEQS, SEQ_LEN), 0, 16) == 0).astype(jnp.int32)
    edge_marks = (jax.random.randint(edge_key, (SEQS, SEQ_LEN), 0, 4) == 0).astype(jnp.int32)
    position = jnp.arange(SEQ_LEN)[None, :]
    margin = max(SEG // 2, 1)
    in_edges = (position < margin) | (position >= SEQ_LEN - margin)
    chosen = jax.random.randint(pick_key, (), 0, SEQS)
    row_ids = jnp.arange(SEQS)[:, None]
    long_row = jnp.where(in_edges, edge_marks, 0)
    marked = jnp.where(row_ids == chosen, long_row, marked)
    leading = position == 0
    return jnp.where(leading, 1, marked).astype(jnp.int32)


def shard_levels(rng, extent, cuts, least, largest):
    loudness, own = 1.0, jax.random.fold_in(rng, 6)
    for dim, parts in cuts:
        draws = jnp.exp(jax.random.uniform(jax.random.fold_in(own, dim), (parts,), jnp.float32, least / len(cuts), largest / len(cuts)))
        loudness = loudness * jnp.repeat(draws, extent[dim] // parts).reshape([-1 if axis == dim else 1 for axis in range(len(extent))])
    return loudness


def scatter_about(own_key, shape, scale, most, cuts=(), held_as=jnp.bfloat16):
    gain = shard_levels(own_key, shape, cuts, -0.22, 0.18) if cuts else 1.0
    values = jax.random.normal(own_key, shape, jnp.float32) * scale * gain
    return jnp.minimum(jnp.maximum(values, -most), most).astype(held_as)


def setup_inputs(seed: int = 0) -> dict:
    key_list = jax.random.split(jax.random.key(seed), 17)
    tokens = scatter_about(key_list[0], (SEQS, SEQ_LEN, D), 1.0, 6.0, ((1, 8),))
    starts = draw_starts(jax.random.fold_in(key_list[16], 71), 0)
    norm_in_gain = jnp.clip(1.0 + 0.18 * jax.random.normal(key_list[2], (D,), jnp.float32), 0.1, 1.9)
    inner_weight = scatter_about(key_list[3], (D, 2, DI), D ** -0.5, 0.21875, ((2, 4),))
    state_weight = scatter_about(key_list[4], (D, 2, N), D ** -0.5, 0.21875, ((2, 4),))
    step_weight = scatter_about(key_list[5], (D, H), D ** -0.5, 0.21875, ((1, 4),))
    conv_inner = scatter_about(key_list[6], (K, DI), K ** -0.5, 3.0, ((1, 4),))
    conv_inner_bias = scatter_about(key_list[7], (DI,), 0.3, 3.0, ((0, 4),))
    conv_state = scatter_about(key_list[8], (K, 2, N), K ** -0.5, 3.0, ((2, 4),))
    conv_state_bias = scatter_about(key_list[9], (2, N), 0.3, 3.0, ((1, 4),))
    step_bias = jnp.clip(-7.0 + 5.0 * jax.random.uniform(key_list[10], (H,), jnp.float32) ** shard_levels(key_list[10], (H,), ((0, 4),), -0.2, 0.2), -7.0, -2.0)
    decay_log = jnp.clip(-7.0 + 7.5 * jax.random.uniform(key_list[11], (H,), jnp.float32) ** shard_levels(key_list[11], (H,), ((0, 4),), -0.2, 0.2), -7.0, 0.5)
    skip_gain = jnp.clip(0.5 + 1.0 * jax.random.uniform(key_list[12], (H,), jnp.float32) ** shard_levels(key_list[12], (H,), ((0, 4),), -0.2, 0.2), 0.5, 1.5)
    norm_out_gain = jnp.clip(1.0 + 0.18 * jax.random.normal(key_list[13], (DI,), jnp.float32), 0.1, 1.9)
    out_weight = scatter_about(key_list[14], (DI, D), DI ** -0.5, 0.15625, ((0, 4),))
    cotangent = scatter_about(key_list[15], (SEQS, SEQ_LEN, D), 1.0, 6.0, ((1, 8),))
    return {"tokens": tokens, "starts": starts, "norm_in_gain": norm_in_gain, "inner_weight": inner_weight, "state_weight": state_weight, "step_weight": step_weight, "conv_inner": conv_inner, "conv_inner_bias": conv_inner_bias, "conv_state": conv_state, "conv_state_bias": conv_state_bias, "step_bias": step_bias, "decay_log": decay_log, "skip_gain": skip_gain, "norm_out_gain": norm_out_gain, "out_weight": out_weight, "cotangent": cotangent}


EPSILON = 1e-05
HIGHEST = lax.Precision.HIGHEST

@jax.custom_vjp
def low(v):
    return lax.optimization_barrier(v.astype(jnp.bfloat16)).astype(jnp.float32)

@jax.custom_vjp
def low_back(v):
    return v

def low_keep(v):
    return (low(v), None)

def low_pass(kept, grad):
    return (grad,)

def back_keep(v):
    return (v, None)

def back_low(kept, grad):
    return (low(grad),)
low.defvjp(low_keep, low_pass)
low_back.defvjp(back_keep, back_low)

def sigmoid_linear(tensor):
    return tensor * jax.nn.sigmoid(tensor)

def causal_conv(values, kernel, offset_bias, keeping):
    length = values.shape[0]
    summed = offset_bias + kernel[K - 1] * values
    running = jnp.ones_like(keeping)
    for offset in range(1, K):
        shifted = jnp.concatenate([jnp.ones((offset - 1,), jnp.float32), keeping[:length - offset + 1]])
        running = running * shifted
        earlier_rows = jnp.concatenate([jnp.zeros((offset, values.shape[1]), jnp.float32), values[:length - offset]])
        summed = summed + kernel[K - 1 - offset] * earlier_rows * running[:, None]
    return summed

def group_core(carried, inputs, step_sizes, log_rates, state_in, read_out, marked):
    length = marked.shape[0]
    cumulative = jnp.cumsum(log_rates, axis=0)
    counts = jnp.cumsum(marked)
    position = jnp.arange(length)
    connected = (position[:, None] >= position[None, :]) & (counts[:, None] == counts[None, :])
    log_gaps = jnp.where(connected[:, :, None], cumulative[:, None, :] - cumulative[None, :, :], 0.0)
    decays = jnp.exp(log_gaps) * connected[:, :, None].astype(jnp.float32)
    scores = jnp.dot(read_out, state_in.T, precision=HIGHEST)
    mixing = scores[:, :, None] * decays * step_sizes[None, :, :]
    inside = jnp.einsum('ijh,jhp->ihp', mixing, inputs, precision=HIGHEST)
    living = (counts == 0).astype(jnp.float32)
    reaching = jnp.exp(cumulative) * living[:, None]
    outside = reaching[:, :, None] * jnp.einsum('in,hpn->ihp', read_out, carried, precision=HIGHEST)
    ending = (counts == counts[-1]).astype(jnp.float32)
    weights = jnp.exp(cumulative[-1][None, :] - cumulative) * ending[:, None] * step_sizes
    fresh_state = jnp.einsum('jh,jhp,jn->hpn', weights, inputs, state_in, precision=HIGHEST)
    fading = jnp.exp(cumulative[-1]) * living[-1]
    return (fading[:, None, None] * carried + fresh_state, inside + outside)

def layer(token_row, marked, params):
    norm_in_gain, inner_weight, state_weight, step_weight, conv_inner, conv_inner_bias, conv_state, conv_state_bias, step_bias, decay_log, skip_gain, norm_out_gain, out_weight = params
    length = token_row.shape[0]
    keeping = 1.0 - marked.astype(jnp.float32)
    inv_scale = lax.rsqrt(lax.optimization_barrier(jnp.mean(token_row * token_row, axis=-1, keepdims=True)) + EPSILON)
    normed_in = low(token_row * inv_scale * norm_in_gain)
    projected = jnp.einsum('td,dkc->tkc', normed_in, inner_weight, precision=HIGHEST)
    inner_pre = low_back(low(projected[:, 0]))
    gate_pre = low_back(projected[:, 1])
    state_pre = low_back(low(jnp.einsum('td,dkn->tkn', normed_in, state_weight, precision=HIGHEST)))
    step_raw = low_back(jnp.dot(normed_in, step_weight, precision=HIGHEST))
    inner_act = low(sigmoid_linear(causal_conv(inner_pre, conv_inner, conv_inner_bias, keeping)))
    state_act = low(sigmoid_linear(causal_conv(state_pre.reshape(length, 2 * N), conv_state.reshape(K, 2 * N), conv_state_bias.reshape(2 * N), keeping))).reshape(length, 2, N)
    step_sizes = jax.nn.softplus(step_raw + step_bias)
    decay_rate = -jnp.exp(decay_log)
    inputs = inner_act.reshape(length, H, P_SIZE)
    group_count = length // GROUP
    pieces = (inputs.reshape(group_count, GROUP, H, P_SIZE), step_sizes.reshape(group_count, GROUP, H), (step_sizes * decay_rate).reshape(group_count, GROUP, H), state_act[:, 0].reshape(group_count, GROUP, N), state_act[:, 1].reshape(group_count, GROUP, N), marked.reshape(group_count, GROUP))

    def advance(carried, piece):
        return group_core(carried, piece[0], piece[1], piece[2], piece[3], piece[4], piece[5])
    final_state, mixed = lax.scan(jax.checkpoint(advance), jnp.zeros((H, P_SIZE, N), jnp.float32), pieces)
    mixer_out = mixed.reshape(length, H, P_SIZE) + skip_gain[:, None] * inputs
    gated = mixer_out.reshape(length, DI) * sigmoid_linear(gate_pre)
    out_scale = lax.rsqrt(lax.optimization_barrier(jnp.mean(gated * gated, axis=-1, keepdims=True)) + EPSILON)
    normed_out = low(gated * out_scale * norm_out_gain)
    return token_row + jnp.dot(normed_out, out_weight, precision=HIGHEST)

def reference(tokens, starts, norm_in_gain, inner_weight, state_weight, step_weight, conv_inner, conv_inner_bias, conv_state, conv_state_bias, step_bias, decay_log, skip_gain, norm_out_gain, out_weight, cotangent):
    params = tuple((weight_arg.astype(jnp.float32) for weight_arg in (norm_in_gain, inner_weight, state_weight, step_weight, conv_inner, conv_inner_bias, conv_state, conv_state_bias, step_bias, decay_log, skip_gain, norm_out_gain, out_weight)))

    def one_row(running_sum, pieces):
        token_row, marked, cotangent_row = pieces
        layer_value, pullback = jax.vjp(lambda row_value, param_values: layer(row_value, marked, param_values), token_row.astype(jnp.float32), params)
        grad_row, grad_params = pullback(cotangent_row.astype(jnp.float32))
        running_sum = jax.tree.map(lambda former, latter: former + latter, running_sum, grad_params)
        return (running_sum, (layer_value.astype(jnp.bfloat16), grad_row))
    initial = jax.tree.map(jnp.zeros_like, params)
    gradients, (outputs, grad_tokens) = lax.scan(one_row, initial, (tokens, starts, cotangent))
    return (outputs, grad_tokens, gradients[0], gradients[1], gradients[2], gradients[3], gradients[4], gradients[5], gradients[6], gradients[7], gradients[8], gradients[9], gradients[10], gradients[11], gradients[12])
```

```python
import functools

import jax
import jax.numpy as jnp
from jax import lax
from jax.experimental import pallas as pl
from jax.experimental.pallas import tpu as pltpu
from jax.sharding import PartitionSpec as P

K = 4
GROUP = 256
DI = 1536
WIDTH = 64
LANES = 128
EDGE = 16
EPSILON = 1e-05
HIGHEST = lax.Precision.HIGHEST
F32 = jnp.float32
BF16 = jnp.bfloat16
FAR = -1e30
PARAMS = pltpu.CompilerParams(
    dimension_semantics=("arbitrary", "arbitrary"), vmem_limit_bytes=50 * 2**20
)


def rounded(tensor):
    return tensor.astype(BF16)


def dot(a, b, exact=False):
    return jnp.dot(a, b, preferred_element_type=F32, precision=HIGHEST if exact else None)


def dot_nt(a, b, exact=False):
    return lax.dot_general(
        a, b, (((1,), (1,)), ((), ())), preferred_element_type=F32,
        precision=HIGHEST if exact else None,
    )


def dot_tn(a, b, exact=False):
    return lax.dot_general(
        a, b, (((0,), (0,)), ((), ())), preferred_element_type=F32,
        precision=HIGHEST if exact else None,
    )


def iota(shape, dim):
    return lax.broadcasted_iota(jnp.int32, shape, dim)


def halves(tensor):
    high = rounded(tensor)
    return high, rounded(tensor - high.astype(F32))


def expand(tensor, channels):
    both = jnp.concatenate(halves(tensor), axis=1)
    table = iota((2 * LANES, channels), 1) // WIDTH == iota((2 * LANES, channels), 0) % LANES
    return dot(both, table.astype(F32).astype(BF16))


def collect(tensor):
    channels = tensor.shape[1]
    table = iota((channels, LANES), 0) // WIDTH == iota((channels, LANES), 1)
    table = table.astype(F32).astype(BF16)
    high, low = halves(tensor)
    return dot(high, table) + dot(low, table)


def expand_row(row, channels):
    return expand(jnp.broadcast_to(row, (8, LANES)), channels)[:1]


def collect_row(row):
    return collect(jnp.broadcast_to(row, (8, row.shape[1])))[:1]


def triangle(compare):
    return compare(iota((GROUP, GROUP), 0), iota((GROUP, GROUP), 1)).astype(F32).astype(BF16)


def running_counts(marked):
    return dot(marked.astype(BF16), triangle(lambda i, j: i <= j))


def fade_of(cum, counts):
    return jnp.exp(cum[GROUP - 1 :, :]) * (counts[:1, GROUP - 1 :] == 0).astype(F32)


def pack_state(ref, state, fade):
    ref[:LANES, :] = state
    ref[LANES:, :] = jnp.broadcast_to(fade, (8, fade.shape[1]))


def fold_states(pieces):
    state = jnp.zeros((LANES, pieces[0].shape[1]), F32)
    for piece in reversed(pieces):
        state = piece[LANES : LANES + 1, :] * state + piece[:LANES, :]
    return state


def rms_scale(tokens):
    return lax.rsqrt(jnp.mean(tokens * tokens, axis=-1, keepdims=True) + EPSILON)


def head_parts(channels):
    for start in range(0, channels, LANES):
        width = min(LANES, channels - start)
        yield start, width, [start // WIDTH + i for i in range(width // WIDTH)]


def project_kernel(tok, gain, win, wst, hp, normed, xpre, gate, spre, step, cum):
    channels = xpre.shape[-1]
    tokens = tok[...].astype(F32)
    row = rounded(tokens * rms_scale(tokens) * gain[...])
    normed[...] = row
    product = dot(row, win[...])
    xpre[...] = rounded(product[:, :channels])
    gate[...] = product[:, channels:]
    raw = dot(row, wst[...]) + hp[0:1, :]
    sizes = jax.nn.softplus(raw)
    spre[...] = raw
    step[...] = sizes
    rates = sizes * -jnp.exp(hp[1:2, :])
    lower = triangle(lambda i, j: i >= j)
    high, rest = rounded(rates), rates - rounded(rates).astype(F32)
    middle, low = halves(rest)
    cum[...] = dot(lower, high) + dot(lower, middle) + dot(lower, low)


def convolve(ext, taps, runs):
    summed = taps[K : K + 1, :] + taps[K - 1 : K, :] * ext[pl.ds(EDGE, GROUP), :]
    for lag in range(1, K):
        summed = summed + (
            taps[K - 1 - lag : K - lag, :] * ext[pl.ds(EDGE - lag, GROUP), :]
        ) * runs[lag - 1]
    return summed


def edge_rows(halo, gain, width):
    tokens = halo[:, :width].astype(F32)
    return tokens, rounded(tokens * rms_scale(tokens) * gain[...])


def forward_kernel(count, *refs):
    pieces = refs[:count]
    (
        marked, normed, xpre, step, cum, win, halo, gain, ci,
        yin, xact, bc, spre, fresh, fades, message, halo_x, halo_s, run_out, ws, cs,
        ext_x, ext_s, ext_k, state, total,
    ) = refs[count:]
    group = pl.program_id(1)
    channels = xpre.shape[-1]
    width = normed.shape[-1]
    own = pieces[0].shape[0] // 2

    @pl.when((group == 0) & (pl.program_id(0) == 0))
    def _():
        for place, piece in enumerate(pieces):
            for kind in range(2):
                row = (kind * count + place) * own
                ws[row : row + own, :] = piece[kind * own : (kind + 1) * own, :width]
        taps = jnp.concatenate(
            [p[kind * own : (kind + 1) * own, width:] for kind in range(2) for p in pieces], axis=0
        )
        cs[...] = taps.astype(F32).T[:8]

    @pl.when(group == 0)
    def _():
        _, row = edge_rows(halo, gain, width)
        edge_x = rounded(dot(row, win[:, :channels]))
        edge_s = rounded(dot_nt(row, ws[...]))
        halo_x[...] = edge_x
        halo_s[...] = edge_s
        ext_x[pl.ds(0, EDGE), :] = edge_x.astype(F32)
        ext_s[pl.ds(0, EDGE), :] = edge_s.astype(F32)
        ext_k[pl.ds(0, EDGE), :] = 1.0 - halo[:, width:].astype(F32)
        state[...] = jnp.zeros_like(state)
        total[...] = jnp.ones_like(total)

    @pl.when(group > 0)
    def _():
        ext_x[pl.ds(0, EDGE), :] = ext_x[pl.ds(GROUP, EDGE), :]
        ext_s[pl.ds(0, EDGE), :] = ext_s[pl.ds(GROUP, EDGE), :]
        ext_k[pl.ds(0, EDGE), :] = ext_k[pl.ds(GROUP, EDGE), :]

    counts = running_counts(marked[...])
    counts_column = counts.T[:, :1]
    run1 = 1.0 - marked[...].T[:, :1]
    ext_k[pl.ds(EDGE, GROUP), :] = jnp.broadcast_to(run1, (GROUP, LANES))
    run2 = run1 * ext_k[pl.ds(EDGE - 1, GROUP), :1]
    run3 = run2 * ext_k[pl.ds(EDGE - 2, GROUP), :1]
    runs = (run1, run2, run3)
    lane = iota((GROUP, LANES), 1)
    run_out[...] = jnp.where(lane == 0, run1, jnp.where(lane == 1, run2, run3))
    state_pre = rounded(dot_nt(normed[...], ws[...]))
    spre[...] = state_pre
    ext_s[pl.ds(EDGE, GROUP), :] = state_pre.astype(F32)
    ext_x[pl.ds(EDGE, GROUP), :] = xpre[...].astype(F32)
    conv_x = convolve(ext_x, ci, runs)
    conv_s = convolve(ext_s, cs, runs)
    x = rounded(conv_x * jax.nn.sigmoid(conv_x))
    both = rounded(conv_s * jax.nn.sigmoid(conv_s))
    xact[...] = x
    bc[...] = both
    half = both.shape[1] // 2
    b, c = both[:, :half], both[:, half:]
    cums = cum[...]
    causal = iota((GROUP, GROUP), 0) >= iota((GROUP, GROUP), 1)
    mask = jnp.where(causal & (counts_column == counts[:1]), 0.0, FAR)
    scores = dot_nt(c, b)
    weighted = x.astype(F32) * expand(step[...], channels)
    scaled = rounded(weighted)
    cum_rows = cums.T
    for start, size, heads in head_parts(channels):
        part = scaled[:, start : start + size]
        results = []
        for head in heads:
            decay = jnp.exp(cums[:, head : head + 1] - cum_rows[head : head + 1, :] + mask)
            results.append(dot(rounded(scores * decay), part))
        if len(results) == 2:
            results = [jnp.where(iota((GROUP, size), 1) < WIDTH, results[0], results[1])]
        yin[:, start : start + size] = results[0]
    ending = (counts_column == counts[:1, GROUP - 1 :]).astype(F32)
    reach_end = jnp.exp(cums[GROUP - 1 :, :] - cums) * ending
    new = dot_tn(b, rounded(weighted * expand(reach_end, channels)))
    fresh[...] = new
    fade = expand_row(fade_of(cums, counts), channels)
    fades[...] = jnp.broadcast_to(fade, (8, channels))
    state[...] = fade * state[...] + new
    total[...] = total[...] * fade

    @pl.when(group == pl.num_programs(1) - 1)
    def _():
        pack_state(message, state[...], total[0:1, :])


def mix_kernel(count, *refs):
    pieces = refs[:count]
    (
        yin, x, c, gate, dn, cum, marked, gain, hp, fresh, fades,
        mixer, sums, states, state,
    ) = refs[count:]
    channels = x.shape[-1]

    @pl.when(pl.program_id(1) == 0)
    def _():
        state[...] = fold_states(pieces)

    counts = running_counts(marked[...])
    living = (counts.T[:, :1] == 0).astype(F32)
    now = state[...]
    states[...] = now
    reach = expand(jnp.exp(cum[...]) * living, channels)
    skip = expand_row(hp[2:3, :], channels)
    high, low = halves(now)
    reads = c[...]
    mixed = yin[...] + reach * (dot(reads, high) + dot(reads, low)) + skip * x[...].astype(F32)
    mixer[...] = mixed
    gates = gate[...]
    gated = mixed * (gates * jax.nn.sigmoid(gates))
    square = jnp.sum(gated * gated, axis=1, keepdims=True)
    cross = jnp.sum(gated * (dn[...] * gain[...]), axis=1, keepdims=True)
    lane = iota((GROUP, LANES), 1)
    sums[...] = jnp.where(lane == 0, square, cross).T[:8]
    state[...] = fades[0:1, :] * now + fresh[...]


def gate_kernel(count, *refs):
    pieces = refs[:count]
    (
        mixer, gate, dn, x, c, cum, marked, gain, hp, fades,
        dy, dgate, normed_out, entering, message, grad_gain, grad_skip, state, total,
    ) = refs[count:]
    channels = x.shape[-1]
    last = pl.program_id(1) == 0

    @pl.when(last & (pl.program_id(0) == 0))
    def _():
        grad_gain[...] = jnp.zeros_like(grad_gain)
        grad_skip[...] = jnp.zeros_like(grad_skip)

    @pl.when(last)
    def _():
        state[...] = jnp.zeros_like(state)
        total[...] = jnp.ones_like(total)

    sums = pieces[0][...]
    for piece in pieces[1:]:
        sums = sums + piece[...]
    columns = sums.T
    scale = lax.rsqrt(columns[:, 0:1] / DI + EPSILON)
    pull = scale * scale * scale * (columns[:, 1:2] / DI)
    counts = running_counts(marked[...])
    living = (counts.T[:, :1] == 0).astype(F32)
    mixed = mixer[...]
    gates = gate[...]
    squash = jax.nn.sigmoid(gates)
    act = gates * squash
    gated = mixed * act
    norm_grad = dn[...]
    grad_gated = scale * (norm_grad * gain[...]) - gated * pull
    down = grad_gated * act
    dy[...] = down
    dgate[...] = rounded(grad_gated * mixed * (squash * (1.0 + gates * (1.0 - squash))))
    scaled = gated * scale
    normed_out[...] = rounded(scaled * gain[...])
    grad_gain[...] += jnp.sum(norm_grad * scaled, axis=0, keepdims=True)
    grad_skip[...] += jnp.sum(down * x[...].astype(F32), axis=0, keepdims=True)
    reach = expand(jnp.exp(cum[...]) * living, channels)
    new = dot_tn(c[...], rounded(reach * down))
    entering[...] = new
    fade = fades[0:1, :]
    state[...] = fade * state[...] + new
    total[...] = total[...] * fade

    @pl.when(pl.program_id(1) == pl.num_programs(1) - 1)
    def _():
        pack_state(message, state[...], total[0:1, :])


def store_parts(refs, tensor, me):
    width = tensor.shape[1]
    own = width // len(refs)
    turned = rounded(pltpu.roll(tensor, (len(refs) - me) % len(refs) * own, 1))
    for part, ref in enumerate(refs):
        ref[...] = turned[:, part * own : (part + 1) * own]


def out_kernel(parts, me, normed_out, cot, dgate, normed, wout, win, gain, skip, back, grads, *branch):
    channels = wout.shape[0]
    width = wout.shape[1]

    @pl.when((pl.program_id(1) == 0) & (pl.program_id(0) == 0))
    def _():
        grads[...] = jnp.zeros_like(grads)
        grads[2 * channels : 2 * channels + 1, :channels] = gain[...]
        grads[2 * channels + 1 : 2 * channels + 2, :channels] = skip[...]

    store_parts(branch, dot(normed_out[...], wout[...]), me[0])
    grads[:channels, :] += dot_tn(normed_out[...], cot[...])
    grads[channels : 2 * channels, :] += dot_tn(dgate[...], normed[...])
    back[...] = dot_nt(dgate[...], win[:, channels:])


def token_grad(tokens, gain, down):
    scale = rms_scale(tokens)
    pulled = down * gain
    inner = jnp.mean(pulled * tokens, axis=-1, keepdims=True)
    grad = scale * pulled - tokens * (scale * scale * scale * inner)
    return grad, jnp.sum(down * tokens * scale, axis=0, keepdims=True)


def deconvolve(ext, buffers, taps, runs, grad_out, grad_taps):
    rows = GROUP + EDGE
    grad_taps[K : K + 1, :] += jnp.sum(grad_out, axis=0, keepdims=True)
    result = None
    for lag in range(K):
        masked = grad_out if lag == 0 else grad_out * runs[lag - 1]
        buffer = buffers.at[lag]
        buffer[pl.ds(EDGE, GROUP), :] = masked
        tap = K - 1 - lag
        grad_taps[tap : tap + 1, :] += jnp.sum(
            masked * ext[pl.ds(EDGE - lag, GROUP), :], axis=0, keepdims=True
        )
        piece = taps[tap : tap + 1, :] * buffer[pl.ds(lag, rows), :]
        result = piece if result is None else result + piece
        buffer[pl.ds(EDGE + GROUP, 8), :] = masked[:8]
    return rounded(result)


def swish_slope(tensor):
    squash = jax.nn.sigmoid(tensor)
    return squash * (1.0 + tensor * (1.0 - squash))


def backward_kernel(start_call, end_call, count, parts, *refs):
    pieces, refs = refs[:count], refs[count:]
    carried, refs = (refs[:0], refs) if start_call else (refs[:6], refs[6:])
    (
        me, tok, halo, marked, normed, xpre, xprev, halo_x, spre, sprev, halo_s, xact, bc, yin, dy,
        back, step, cum, raw, run_in, states, entering, fades, win, ws, wst, hp, ci, cs, gain,
    ), refs = refs[:30], refs[30:]
    gtok, refs = refs[:parts], refs[parts:]
    if end_call:
        (packed, *rest), refs = refs[: 1 + 2 * parts], refs[1 + 2 * parts :]
        edge_out, state_out = rest[:parts], rest[parts:]
    else:
        carry_out, refs = refs[:6], refs[6:]
    ext_x, ext_s, buf_x, buf_s, state, grad_x, grad_s, grad_misc, grad_ci, grad_cs = refs
    channels = xact.shape[-1]
    width = tok.shape[-1]
    half = bc.shape[-1] // 2
    order = pl.program_id(1)
    row_id = pl.program_id(0)
    closing = order == pl.num_programs(1) - 1
    sums = (grad_x, grad_s, grad_misc, grad_ci, grad_cs)

    @pl.when((order == 0) & (row_id == 0))
    def _():
        if start_call:
            for ref in sums:
                ref[...] = jnp.zeros_like(ref)
        else:
            grad_x[...] = carried[3][:channels]
            grad_s[...] = carried[3][channels : channels + 2 * half]
            grad_misc[...] = carried[3][channels + 2 * half :]
            grad_ci[...] = carried[4][...]
            grad_cs[...] = carried[5][...]

    @pl.when(order == 0)
    def _():
        for buf in (buf_x, buf_s):
            buf[...] = jnp.zeros_like(buf)
        if start_call:
            state[...] = fold_states(pieces)
        else:
            state[...] = carried[0][...]
            buf_x[:, pl.ds(EDGE + GROUP, 8), :] = carried[1][...]
            buf_s[:, pl.ds(EDGE + GROUP, 8), :] = carried[2][...]

    first_group = closing if end_call else False
    ext_x[pl.ds(EDGE, GROUP), :] = xpre[...].astype(F32)
    ext_s[pl.ds(EDGE, GROUP), :] = spre[...].astype(F32)
    before_x, before_s = xprev[...].astype(F32), sprev[...].astype(F32)
    if end_call:
        before_x = jnp.where(first_group, halo_x[...].astype(F32), before_x)
        before_s = jnp.where(first_group, halo_s[...].astype(F32), before_s)
    ext_x[pl.ds(0, EDGE), :] = before_x
    ext_s[pl.ds(0, EDGE), :] = before_s

    counts = running_counts(marked[...])
    counts_column = counts.T[:, :1]
    runs = [run_in[:, lag : lag + 1] for lag in range(K - 1)]
    living = (counts_column == 0).astype(F32)
    x = xact[...].astype(F32)
    both = bc[...]
    b, c = both[:, :half], both[:, half:]
    cums = cum[...]
    cum_rows = cums.T
    steps = step[...]
    step_wide = expand(steps, channels)
    weighted = x * step_wide
    scaled = rounded(weighted)
    down = dy[...]
    down_low = rounded(down)
    causal = iota((GROUP, GROUP), 0) <= iota((GROUP, GROUP), 1)
    mask = jnp.where(causal & (counts_column == counts[:1]), 0.0, FAR)
    scores = dot_nt(b, c)
    grad_scores = jnp.zeros((GROUP, GROUP), F32)
    inside = []
    for start, size, heads in head_parts(channels):
        part = scaled[:, start : start + size]
        slope = down_low[:, start : start + size]
        lane = iota((GROUP, size), 1)
        results = []
        for place, head in enumerate(heads):
            decay = jnp.exp(cum_rows[head : head + 1, :] - cums[:, head : head + 1] + mask)
            results.append(dot(rounded(scores * decay), slope))
            own = part
            if len(heads) == 2:
                keep = (lane < WIDTH) if place == 0 else (lane >= WIDTH)
                own = jnp.where(keep, part, jnp.zeros_like(part))
            grad_scores = grad_scores + dot_nt(own, slope) * decay
        if len(results) == 2:
            results = [jnp.where(lane < WIDTH, results[0], results[1])]
        inside.append(results[0])
    inside = jnp.concatenate(inside, axis=1) if len(inside) > 1 else inside[0]

    later = state[...]
    later_high, later_low = halves(later)
    now = states[...]
    now_high, now_low = halves(now)
    ending = (counts_column == counts[:1, GROUP - 1 :]).astype(F32)
    reach_end = expand(jnp.exp(cums[GROUP - 1 :, :] - cums) * ending, channels)
    reach = expand(jnp.exp(cums) * living, channels)
    arriving = reach_end * (dot(b, later_high) + dot(b, later_low))
    grad_weighted = inside + arriving
    reached = reach * down
    outside = reached * (dot(c, now_high) + dot(c, now_low))
    fade = fades[0:1, :]
    fade_grad = collect_row(fade * jnp.sum(later * now, axis=0, keepdims=True))
    per_position = collect(
        down_low.astype(F32) * yin[...] - scaled.astype(F32) * inside + outside
    )
    per_ending = collect(weighted * arriving)
    direct = collect(x * grad_weighted)
    position_high, position_low = halves(per_position)
    ending_high, ending_low = halves(per_ending)
    upper = triangle(lambda i, j: i <= j)
    under = triangle(lambda i, j: i > j)
    grad_rate = (
        dot(upper, position_high) + dot(upper, position_low)
        + dot(under, ending_high) + dot(under, ending_low) + fade_grad
    )
    rate = -jnp.exp(hp[1:2, :])
    grad_pre = (direct + rate * grad_rate) * jax.nn.sigmoid(raw[...])
    grad_raw = rounded(grad_pre)
    skip = expand_row(hp[2:3, :], channels)
    grad_inputs = step_wide * grad_weighted + skip * down
    low_scores = rounded(grad_scores)
    ended = rounded(weighted * reach_end)
    reached_low = rounded(reached)
    grad_b = dot(low_scores, c) + dot_nt(ended, later_high) + dot_nt(ended, later_low)
    grad_c = dot_tn(low_scores, b) + dot_nt(reached_low, now_high) + dot_nt(reached_low, now_low)
    state[...] = fade * later + entering[...]

    conv_x = convolve(ext_x, ci, runs)
    grad_x_out = grad_inputs * swish_slope(conv_x)
    conv_s = convolve(ext_s, cs, runs)
    grad_s_out = jnp.concatenate([grad_b, grad_c], axis=1) * swish_slope(conv_s)
    back_x = deconvolve(ext_x, buf_x, ci, runs, grad_x_out, grad_ci)
    back_s = deconvolve(ext_s, buf_s, cs, runs, grad_s_out, grad_cs)
    row = normed[...]
    main_x, main_s = back_x[EDGE:], back_s[EDGE:]
    grad_x[...] += dot_tn(main_x, row)
    grad_s[...] += dot_tn(main_s, row)
    grad_normed = (
        back[...] + dot_nt(main_x, win[:, :channels]) + dot(main_s, ws[...])
        + dot_nt(grad_raw, wst[...])
    )
    grad, gain_part = token_grad(tok[...].astype(F32), gain[...], grad_normed)
    grad_misc[0:8, :] += dot_tn(grad_raw, row)[:8]
    grad_misc[8:9, :] += gain_part
    grad_misc[9:10, :LANES] += jnp.sum(grad_pre, axis=0, keepdims=True)
    grad_misc[10:11, :LANES] += rate * jnp.sum(steps * grad_rate, axis=0, keepdims=True)
    store_parts(gtok, grad, me[0])

    if not end_call:
        @pl.when(closing)
        def _():
            carry_out[0][...] = state[...]
            carry_out[1][...] = buf_x[:, pl.ds(EDGE + GROUP, 8), :]
            carry_out[2][...] = buf_s[:, pl.ds(EDGE + GROUP, 8), :]

            @pl.when(row_id == pl.num_programs(0) - 1)
            def _():
                carry_out[3][:channels] = grad_x[...]
                carry_out[3][channels : channels + 2 * half] = grad_s[...]
                carry_out[3][channels + 2 * half :] = grad_misc[...]
                carry_out[4][...] = grad_ci[...]
                carry_out[5][...] = grad_cs[...]
        return

    @pl.when(closing)
    def _():
        tokens, edge_row = edge_rows(halo, gain, width)
        edge_x, edge_s = back_x[:EDGE], back_s[:EDGE]
        grad_x[...] += dot_tn(edge_x, edge_row)
        grad_s[...] += dot_tn(edge_s, edge_row)
        edge_grad = dot_nt(edge_x, win[:, :channels]) + dot(edge_s, ws[...])
        grad, gain_part = token_grad(tokens, gain[...], edge_grad)
        grad_misc[8:9, :] += gain_part
        everything = grad_misc[8:9, :]
        high = everything.astype(BF16).astype(F32)
        place = iota((EDGE, 1), 0)
        final = row_id == pl.num_programs(0) - 1
        nothing = jnp.zeros_like(high)
        high, rest = jnp.where(final, high, nothing), jnp.where(final, everything - high, nothing)
        edge = jnp.where(place == 0, high, jnp.where(place == 1, rest, grad))
        store_parts(edge_out, edge, me[0])

        @pl.when(final)
        def _():
            def padded(block):
                if block.shape[1] == width:
                    return block
                blank = jnp.zeros((8, width - block.shape[1]), F32)
                return jnp.concatenate([block, blank], axis=1)

            def both_halves(block):
                whole = padded(block)
                upper_half = whole.astype(BF16).astype(F32)
                return rounded(jnp.concatenate([upper_half, whole - upper_half], axis=0))

            packed[:channels, :] = rounded(grad_x[...])
            packed[channels : channels + EDGE, :] = rounded(grad_misc[...])
            packed[channels + EDGE : channels + 2 * EDGE, :] = both_halves(grad_ci[...])
            own = half // parts
            taps = grad_cs[...]
            for part, ref in enumerate(state_out):
                lo, hi = part * own, (part + 1) * own
                ref[:own, :] = rounded(grad_s[lo:hi, :])
                ref[own : 2 * own, :] = rounded(grad_s[half + lo : half + hi, :])
                ref[2 * own :, :] = both_halves(
                    jnp.concatenate([taps[:, lo:hi], taps[:, half + lo : half + hi]], axis=1)
                )


def ring(axis, distance):
    count = lax.axis_size(axis)
    return [(i, (i + distance) % count) for i in range(count)]


def shifted(block, axis, distance):
    devices = range(lax.axis_size(axis))
    return lax.ppermute(block, axis, [(i - distance, i) for i in devices if i - distance in devices])


def passed_on(parts, axis):
    total = parts[0].astype(F32)
    for distance, part in enumerate(parts[1:], 1):
        total = total + lax.ppermute(part, axis, ring(axis, distance)).astype(F32)
    return total


def all_sum(whole, axis):
    count = lax.axis_size(axis)
    chunk = whole.shape[0] // count
    parts = lax.all_to_all(whole.reshape(count, chunk, -1), axis, 0, 0, tiled=True)
    own = rounded(jnp.sum(parts.astype(F32), axis=0))
    return lax.all_gather(own, axis, axis=0, tiled=True).astype(F32)


def on_device(
    tokens, starts, norm_in_gain, inner_weight, state_weight, step_weight, conv_inner,
    conv_inner_bias, conv_state, conv_state_bias, step_bias, decay_log, skip_gain,
    norm_out_gain, out_weight, cotangent,
):
    rows, length, width = tokens.shape
    head_count = step_weight.shape[1]
    channels = inner_weight.shape[2]
    own_state = state_weight.shape[2]
    seq_count, head_devices = lax.axis_size("seq"), lax.axis_size("head")
    groups = length // GROUP
    grid = (rows, groups)
    states = 2 * own_state * head_devices
    own_width = width // head_devices
    me = lax.axis_index("head").reshape(1)

    def sds(shape, dtype=F32):
        return jax.ShapeDtypeStruct(shape, dtype)

    def whole(shape):
        return pl.BlockSpec(shape, lambda r, g: (0,) * len(shape))

    def place(g, reverse):
        return groups - 1 - g if reverse else g

    def block(cols, reverse=False, part=0):
        return pl.BlockSpec((None, GROUP, cols), lambda r, g: (r, place(g, reverse), part))

    def per_row(height, cols):
        return pl.BlockSpec((None, height, cols), lambda r, g: (r, 0, 0))

    def per_group(height, cols, reverse=False):
        return pl.BlockSpec(
            (None, None, height, cols), lambda r, g: (r, place(g, reverse), 0, 0)
        )

    scalar = pl.BlockSpec(memory_space=pltpu.SMEM)
    halo_width = width + LANES
    tail = jnp.concatenate(
        [
            tokens[:, length - EDGE :],
            jnp.broadcast_to(starts[:, length - EDGE :, None], (rows, EDGE, LANES)).astype(BF16),
        ],
        axis=2,
    )
    halo = shifted(tail, "seq", 1)
    state_own = jnp.concatenate(
        [
            state_weight, conv_state, conv_state_bias[None],
            jnp.zeros((LANES - K - 1, 2, own_state), BF16),
        ],
        axis=0,
    ).transpose(1, 2, 0).reshape(2 * own_state, width + LANES)
    found = [state_own] + [
        lax.ppermute(state_own, "head", ring("head", d)) for d in range(1, head_devices)
    ]

    gain_in = norm_in_gain[None]
    gain_out = norm_out_gain[None]
    win = inner_weight.reshape(width, 2 * channels)
    wst = jnp.pad(step_weight, ((0, 0), (0, LANES - head_count)))
    hp = jnp.pad(
        jnp.stack([step_bias, decay_log, skip_gain]), ((0, 5), (0, LANES - head_count))
    )
    ci = jnp.pad(
        jnp.concatenate([conv_inner, conv_inner_bias[None]], axis=0).astype(F32), ((0, 3), (0, 0))
    )
    marked = jnp.broadcast_to(
        starts.astype(F32).reshape(rows, groups, 1, GROUP), (rows, groups, 8, GROUP)
    )

    def act(cols, dtype=F32):
        return sds((rows, length, cols), dtype)

    normed, xpre, gate, raw, step, cum = pl.pallas_call(
        project_kernel,
        grid=grid,
        in_specs=[
            block(width), whole((1, width)), whole((width, 2 * channels)),
            whole((width, LANES)), whole((8, LANES)),
        ],
        out_specs=[
            block(width), block(channels), block(channels), block(LANES), block(LANES),
            block(LANES),
        ],
        out_shape=[
            act(width, BF16), act(channels, BF16), act(channels), act(LANES), act(LANES),
            act(LANES),
        ],
        compiler_params=PARAMS,
        name="project",
    )(tokens, gain_in, win, wst, hp)
    dn = jnp.einsum("rsd,cd->rsc", cotangent, out_weight, preferred_element_type=F32)

    (
        yin, xact, bc, spre, fresh, fades, message, halo_x, halo_s, run_all, ws, cs,
    ) = pl.pallas_call(
        functools.partial(forward_kernel, len(found)),
        grid=grid,
        in_specs=[whole((2 * own_state, width + LANES))] * len(found) + [
            per_group(8, GROUP), block(width), block(channels), block(LANES), block(LANES),
            whole((width, 2 * channels)), per_row(EDGE, halo_width), whole((1, width)),
            whole((8, channels)),
        ],
        out_specs=[
            block(channels), block(channels), block(states), block(states),
            per_group(LANES, channels), per_group(8, channels), per_row(LANES + 8, channels),
            per_row(EDGE, channels), per_row(EDGE, states), block(LANES),
            whole((states, width)), whole((8, states)),
        ],
        out_shape=[
            act(channels), act(channels, BF16), act(states, BF16), act(states, BF16),
            sds((rows, groups, LANES, channels)), sds((rows, groups, 8, channels)),
            sds((rows, LANES + 8, channels)), sds((rows, EDGE, channels), BF16),
            sds((rows, EDGE, states), BF16), act(LANES), sds((states, width), BF16),
            sds((8, states)),
        ],
        scratch_shapes=[
            pltpu.VMEM((GROUP + EDGE, channels), F32), pltpu.VMEM((GROUP + EDGE, states), F32),
            pltpu.VMEM((GROUP + EDGE, LANES), F32),
            pltpu.VMEM((LANES, channels), F32), pltpu.VMEM((8, channels), F32),
        ],
        compiler_params=PARAMS,
        name="forward",
    )(*found, marked, normed, xpre, step, cum, win, halo, gain_in, ci)

    arrived = [shifted(message, "seq", d) for d in range(1, seq_count)]
    mixer, sums, entry_states = pl.pallas_call(
        functools.partial(mix_kernel, len(arrived)),
        grid=grid,
        in_specs=[per_row(LANES + 8, channels)] * len(arrived) + [
            block(channels), block(channels), block(states // 2, part=1), block(channels),
            block(channels), block(LANES), per_group(8, GROUP), whole((1, channels)),
            whole((8, LANES)), per_group(LANES, channels), per_group(8, channels),
        ],
        out_specs=[block(channels), per_group(8, GROUP), per_group(LANES, channels)],
        out_shape=[
            act(channels), sds((rows, groups, 8, GROUP)), sds((rows, groups, LANES, channels)),
        ],
        scratch_shapes=[pltpu.VMEM((LANES, channels), F32)],
        compiler_params=PARAMS,
        name="mix",
    )(*arrived, yin, xact, bc, gate, dn, cum, marked, gain_out, hp, fresh, fades)

    sums_all = [sums] + [
        lax.ppermute(sums, "head", ring("head", d)) for d in range(1, head_devices)
    ]
    dy, dgate, normed_out, entering, back_message, grad_gain_out, grad_skip = pl.pallas_call(
        functools.partial(gate_kernel, len(sums_all)),
        grid=grid,
        in_specs=[per_group(8, GROUP, True)] * len(sums_all) + [
            block(channels, True), block(channels, True), block(channels, True),
            block(channels, True), block(states // 2, True, 1), block(LANES, True),
            per_group(8, GROUP, True), whole((1, channels)), whole((8, LANES)),
            per_group(8, channels, True),
        ],
        out_specs=[
            block(channels, True), block(channels, True), block(channels, True),
            per_group(LANES, channels, True), per_row(LANES + 8, channels),
            whole((1, channels)), whole((1, channels)),
        ],
        out_shape=[
            act(channels), act(channels, BF16), act(channels, BF16),
            sds((rows, groups, LANES, channels)), sds((rows, LANES + 8, channels)),
            sds((1, channels)), sds((1, channels)),
        ],
        scratch_shapes=[pltpu.VMEM((LANES, channels), F32), pltpu.VMEM((8, channels), F32)],
        compiler_params=PARAMS,
        name="gate",
    )(*sums_all, mixer, gate, dn, xact, bc, cum, marked, gain_out, hp, fades)

    returned = [shifted(back_message, "seq", -d) for d in range(1, seq_count)]
    back, early, *branch = pl.pallas_call(
        functools.partial(out_kernel, head_devices),
        grid=grid,
        in_specs=[
            scalar, block(channels), block(width), block(channels), block(width),
            whole((channels, width)), whole((width, 2 * channels)), whole((1, channels)),
            whole((1, channels)),
        ],
        out_specs=[block(width), whole((2 * channels + 8, width))]
        + [block(own_width)] * head_devices,
        out_shape=[act(width), sds((2 * channels + 8, width))]
        + [act(own_width, BF16)] * head_devices,
        compiler_params=PARAMS,
        name="out",
    )(me, normed_out, cotangent, dgate, normed, out_weight, win, grad_gain_out, grad_skip)

    column = lax.axis_index("head") * own_width
    own_tokens = lax.dynamic_slice_in_dim(tokens, column, own_width, 2).astype(F32)
    output = rounded(own_tokens + passed_on(branch, "head"))
    early = lax.psum(early, "seq")

    late_rows = channels + 3 * EDGE + 2 * own_state + EDGE
    chunk = -(-late_rows // (seq_count * EDGE)) * EDGE
    packed_rows = channels + 2 * EDGE
    piece_rows = 2 * own_state + EDGE

    def backward_call(start_call, end_call, offset, steps, carried):
        step_size = GROUP // EDGE

        def at(g):
            return offset + steps - 1 - g

        def tile(cols):
            return pl.BlockSpec((None, GROUP, cols), lambda r, g: (r, at(g), 0))

        def before(cols):
            return pl.BlockSpec(
                (None, EDGE, cols), lambda r, g: (r, jnp.maximum(at(g) * step_size - 1, 0), 0)
            )

        def group_tile(height, cols):
            return pl.BlockSpec((None, None, height, cols), lambda r, g: (r, at(g), 0, 0))

        carry_specs = [
            per_row(LANES, channels),
            pl.BlockSpec((None, K, 8, channels), lambda r, g: (r, 0, 0, 0)),
            pl.BlockSpec((None, K, 8, states), lambda r, g: (r, 0, 0, 0)),
            whole((channels + states + EDGE, width)), whole((8, channels)), whole((8, states)),
        ]
        carry_shapes = [
            sds((rows, LANES, channels)), sds((rows, K, 8, channels)), sds((rows, K, 8, states)),
            sds((channels + states + EDGE, width)), sds((8, channels)), sds((8, states)),
        ]
        local = pl.BlockSpec((None, GROUP, own_width), lambda r, g: (r, steps - 1 - g, 0))
        out_specs = [local] * head_devices
        out_shape = [sds((rows, steps * GROUP, own_width), BF16)] * head_devices
        if end_call:
            out_specs += [whole((packed_rows, width))]
            out_specs += [per_row(EDGE, own_width)] * head_devices
            out_specs += [whole((piece_rows, width))] * head_devices
            out_shape += [sds((packed_rows, width), BF16)]
            out_shape += [sds((rows, EDGE, own_width), BF16)] * head_devices
            out_shape += [sds((piece_rows, width), BF16)] * head_devices
        else:
            out_specs += carry_specs
            out_shape += carry_shapes
        lead = returned if start_call else []
        return pl.pallas_call(
            functools.partial(backward_kernel, start_call, end_call, len(lead), head_devices),
            grid=(rows, steps),
            in_specs=[per_row(LANES + 8, channels)] * len(lead)
            + ([] if start_call else carry_specs)
            + [
                scalar, tile(width), per_row(EDGE, halo_width), group_tile(8, GROUP), tile(width),
                tile(channels), before(channels), per_row(EDGE, channels), tile(states),
                before(states), per_row(EDGE, states), tile(channels), tile(states),
                tile(channels), tile(channels), tile(width), tile(LANES), tile(LANES),
                tile(LANES), tile(LANES), group_tile(LANES, channels),
                group_tile(LANES, channels), group_tile(8, channels),
                whole((width, 2 * channels)), whole((states, width)), whole((width, LANES)),
                whole((8, LANES)), whole((8, channels)), whole((8, states)), whole((1, width)),
            ],
            out_specs=out_specs,
            out_shape=out_shape,
            scratch_shapes=[
                pltpu.VMEM((GROUP + EDGE, channels), F32),
                pltpu.VMEM((GROUP + EDGE, states), F32),
                pltpu.VMEM((K, GROUP + 2 * EDGE, channels), F32),
                pltpu.VMEM((K, GROUP + 2 * EDGE, states), F32),
                pltpu.VMEM((LANES, channels), F32),
                pltpu.VMEM((channels, width), F32), pltpu.VMEM((states, width), F32),
                pltpu.VMEM((EDGE, width), F32), pltpu.VMEM((8, channels), F32),
                pltpu.VMEM((8, states), F32),
            ],
            compiler_params=PARAMS,
            name="backward",
        )(
            *lead, *carried, me, tokens, halo, marked, normed, xpre, xpre, halo_x, spre, spre,
            halo_s, xact, bc, yin, dy, back, step, cum, raw, run_all, entry_states, entering,
            fades, win, ws, wst, hp, ci, cs, gain_in,
        )

    first = groups // 2
    if first:
        outs = backward_call(True, False, first, groups - first, [])
        token_sums = [passed_on(outs[:head_devices], "head")]
        outs = backward_call(False, True, 0, first, outs[head_devices:])
    else:
        token_sums = []
        outs = backward_call(True, True, 0, groups, [])
    gtok, packed = outs[:head_devices], outs[head_devices]
    edge_parts = outs[head_devices + 1 : 2 * head_devices + 1]
    state_parts = outs[2 * head_devices + 1 :]

    state_total = state_parts[0].astype(F32)
    for d in range(1, head_devices):
        state_total = state_total + lax.ppermute(
            state_parts[d], "head", ring("head", -d)
        ).astype(F32)
    edge = passed_on(edge_parts, "head")
    token_sums = [passed_on(gtok, "head")] + token_sums
    own_cot = lax.dynamic_slice_in_dim(cotangent, column, own_width, 2).astype(F32)
    from_next = shifted(edge, "seq", -1)[:, EDGE - K + 1 :]
    padding = jnp.zeros((rows, length - K + 1, own_width), F32)
    grad_tokens = (
        own_cot + jnp.concatenate(token_sums, axis=1)
        + jnp.concatenate([padding, from_next], axis=1)
    )
    gain_row = (edge[rows - 1, 0] + edge[rows - 1, 1])[None]
    gain_high = gain_row.astype(BF16).astype(F32)
    gain_rows = jnp.pad(
        jnp.concatenate([gain_high, gain_row - gain_high]),
        ((0, EDGE - 2), (0, width - own_width)),
    )
    taps = state_total[2 * own_state : 2 * own_state + 8] + state_total[2 * own_state + 8 :]
    taps_high = taps.astype(BF16).astype(F32)
    late = jnp.concatenate(
        [
            packed, rounded(state_total[: 2 * own_state]), rounded(taps_high),
            rounded(taps - taps_high), rounded(gain_rows),
            jnp.zeros((chunk * seq_count - late_rows, width), BF16),
        ],
        axis=0,
    )
    late = all_sum(late, "seq")

    def take(start, count):
        return late[start : start + count]

    grad_inner = jnp.stack([take(0, channels), early[channels : 2 * channels]]).transpose(2, 0, 1)
    misc = take(channels, EDGE)
    conv = take(channels + EDGE, 8) + take(channels + EDGE + 8, 8)
    base = packed_rows
    grad_state = take(base, 2 * own_state).reshape(2, own_state, width).transpose(2, 0, 1)
    base += 2 * own_state
    taps = (take(base, 8) + take(base + 8, 8))[: K + 1, : 2 * own_state]
    taps = taps.reshape(K + 1, 2, own_state)
    gain = take(base + EDGE, 1) + take(base + EDGE + 1, 1)
    skip = early[2 * channels + 1, :channels].reshape(head_count, WIDTH).sum(axis=1)
    return (
        output, grad_tokens, gain[0, :own_width], grad_inner, grad_state,
        misc[:head_count].T, conv[:K, :channels], conv[K, :channels], taps[:K], taps[K],
        misc[9, :head_count], misc[10, :head_count], skip, early[2 * channels, :channels],
        early[:channels],
    )


def solution(mesh):
    return jax.shard_map(
        on_device,
        mesh=mesh,
        in_specs=(
            P(None, "seq", None), P(None, "seq"), P(), P(None, None, "head"),
            P(None, None, "head"), P(None, "head"), P(None, "head"), P("head"),
            P(None, None, "head"), P(None, "head"), P("head"), P("head"), P("head"), P("head"),
            P("head", None), P(None, "seq", None),
        ),
        out_specs=(
            P(None, "seq", "head"), P(None, "seq", "head"), P("head"), P(None, None, "head"),
            P(None, None, "head"), P(None, "head"), P(None, "head"), P("head"),
            P(None, None, "head"), P(None, "head"), P("head"), P("head"), P("head"), P("head"),
            P("head", None),
        ),
        check_vma=False,
    )
```

```python
import functools

import jax
import jax.numpy as jnp
from jax import lax
from jax.experimental import pallas as pl
from jax.experimental.pallas import tpu as pltpu
from jax.sharding import PartitionSpec as P

K = 4
GROUP = 256
DI = 1536
WIDTH = 64
LANES = 128
EDGE = 16
EPSILON = 1e-05
HIGHEST = lax.Precision.HIGHEST
F32 = jnp.float32
BF16 = jnp.bfloat16
FAR = -1e30
PARAMS = pltpu.CompilerParams(
    dimension_semantics=("arbitrary", "arbitrary"), vmem_limit_bytes=62 * 2**20
)


def cost(microseconds):
    return pl.CostEstimate(
        flops=int(microseconds * 1e9), bytes_accessed=int(microseconds * 1e5), transcendentals=0
    )


def rounded(tensor):
    return tensor.astype(BF16)


def dot(a, b, exact=False):
    return jnp.dot(a, b, preferred_element_type=F32, precision=HIGHEST if exact else None)


def dot_nt(a, b, exact=False):
    return lax.dot_general(
        a, b, (((1,), (1,)), ((), ())), preferred_element_type=F32,
        precision=HIGHEST if exact else None,
    )


def dot_tn(a, b, exact=False):
    return lax.dot_general(
        a, b, (((0,), (0,)), ((), ())), preferred_element_type=F32,
        precision=HIGHEST if exact else None,
    )


def iota(shape, dim):
    return lax.broadcasted_iota(jnp.int32, shape, dim)


def halves(tensor):
    high = rounded(tensor)
    return high, rounded(tensor - high.astype(F32))


def expand(tensor, channels):
    both = jnp.concatenate(halves(tensor), axis=1)
    table = iota((2 * LANES, channels), 1) // WIDTH == iota((2 * LANES, channels), 0) % LANES
    return dot(both, table.astype(F32).astype(BF16))


def collect(tensor):
    channels = tensor.shape[1]
    table = iota((channels, LANES), 0) // WIDTH == iota((channels, LANES), 1)
    table = table.astype(F32).astype(BF16)
    high, low = halves(tensor)
    return dot(high, table) + dot(low, table)


def expand_row(row, channels):
    return expand(jnp.broadcast_to(row, (8, LANES)), channels)[:1]


def collect_row(row):
    return collect(jnp.broadcast_to(row, (8, row.shape[1])))[:1]


def triangle(compare):
    return compare(iota((GROUP, GROUP), 0), iota((GROUP, GROUP), 1)).astype(F32).astype(BF16)


def running_counts(marked):
    return dot(marked.astype(BF16), triangle(lambda i, j: i <= j))


def fade_of(cum, counts):
    return jnp.exp(cum[GROUP - 1 :, :]) * (counts[:1, GROUP - 1 :] == 0).astype(F32)


def pack_state(ref, state, fade):
    ref[:LANES, :] = state
    ref[LANES:, :] = jnp.broadcast_to(fade, (8, fade.shape[1]))


def fold_states(pieces):
    state = jnp.zeros((LANES, pieces[0].shape[1]), F32)
    for piece in reversed(pieces):
        state = piece[LANES : LANES + 1, :] * state + piece[:LANES, :]
    return state


def rms_scale(tokens):
    return lax.rsqrt(jnp.mean(tokens * tokens, axis=-1, keepdims=True) + EPSILON)


def head_parts(channels):
    for start in range(0, channels, LANES):
        width = min(LANES, channels - start)
        yield start, width, [start // WIDTH + i for i in range(width // WIDTH)]


def project_kernel(tok, gain, win, wst, hp, normed, xpre, gate, spre, step, cum):
    channels = xpre.shape[-1]
    tokens = tok[...].astype(F32)
    row = rounded(tokens * rms_scale(tokens) * gain[...])
    normed[...] = row
    product = dot(row, win[...])
    xpre[...] = rounded(product[:, :channels])
    gate[...] = product[:, channels:]
    raw = dot(row, wst[...]) + hp[0:1, :]
    sizes = jax.nn.softplus(raw)
    spre[...] = raw
    step[...] = sizes
    rates = sizes * -jnp.exp(hp[1:2, :])
    lower = triangle(lambda i, j: i >= j)
    high, rest = rounded(rates), rates - rounded(rates).astype(F32)
    middle, low = halves(rest)
    cum[...] = dot(lower, high) + dot(lower, middle) + dot(lower, low)


def convolve(ext, taps, runs):
    summed = taps[K : K + 1, :] + taps[K - 1 : K, :] * ext[pl.ds(EDGE, GROUP), :]
    for lag in range(1, K):
        summed = summed + (
            taps[K - 1 - lag : K - lag, :] * ext[pl.ds(EDGE - lag, GROUP), :]
        ) * runs[lag - 1]
    return summed


def edge_rows(halo, gain, width):
    tokens = halo[:, :width].astype(F32)
    return tokens, rounded(tokens * rms_scale(tokens) * gain[...])


def forward_kernel(count, *refs):
    pieces = refs[:count]
    (
        marked, normed, xpre, step, cum, win, halo, gain, ci,
        yin, xact, bc, spre, fresh, fades, message, halo_x, halo_s, run_out, ws, cs,
        ext_x, ext_s, ext_k, state, total,
    ) = refs[count:]
    group = pl.program_id(1)
    channels = xpre.shape[-1]
    width = normed.shape[-1]
    own = pieces[0].shape[0] // 2

    @pl.when((group == 0) & (pl.program_id(0) == 0))
    def _():
        for place, piece in enumerate(pieces):
            for kind in range(2):
                row = (kind * count + place) * own
                ws[row : row + own, :] = piece[kind * own : (kind + 1) * own, :width]
        taps = jnp.concatenate(
            [p[kind * own : (kind + 1) * own, width:] for kind in range(2) for p in pieces], axis=0
        )
        cs[...] = taps.astype(F32).T[:8]

    @pl.when(group == 0)
    def _():
        _, row = edge_rows(halo, gain, width)
        edge_x = rounded(dot(row, win[:, :channels]))
        edge_s = rounded(dot_nt(row, ws[...]))
        halo_x[...] = edge_x
        halo_s[...] = edge_s
        ext_x[pl.ds(0, EDGE), :] = edge_x.astype(F32)
        ext_s[pl.ds(0, EDGE), :] = edge_s.astype(F32)
        ext_k[pl.ds(0, EDGE), :] = 1.0 - halo[:, width:].astype(F32)
        state[...] = jnp.zeros_like(state)
        total[...] = jnp.ones_like(total)

    @pl.when(group > 0)
    def _():
        ext_x[pl.ds(0, EDGE), :] = ext_x[pl.ds(GROUP, EDGE), :]
        ext_s[pl.ds(0, EDGE), :] = ext_s[pl.ds(GROUP, EDGE), :]
        ext_k[pl.ds(0, EDGE), :] = ext_k[pl.ds(GROUP, EDGE), :]

    counts = running_counts(marked[...])
    counts_column = counts.T[:, :1]
    run1 = 1.0 - marked[...].T[:, :1]
    ext_k[pl.ds(EDGE, GROUP), :] = jnp.broadcast_to(run1, (GROUP, LANES))
    run2 = run1 * ext_k[pl.ds(EDGE - 1, GROUP), :1]
    run3 = run2 * ext_k[pl.ds(EDGE - 2, GROUP), :1]
    runs = (run1, run2, run3)
    lane = iota((GROUP, LANES), 1)
    run_out[...] = jnp.where(lane == 0, run1, jnp.where(lane == 1, run2, run3))
    state_pre = rounded(dot_nt(normed[...], ws[...]))
    spre[...] = state_pre
    ext_s[pl.ds(EDGE, GROUP), :] = state_pre.astype(F32)
    ext_x[pl.ds(EDGE, GROUP), :] = xpre[...].astype(F32)
    conv_x = convolve(ext_x, ci, runs)
    conv_s = convolve(ext_s, cs, runs)
    x = rounded(conv_x * jax.nn.sigmoid(conv_x))
    both = rounded(conv_s * jax.nn.sigmoid(conv_s))
    xact[...] = x
    bc[...] = both
    half = both.shape[1] // 2
    b, c = both[:, :half], both[:, half:]
    cums = cum[...]
    causal = iota((GROUP, GROUP), 0) >= iota((GROUP, GROUP), 1)
    mask = jnp.where(causal & (counts_column == counts[:1]), 0.0, FAR)
    scores = dot_nt(c, b)
    weighted = x.astype(F32) * expand(step[...], channels)
    scaled = rounded(weighted)
    cum_rows = cums.T
    for start, size, heads in head_parts(channels):
        part = scaled[:, start : start + size]
        results = []
        for head in heads:
            decay = jnp.exp(cums[:, head : head + 1] - cum_rows[head : head + 1, :] + mask)
            results.append(dot(rounded(scores * decay), part))
        if len(results) == 2:
            results = [jnp.where(iota((GROUP, size), 1) < WIDTH, results[0], results[1])]
        yin[:, start : start + size] = results[0]
    ending = (counts_column == counts[:1, GROUP - 1 :]).astype(F32)
    reach_end = jnp.exp(cums[GROUP - 1 :, :] - cums) * ending
    new = dot_tn(b, rounded(weighted * expand(reach_end, channels)))
    fresh[...] = new
    fade = expand_row(fade_of(cums, counts), channels)
    fades[...] = jnp.broadcast_to(fade, (8, channels))
    state[...] = fade * state[...] + new
    total[...] = total[...] * fade

    @pl.when(group == pl.num_programs(1) - 1)
    def _():
        pack_state(message, state[...], total[0:1, :])


def mix_kernel(count, *refs):
    pieces = refs[:count]
    (
        yin, x, c, gate, dn, cum, marked, gain, hp, fresh, fades,
        mixer, sums, states, state,
    ) = refs[count:]
    channels = x.shape[-1]

    @pl.when(pl.program_id(1) == 0)
    def _():
        state[...] = fold_states(pieces)

    counts = running_counts(marked[...])
    living = (counts.T[:, :1] == 0).astype(F32)
    now = state[...]
    states[...] = now
    reach = expand(jnp.exp(cum[...]) * living, channels)
    skip = expand_row(hp[2:3, :], channels)
    high, low = halves(now)
    reads = c[...]
    mixed = yin[...] + reach * (dot(reads, high) + dot(reads, low)) + skip * x[...].astype(F32)
    mixer[...] = mixed
    gates = gate[...]
    gated = mixed * (gates * jax.nn.sigmoid(gates))
    square = jnp.sum(gated * gated, axis=1, keepdims=True)
    cross = jnp.sum(gated * (dn[...] * gain[...]), axis=1, keepdims=True)
    lane = iota((GROUP, LANES), 1)
    sums[...] = jnp.where(lane == 0, square, cross).T[:8]
    state[...] = fades[0:1, :] * now + fresh[...]


def gate_kernel(count, *refs):
    pieces = refs[:count]
    (
        mixer, gate, dn, x, c, cum, marked, gain, hp, fades,
        dy, dgate, normed_out, entering, message, grad_gain, grad_skip, state, total,
    ) = refs[count:]
    channels = x.shape[-1]
    last = pl.program_id(1) == 0

    @pl.when(last & (pl.program_id(0) == 0))
    def _():
        grad_gain[...] = jnp.zeros_like(grad_gain)
        grad_skip[...] = jnp.zeros_like(grad_skip)

    @pl.when(last)
    def _():
        state[...] = jnp.zeros_like(state)
        total[...] = jnp.ones_like(total)

    sums = pieces[0][...]
    for piece in pieces[1:]:
        sums = sums + piece[...]
    columns = sums.T
    scale = lax.rsqrt(columns[:, 0:1] / DI + EPSILON)
    pull = scale * scale * scale * (columns[:, 1:2] / DI)
    counts = running_counts(marked[...])
    living = (counts.T[:, :1] == 0).astype(F32)
    mixed = mixer[...]
    gates = gate[...]
    squash = jax.nn.sigmoid(gates)
    act = gates * squash
    gated = mixed * act
    norm_grad = dn[...]
    grad_gated = scale * (norm_grad * gain[...]) - gated * pull
    down = grad_gated * act
    dy[...] = down
    dgate[...] = rounded(grad_gated * mixed * (squash * (1.0 + gates * (1.0 - squash))))
    scaled = gated * scale
    normed_out[...] = rounded(scaled * gain[...])
    grad_gain[...] += jnp.sum(norm_grad * scaled, axis=0, keepdims=True)
    grad_skip[...] += jnp.sum(down * x[...].astype(F32), axis=0, keepdims=True)
    reach = expand(jnp.exp(cum[...]) * living, channels)
    new = dot_tn(c[...], rounded(reach * down))
    entering[...] = new
    fade = fades[0:1, :]
    state[...] = fade * state[...] + new
    total[...] = total[...] * fade

    @pl.when(pl.program_id(1) == pl.num_programs(1) - 1)
    def _():
        pack_state(message, state[...], total[0:1, :])


def store_parts(refs, tensor, me):
    width = tensor.shape[1]
    own = width // len(refs)
    turned = rounded(pltpu.roll(tensor, (len(refs) - me) % len(refs) * own, 1))
    blocks = [turned[:, part * own : (part + 1) * own] for part in range(len(refs))]
    if len(refs) == 4:
        odd = me % 2 == 1
        swapped = [jnp.where(odd, blocks[4 - part], blocks[part]) for part in (1, 3)]
        blocks = [blocks[0], swapped[0], blocks[2], swapped[1]]
    for block, ref in zip(blocks, refs):
        ref[...] = block


def out_kernel(parts, me, normed_out, cot, dgate, normed, wout, win, gain, skip, back, grads, *branch):
    channels = wout.shape[0]
    width = wout.shape[1]

    @pl.when((pl.program_id(1) == 0) & (pl.program_id(0) == 0))
    def _():
        grads[...] = jnp.zeros_like(grads)
        grads[2 * channels : 2 * channels + 1, :channels] = gain[...]
        grads[2 * channels + 1 : 2 * channels + 2, :LANES] = collect_row(skip[...])

    store_parts(branch, dot(normed_out[...], wout[...]), me[0])
    grads[:channels, :] += dot_tn(normed_out[...], cot[...])
    grads[channels : 2 * channels, :] += dot_tn(dgate[...], normed[...])
    back[...] = dot_nt(dgate[...], win[:, channels:])


def token_grad(tokens, gain, down):
    scale = rms_scale(tokens)
    pulled = down * gain
    inner = jnp.mean(pulled * tokens, axis=-1, keepdims=True)
    grad = scale * pulled - tokens * (scale * scale * scale * inner)
    return grad, jnp.sum(down * tokens * scale, axis=0, keepdims=True)


def deconvolve(ext, buffers, taps, runs, grad_out, grad_taps):
    rows = GROUP + EDGE
    grad_taps[K : K + 1, :] += jnp.sum(grad_out, axis=0, keepdims=True)
    result = None
    for lag in range(K):
        masked = grad_out if lag == 0 else grad_out * runs[lag - 1]
        buffer = buffers.at[lag]
        buffer[pl.ds(EDGE, GROUP), :] = masked
        tap = K - 1 - lag
        grad_taps[tap : tap + 1, :] += jnp.sum(
            masked * ext[pl.ds(EDGE - lag, GROUP), :], axis=0, keepdims=True
        )
        piece = taps[tap : tap + 1, :] * buffer[pl.ds(lag, rows), :]
        result = piece if result is None else result + piece
        buffer[pl.ds(EDGE + GROUP, 8), :] = masked[:8]
    return rounded(result)


def swish_slope(tensor):
    squash = jax.nn.sigmoid(tensor)
    return squash * (1.0 + tensor * (1.0 - squash))


def backward_kernel(start_call, end_call, count, parts, *refs):
    pieces, refs = refs[:count], refs[count:]
    carried, refs = (refs[:0], refs) if start_call else (refs[:6], refs[6:])
    (
        me, tok, halo, marked, normed, xpre, xprev, halo_x, spre, sprev, halo_s, xact, bc, yin, dy,
        back, step, cum, raw, run_in, states, entering, fades, win, ws, wst, hp, ci, cs, gain,
    ), refs = refs[:30], refs[30:]
    gtok, refs = refs[:parts], refs[parts:]
    if end_call:
        (packed, *rest), refs = refs[: 1 + 2 * parts], refs[1 + 2 * parts :]
        edge_out, state_out = rest[:parts], rest[parts:]
    else:
        carry_out, refs = refs[:6], refs[6:]
    ext_x, ext_s, buf_x, buf_s, state, grad_x, grad_s, grad_misc, grad_ci, grad_cs = refs
    channels = xact.shape[-1]
    width = tok.shape[-1]
    half = bc.shape[-1] // 2
    order = pl.program_id(1)
    row_id = pl.program_id(0)
    closing = order == pl.num_programs(1) - 1
    sums = (grad_x, grad_s, grad_misc, grad_ci, grad_cs)

    @pl.when((order == 0) & (row_id == 0))
    def _():
        if start_call:
            for ref in sums:
                ref[...] = jnp.zeros_like(ref)
        else:
            grad_x[...] = carried[3][:channels]
            grad_s[...] = carried[3][channels : channels + 2 * half]
            grad_misc[...] = carried[3][channels + 2 * half :]
            grad_ci[...] = carried[4][...]
            grad_cs[...] = carried[5][...]

    @pl.when(order == 0)
    def _():
        for buf in (buf_x, buf_s):
            buf[...] = jnp.zeros_like(buf)
        if start_call:
            state[...] = fold_states(pieces)
        else:
            state[...] = carried[0][...]
            buf_x[:, pl.ds(EDGE + GROUP, 8), :] = carried[1][...]
            buf_s[:, pl.ds(EDGE + GROUP, 8), :] = carried[2][...]

    first_group = closing if end_call else False
    ext_x[pl.ds(EDGE, GROUP), :] = xpre[...].astype(F32)
    ext_s[pl.ds(EDGE, GROUP), :] = spre[...].astype(F32)
    before_x, before_s = xprev[...].astype(F32), sprev[...].astype(F32)
    if end_call:
        before_x = jnp.where(first_group, halo_x[...].astype(F32), before_x)
        before_s = jnp.where(first_group, halo_s[...].astype(F32), before_s)
    ext_x[pl.ds(0, EDGE), :] = before_x
    ext_s[pl.ds(0, EDGE), :] = before_s

    counts = running_counts(marked[...])
    counts_column = counts.T[:, :1]
    runs = [run_in[:, lag : lag + 1] for lag in range(K - 1)]
    living = (counts_column == 0).astype(F32)
    x = xact[...].astype(F32)
    both = bc[...]
    b, c = both[:, :half], both[:, half:]
    cums = cum[...]
    cum_rows = cums.T
    steps = step[...]
    step_wide = expand(steps, channels)
    weighted = x * step_wide
    scaled = rounded(weighted)
    down = dy[...]
    down_low = rounded(down)
    causal = iota((GROUP, GROUP), 0) <= iota((GROUP, GROUP), 1)
    mask = jnp.where(causal & (counts_column == counts[:1]), 0.0, FAR)
    scores = dot_nt(b, c)
    grad_scores = jnp.zeros((GROUP, GROUP), F32)
    inside = []
    for start, size, heads in head_parts(channels):
        part = scaled[:, start : start + size]
        slope = down_low[:, start : start + size]
        lane = iota((GROUP, size), 1)
        results = []
        for place, head in enumerate(heads):
            decay = jnp.exp(cum_rows[head : head + 1, :] - cums[:, head : head + 1] + mask)
            results.append(dot(rounded(scores * decay), slope))
            own = part
            if len(heads) == 2:
                keep = (lane < WIDTH) if place == 0 else (lane >= WIDTH)
                own = jnp.where(keep, part, jnp.zeros_like(part))
            grad_scores = grad_scores + dot_nt(own, slope) * decay
        if len(results) == 2:
            results = [jnp.where(lane < WIDTH, results[0], results[1])]
        inside.append(results[0])
    inside = jnp.concatenate(inside, axis=1) if len(inside) > 1 else inside[0]

    later = state[...]
    later_high, later_low = halves(later)
    now = states[...]
    now_high, now_low = halves(now)
    ending = (counts_column == counts[:1, GROUP - 1 :]).astype(F32)
    reach_end = expand(jnp.exp(cums[GROUP - 1 :, :] - cums) * ending, channels)
    reach = expand(jnp.exp(cums) * living, channels)
    arriving = reach_end * (dot(b, later_high) + dot(b, later_low))
    grad_weighted = inside + arriving
    reached = reach * down
    outside = reached * (dot(c, now_high) + dot(c, now_low))
    fade = fades[0:1, :]
    fade_grad = collect_row(fade * jnp.sum(later * now, axis=0, keepdims=True))
    per_position = collect(
        down_low.astype(F32) * yin[...] - scaled.astype(F32) * inside + outside
    )
    per_ending = collect(weighted * arriving)
    direct = collect(x * grad_weighted)
    position_high, position_low = halves(per_position)
    ending_high, ending_low = halves(per_ending)
    upper = triangle(lambda i, j: i <= j)
    under = triangle(lambda i, j: i > j)
    grad_rate = (
        dot(upper, position_high) + dot(upper, position_low)
        + dot(under, ending_high) + dot(under, ending_low) + fade_grad
    )
    rate = -jnp.exp(hp[1:2, :])
    grad_pre = (direct + rate * grad_rate) * jax.nn.sigmoid(raw[...])
    grad_raw = rounded(grad_pre)
    skip = expand_row(hp[2:3, :], channels)
    grad_inputs = step_wide * grad_weighted + skip * down
    low_scores = rounded(grad_scores)
    ended = rounded(weighted * reach_end)
    reached_low = rounded(reached)
    grad_b = dot(low_scores, c) + dot_nt(ended, later_high) + dot_nt(ended, later_low)
    grad_c = dot_tn(low_scores, b) + dot_nt(reached_low, now_high) + dot_nt(reached_low, now_low)
    state[...] = fade * later + entering[...]

    conv_x = convolve(ext_x, ci, runs)
    grad_x_out = grad_inputs * swish_slope(conv_x)
    conv_s = convolve(ext_s, cs, runs)
    grad_s_out = jnp.concatenate([grad_b, grad_c], axis=1) * swish_slope(conv_s)
    back_x = deconvolve(ext_x, buf_x, ci, runs, grad_x_out, grad_ci)
    back_s = deconvolve(ext_s, buf_s, cs, runs, grad_s_out, grad_cs)
    row = normed[...]
    main_x, main_s = back_x[EDGE:], back_s[EDGE:]
    grad_x[...] += dot_tn(main_x, row)
    grad_s[...] += dot_tn(main_s, row)
    grad_normed = (
        back[...] + dot_nt(main_x, win[:, :channels]) + dot(main_s, ws[...])
        + dot_nt(grad_raw, wst[...])
    )
    grad, gain_part = token_grad(tok[...].astype(F32), gain[...], grad_normed)
    grad_misc[0:8, :] += dot_tn(grad_raw, row)[:8]
    grad_misc[8:9, :] += gain_part
    grad_misc[9:10, :LANES] += jnp.sum(grad_pre, axis=0, keepdims=True)
    grad_misc[10:11, :LANES] += rate * jnp.sum(steps * grad_rate, axis=0, keepdims=True)
    store_parts(gtok, grad, me[0])

    if not end_call:
        @pl.when(closing)
        def _():
            carry_out[0][...] = state[...]
            carry_out[1][...] = buf_x[:, pl.ds(EDGE + GROUP, 8), :]
            carry_out[2][...] = buf_s[:, pl.ds(EDGE + GROUP, 8), :]

            @pl.when(row_id == pl.num_programs(0) - 1)
            def _():
                carry_out[3][:channels] = grad_x[...]
                carry_out[3][channels : channels + 2 * half] = grad_s[...]
                carry_out[3][channels + 2 * half :] = grad_misc[...]
                carry_out[4][...] = grad_ci[...]
                carry_out[5][...] = grad_cs[...]
        return

    @pl.when(closing)
    def _():
        tokens, edge_row = edge_rows(halo, gain, width)
        edge_x, edge_s = back_x[:EDGE], back_s[:EDGE]
        grad_x[...] += dot_tn(edge_x, edge_row)
        grad_s[...] += dot_tn(edge_s, edge_row)
        edge_grad = dot_nt(edge_x, win[:, :channels]) + dot(edge_s, ws[...])
        grad, gain_part = token_grad(tokens, gain[...], edge_grad)
        grad_misc[8:9, :] += gain_part
        everything = grad_misc[8:9, :]
        high = everything.astype(BF16).astype(F32)
        place = iota((EDGE, 1), 0)
        final = row_id == pl.num_programs(0) - 1
        nothing = jnp.zeros_like(high)
        high, rest = jnp.where(final, high, nothing), jnp.where(final, everything - high, nothing)
        edge = jnp.where(place == 0, high, jnp.where(place == 1, rest, grad))
        store_parts(edge_out, edge, me[0])

        @pl.when(final)
        def _():
            def padded(block):
                if block.shape[1] == width:
                    return block
                blank = jnp.zeros((8, width - block.shape[1]), F32)
                return jnp.concatenate([block, blank], axis=1)

            def both_halves(block):
                whole = padded(block)
                upper_half = whole.astype(BF16).astype(F32)
                return rounded(jnp.concatenate([upper_half, whole - upper_half], axis=0))

            packed[:channels, :] = rounded(grad_x[...])
            misc = grad_misc[...]
            fine = misc - misc.astype(BF16).astype(F32)
            packed[channels : channels + EDGE, :] = rounded(
                jnp.concatenate([misc[:11], fine[9:11], misc[13:]], axis=0)
            )
            packed[channels + EDGE : channels + 2 * EDGE, :] = both_halves(grad_ci[...])
            own = half // parts
            taps = grad_cs[...]
            for part, ref in enumerate(state_out):
                lo, hi = part * own, (part + 1) * own
                ref[:own, :] = rounded(grad_s[lo:hi, :])
                ref[own : 2 * own, :] = rounded(grad_s[half + lo : half + hi, :])
                ref[2 * own :, :] = both_halves(
                    jnp.concatenate([taps[:, lo:hi], taps[:, half + lo : half + hi]], axis=1)
                )


def unpack_kernel(
    own_width, head_count, late, early, gain, inner, state, step, conv, conv_bias, taps,
    taps_bias, step_bias, decay, skip, gain_out, out_weight,
):
    channels, width = out_weight.shape
    own = state.shape[-1]
    inner[:, 0, :] = late[:channels, :].astype(F32).T
    inner[:, 1, :] = early[channels : 2 * channels, :].T
    base = channels
    misc = late[base : base + EDGE, :].astype(F32)
    step[...] = misc.T[:, :head_count]
    step_bias[...] = (misc[9:10] + misc[11:12])[:, :head_count]
    decay[...] = (misc[10:11] + misc[12:13])[:, :head_count]
    base += EDGE
    block = late[base : base + EDGE, :].astype(F32)
    block = block[:8] + block[8:]
    conv[...] = block[:K, :channels]
    conv_bias[...] = block[K : K + 1, :channels]
    base += EDGE
    weights = late[base : base + 2 * own, :].astype(F32).T
    state[:, 0, :] = weights[:, :own]
    state[:, 1, :] = weights[:, own:]
    base += 2 * own
    block = late[base : base + EDGE, :].astype(F32)
    block = block[:8] + block[8:]
    taps[:, 0, :] = block[:K, :own]
    taps[:, 1, :] = block[:K, own : 2 * own]
    taps_bias[0:1, :] = block[K : K + 1, :own]
    taps_bias[1:2, :] = block[K : K + 1, own : 2 * own]
    base += EDGE
    block = late[base : base + EDGE, :].astype(F32)
    gain[...] = (block[0:1] + block[1:2])[:, :own_width]
    out_weight[...] = early[:channels, :]
    gain_out[...] = early[2 * channels : 2 * channels + 1, :channels]
    skip[...] = early[2 * channels + 1 : 2 * channels + 2, :head_count]


def ring(axis, distance):
    count = lax.axis_size(axis)
    return [(i, (i + distance) % count) for i in range(count)]


def shifted(block, axis, distance):
    devices = range(lax.axis_size(axis))
    return lax.ppermute(block, axis, [(i - distance, i) for i in devices if i - distance in devices])


def crossed(block, axis, mask):
    return lax.ppermute(block, axis, [(i, i ^ mask) for i in range(lax.axis_size(axis))])


def send_near(parts, axis):
    if len(parts) == 4:
        return [crossed(parts[3], axis, 1), crossed(parts[1], axis, 1)]
    return [lax.ppermute(part, axis, ring(axis, d)) for d, part in enumerate(parts[1:], 1)]


def send_far(parts, near, axis):
    if len(parts) == 4:
        return [crossed(rounded(parts[2].astype(F32) + near[0].astype(F32)), axis, 2)]
    return []


def add_up(parts, near, far):
    total = parts[0].astype(F32)
    for piece in (near[1:] if far else near) + far:
        total = total + piece.astype(F32)
    return total


def ordered(*groups):
    flat, tree = jax.tree.flatten(groups)
    return jax.tree.unflatten(tree, lax.optimization_barrier(flat))


def chained(message, reverse):
    count = lax.axis_size("seq")
    core = lax.axis_index("seq") % 2
    later = core == (0 if reverse else 1)
    other = crossed(message, "seq", 1)
    fade, other_fade = message[:, LANES:], other[:, LANES:]
    state, other_state = message[:, :LANES], other[:, :LANES]
    pair = jnp.where(
        later, fade[:, :1] * other_state + state, other_fade[:, :1] * state + other_state
    )
    pair = jnp.concatenate([pair, fade * other_fade], axis=1)
    neutral = (lax.broadcasted_iota(jnp.int32, message.shape, 1) >= LANES).astype(F32)
    near = jnp.where(later, other, neutral)
    sign = -2 if reverse else 2
    return [near] + [shifted(pair, "seq", sign * d) for d in range(1, count // 2)]


def all_sum(whole, axis):
    count = lax.axis_size(axis)
    chunk = whole.shape[0] // count
    parts = lax.all_to_all(whole.reshape(count, chunk, -1), axis, 0, 0, tiled=True)
    own = rounded(jnp.sum(parts.astype(F32), axis=0))
    return lax.all_gather(own, axis, axis=0, tiled=True).astype(F32)


def on_device(
    tokens, starts, norm_in_gain, inner_weight, state_weight, step_weight, conv_inner,
    conv_inner_bias, conv_state, conv_state_bias, step_bias, decay_log, skip_gain,
    norm_out_gain, out_weight, cotangent,
):
    rows, length, width = tokens.shape
    head_count = step_weight.shape[1]
    channels = inner_weight.shape[2]
    own_state = state_weight.shape[2]
    seq_count, head_devices = lax.axis_size("seq"), lax.axis_size("head")
    groups = length // GROUP
    grid = (rows, groups)
    states = 2 * own_state * head_devices
    own_width = width // head_devices
    me = lax.axis_index("head").reshape(1)

    def sds(shape, dtype=F32):
        return jax.ShapeDtypeStruct(shape, dtype)

    def whole(shape):
        return pl.BlockSpec(shape, lambda r, g: (0,) * len(shape))

    def place(g, reverse):
        return groups - 1 - g if reverse else g

    def block(cols, reverse=False, part=0):
        return pl.BlockSpec((None, GROUP, cols), lambda r, g: (r, place(g, reverse), part))

    def per_row(height, cols):
        return pl.BlockSpec((None, height, cols), lambda r, g: (r, 0, 0))

    def per_group(height, cols, reverse=False):
        return pl.BlockSpec(
            (None, None, height, cols), lambda r, g: (r, place(g, reverse), 0, 0)
        )

    scalar = pl.BlockSpec(memory_space=pltpu.SMEM)
    halo_width = width + LANES
    tail = jnp.concatenate(
        [
            tokens[:, length - EDGE :],
            jnp.broadcast_to(starts[:, length - EDGE :, None], (rows, EDGE, LANES)).astype(BF16),
        ],
        axis=2,
    )
    halo = shifted(tail, "seq", 1)
    state_own = jnp.concatenate(
        [
            state_weight, conv_state, conv_state_bias[None],
            jnp.zeros((LANES - K - 1, 2, own_state), BF16),
        ],
        axis=0,
    ).transpose(1, 2, 0).reshape(2 * own_state, width + LANES)
    found = [state_own] + [
        lax.ppermute(state_own, "head", ring("head", d)) for d in range(1, head_devices)
    ]

    gain_in = norm_in_gain[None]
    gain_out = norm_out_gain[None]
    win = inner_weight.reshape(width, 2 * channels)
    wst = jnp.pad(step_weight, ((0, 0), (0, LANES - head_count)))
    hp = jnp.pad(
        jnp.stack([step_bias, decay_log, skip_gain]), ((0, 5), (0, LANES - head_count))
    )
    ci = jnp.pad(
        jnp.concatenate([conv_inner, conv_inner_bias[None]], axis=0).astype(F32), ((0, 3), (0, 0))
    )
    marked = jnp.broadcast_to(
        starts.astype(F32).reshape(rows, groups, 1, GROUP), (rows, groups, 8, GROUP)
    )

    def act(cols, dtype=F32):
        return sds((rows, length, cols), dtype)

    normed, xpre, gate, raw, step, cum = pl.pallas_call(
        project_kernel,
        grid=grid,
        in_specs=[
            block(width), whole((1, width)), whole((width, 2 * channels)),
            whole((width, LANES)), whole((8, LANES)),
        ],
        out_specs=[
            block(width), block(channels), block(channels), block(LANES), block(LANES),
            block(LANES),
        ],
        out_shape=[
            act(width, BF16), act(channels, BF16), act(channels), act(LANES), act(LANES),
            act(LANES),
        ],
        compiler_params=PARAMS,
        name="project",
        cost_estimate=cost(6),
    )(tokens, gain_in, win, wst, hp)
    dn = jnp.einsum("rsd,cd->rsc", cotangent, out_weight, preferred_element_type=F32)

    (
        yin, xact, bc, spre, fresh, fades, message, halo_x, halo_s, run_all, ws, cs,
    ) = pl.pallas_call(
        functools.partial(forward_kernel, len(found)),
        grid=grid,
        in_specs=[whole((2 * own_state, width + LANES))] * len(found) + [
            per_group(8, GROUP), block(width), block(channels), block(LANES), block(LANES),
            whole((width, 2 * channels)), per_row(EDGE, halo_width), whole((1, width)),
            whole((8, channels)),
        ],
        out_specs=[
            block(channels), block(channels), block(states), block(states),
            per_group(LANES, channels), per_group(8, channels), per_row(LANES + 8, channels),
            per_row(EDGE, channels), per_row(EDGE, states), block(LANES),
            whole((states, width)), whole((8, states)),
        ],
        out_shape=[
            act(channels), act(channels, BF16), act(states, BF16), act(states, BF16),
            sds((rows, groups, LANES, channels)), sds((rows, groups, 8, channels)),
            sds((rows, LANES + 8, channels)), sds((rows, EDGE, channels), BF16),
            sds((rows, EDGE, states), BF16), act(LANES), sds((states, width), BF16),
            sds((8, states)),
        ],
        scratch_shapes=[
            pltpu.VMEM((GROUP + EDGE, channels), F32), pltpu.VMEM((GROUP + EDGE, states), F32),
            pltpu.VMEM((GROUP + EDGE, LANES), F32),
            pltpu.VMEM((LANES, channels), F32), pltpu.VMEM((8, channels), F32),
        ],
        compiler_params=PARAMS,
        name="forward",
        cost_estimate=cost(10),
    )(*found, marked, normed, xpre, step, cum, win, halo, gain_in, ci)

    arrived = chained(message, False)
    mixer, sums, entry_states = pl.pallas_call(
        functools.partial(mix_kernel, len(arrived)),
        grid=grid,
        in_specs=[per_row(LANES + 8, channels)] * len(arrived) + [
            block(channels), block(channels), block(states // 2, part=1), block(channels),
            block(channels), block(LANES), per_group(8, GROUP), whole((1, channels)),
            whole((8, LANES)), per_group(LANES, channels), per_group(8, channels),
        ],
        out_specs=[block(channels), per_group(8, GROUP), per_group(LANES, channels)],
        out_shape=[
            act(channels), sds((rows, groups, 8, GROUP)), sds((rows, groups, LANES, channels)),
        ],
        scratch_shapes=[pltpu.VMEM((LANES, channels), F32)],
        compiler_params=PARAMS,
        name="mix",
        cost_estimate=cost(6),
    )(*arrived, yin, xact, bc, gate, dn, cum, marked, gain_out, hp, fresh, fades)

    sums_all = [sums] + [
        lax.ppermute(sums, "head", ring("head", d)) for d in range(1, head_devices)
    ]
    dy, dgate, normed_out, entering, back_message, grad_gain_out, grad_skip = pl.pallas_call(
        functools.partial(gate_kernel, len(sums_all)),
        grid=grid,
        in_specs=[per_group(8, GROUP, True)] * len(sums_all) + [
            block(channels, True), block(channels, True), block(channels, True),
            block(channels, True), block(states // 2, True, 1), block(LANES, True),
            per_group(8, GROUP, True), whole((1, channels)), whole((8, LANES)),
            per_group(8, channels, True),
        ],
        out_specs=[
            block(channels, True), block(channels, True), block(channels, True),
            per_group(LANES, channels, True), per_row(LANES + 8, channels),
            whole((1, channels)), whole((1, channels)),
        ],
        out_shape=[
            act(channels), act(channels, BF16), act(channels, BF16),
            sds((rows, groups, LANES, channels)), sds((rows, LANES + 8, channels)),
            sds((1, channels)), sds((1, channels)),
        ],
        scratch_shapes=[pltpu.VMEM((LANES, channels), F32), pltpu.VMEM((8, channels), F32)],
        compiler_params=PARAMS,
        name="gate",
        cost_estimate=cost(6),
    )(*sums_all, mixer, gate, dn, xact, bc, cum, marked, gain_out, hp, fades)

    returned = chained(back_message, True)
    back, early, *branch = pl.pallas_call(
        functools.partial(out_kernel, head_devices),
        grid=grid,
        in_specs=[
            scalar, block(channels), block(width), block(channels), block(width),
            whole((channels, width)), whole((width, 2 * channels)), whole((1, channels)),
            whole((1, channels)),
        ],
        out_specs=[block(width), whole((2 * channels + 8, width))]
        + [block(own_width)] * head_devices,
        out_shape=[act(width), sds((2 * channels + 8, width))]
        + [act(own_width, BF16)] * head_devices,
        compiler_params=PARAMS,
        name="out",
        cost_estimate=cost(8),
    )(me, normed_out, cotangent, dgate, normed, out_weight, win, grad_gain_out, grad_skip)

    column = lax.axis_index("head") * own_width
    own_tokens = lax.dynamic_slice_in_dim(tokens, column, own_width, 2).astype(F32)
    branch_near = send_near(branch, "head")
    early = lax.psum(early, "seq")

    late_rows = channels + 3 * EDGE + 2 * own_state + EDGE
    chunk = -(-late_rows // (seq_count * EDGE)) * EDGE
    packed_rows = channels + 2 * EDGE
    piece_rows = 2 * own_state + EDGE

    def backward_call(start_call, end_call, offset, steps, carried):
        step_size = GROUP // EDGE

        def at(g):
            return offset + steps - 1 - g

        def tile(cols):
            return pl.BlockSpec((None, GROUP, cols), lambda r, g: (r, at(g), 0))

        def before(cols):
            return pl.BlockSpec(
                (None, EDGE, cols), lambda r, g: (r, jnp.maximum(at(g) * step_size - 1, 0), 0)
            )

        def group_tile(height, cols):
            return pl.BlockSpec((None, None, height, cols), lambda r, g: (r, at(g), 0, 0))

        carry_specs = [
            per_row(LANES, channels),
            pl.BlockSpec((None, K, 8, channels), lambda r, g: (r, 0, 0, 0)),
            pl.BlockSpec((None, K, 8, states), lambda r, g: (r, 0, 0, 0)),
            whole((channels + states + EDGE, width)), whole((8, channels)), whole((8, states)),
        ]
        carry_shapes = [
            sds((rows, LANES, channels)), sds((rows, K, 8, channels)), sds((rows, K, 8, states)),
            sds((channels + states + EDGE, width)), sds((8, channels)), sds((8, states)),
        ]
        local = pl.BlockSpec((None, GROUP, own_width), lambda r, g: (r, steps - 1 - g, 0))
        out_specs = [local] * head_devices
        out_shape = [sds((rows, steps * GROUP, own_width), BF16)] * head_devices
        if end_call:
            out_specs += [whole((packed_rows, width))]
            out_specs += [per_row(EDGE, own_width)] * head_devices
            out_specs += [whole((piece_rows, width))] * head_devices
            out_shape += [sds((packed_rows, width), BF16)]
            out_shape += [sds((rows, EDGE, own_width), BF16)] * head_devices
            out_shape += [sds((piece_rows, width), BF16)] * head_devices
        else:
            out_specs += carry_specs
            out_shape += carry_shapes
        lead = returned if start_call else []
        return pl.pallas_call(
            functools.partial(backward_kernel, start_call, end_call, len(lead), head_devices),
            grid=(rows, steps),
            in_specs=[per_row(LANES + 8, channels)] * len(lead)
            + ([] if start_call else carry_specs)
            + [
                scalar, tile(width), per_row(EDGE, halo_width), group_tile(8, GROUP), tile(width),
                tile(channels), before(channels), per_row(EDGE, channels), tile(states),
                before(states), per_row(EDGE, states), tile(channels), tile(states),
                tile(channels), tile(channels), tile(width), tile(LANES), tile(LANES),
                tile(LANES), tile(LANES), group_tile(LANES, channels),
                group_tile(LANES, channels), group_tile(8, channels),
                whole((width, 2 * channels)), whole((states, width)), whole((width, LANES)),
                whole((8, LANES)), whole((8, channels)), whole((8, states)), whole((1, width)),
            ],
            out_specs=out_specs,
            out_shape=out_shape,
            scratch_shapes=[
                pltpu.VMEM((GROUP + EDGE, channels), F32),
                pltpu.VMEM((GROUP + EDGE, states), F32),
                pltpu.VMEM((K, GROUP + 2 * EDGE, channels), F32),
                pltpu.VMEM((K, GROUP + 2 * EDGE, states), F32),
                pltpu.VMEM((LANES, channels), F32),
                pltpu.VMEM((channels, width), F32), pltpu.VMEM((states, width), F32),
                pltpu.VMEM((EDGE, width), F32), pltpu.VMEM((8, channels), F32),
                pltpu.VMEM((8, states), F32),
            ],
            compiler_params=PARAMS,
            name="backward",
            cost_estimate=cost(15),
        )(
            *lead, *carried, me, tokens, halo, marked, normed, xpre, xpre, halo_x, spre, spre,
            halo_s, xact, bc, yin, dy, back, step, cum, raw, run_all, entry_states, entering,
            fades, win, ws, wst, hp, ci, cs, gain_in,
        )

    first = groups // 2
    if first:
        outs = backward_call(True, False, first, groups - first, [])
        outs, branch_near = ordered(outs, branch_near)
        branch_far = send_far(branch, branch_near, "head")
        late_parts, carried = outs[:head_devices], outs[head_devices:]
        late_near = send_near(late_parts, "head")
        outs = backward_call(False, True, 0, first, carried)
        outs, branch_far, late_near = ordered(outs, branch_far, late_near)
    else:
        outs = backward_call(True, True, 0, groups, [])
        branch_far = send_far(branch, branch_near, "head")
    gtok, packed = outs[:head_devices], outs[head_devices]
    edge_parts = outs[head_devices + 1 : 2 * head_devices + 1]
    state_parts = outs[2 * head_devices + 1 :]
    state_pieces = [
        lax.ppermute(state_parts[d], "head", ring("head", -d)) for d in range(1, head_devices)
    ]
    edge_near = send_near(edge_parts, "head")
    edge_far = send_far(edge_parts, edge_near, "head")
    state_total = state_parts[0].astype(F32)
    for piece in state_pieces:
        state_total = state_total + piece.astype(F32)
    edge = add_up(edge_parts, edge_near, edge_far)
    gtok_near = send_near(gtok, "head")
    if first:
        late_far = send_far(late_parts, late_near, "head")
    output = rounded(own_tokens + add_up(branch, branch_near, branch_far))
    gain_row = (edge[rows - 1, 0] + edge[rows - 1, 1])[None]
    gain_high = gain_row.astype(BF16).astype(F32)
    gain_rows = jnp.pad(
        jnp.concatenate([gain_high, gain_row - gain_high]),
        ((0, EDGE - 2), (0, width - own_width)),
    )
    taps = state_total[2 * own_state : 2 * own_state + 8] + state_total[2 * own_state + 8 :]
    taps_high = taps.astype(BF16).astype(F32)
    late = jnp.concatenate(
        [
            packed, rounded(state_total[: 2 * own_state]), rounded(taps_high),
            rounded(taps - taps_high), rounded(gain_rows),
            jnp.zeros((chunk * seq_count - late_rows, width), BF16),
        ],
        axis=0,
    )
    parts = lax.all_to_all(late.reshape(seq_count, chunk, -1), "seq", 0, 0, tiled=True)
    parts, gtok_near = ordered(parts, gtok_near)
    gtok_far = send_far(gtok, gtok_near, "head")
    from_next = shifted(edge, "seq", -1)[:, EDGE - K + 1 :]
    late = lax.all_gather(
        rounded(jnp.sum(parts.astype(F32), axis=0)), "seq", axis=0, tiled=True
    )
    token_sums = [add_up(gtok, gtok_near, gtok_far)]
    if first:
        token_sums.append(add_up(late_parts, late_near, late_far))
    own_cot = lax.dynamic_slice_in_dim(cotangent, column, own_width, 2).astype(F32)
    padding = jnp.zeros((rows, length - K + 1, own_width), F32)
    grad_tokens = (
        own_cot + jnp.concatenate(token_sums, axis=1)
        + jnp.concatenate([padding, from_next], axis=1)
    )
    outs = pl.pallas_call(
        functools.partial(unpack_kernel, own_width, head_count),
        out_shape=[
            sds((1, own_width)), sds((width, 2, channels)), sds((width, 2, own_state)),
            sds((width, head_count)), sds((K, channels)), sds((1, channels)),
            sds((K, 2, own_state)), sds((2, own_state)), sds((1, head_count)),
            sds((1, head_count)), sds((1, head_count)), sds((1, channels)),
            sds((channels, width)),
        ],
        compiler_params=pltpu.CompilerParams(vmem_limit_bytes=62 * 2**20),
        cost_estimate=cost(4),
        name="unpack",
    )(late, early)
    one_row = (0, 5, 8, 9, 10, 11)
    return (output, grad_tokens) + tuple(
        out[0] if place in one_row else out for place, out in enumerate(outs)
    )


def solution(mesh):
    return jax.shard_map(
        on_device,
        mesh=mesh,
        in_specs=(
            P(None, "seq", None), P(None, "seq"), P(), P(None, None, "head"),
            P(None, None, "head"), P(None, "head"), P(None, "head"), P("head"),
            P(None, None, "head"), P(None, "head"), P("head"), P("head"), P("head"), P("head"),
            P("head", None), P(None, "seq", None),
        ),
        out_specs=(
            P(None, "seq", "head"), P(None, "seq", "head"), P("head"), P(None, None, "head"),
            P(None, None, "head"), P(None, "head"), P(None, "head"), P("head"),
            P(None, None, "head"), P(None, "head"), P("head"), P("head"), P("head"), P("head"),
            P("head", None),
        ),
        check_vma=False,
    )
```

```python
import functools

import jax
import jax.numpy as jnp
from jax import lax
from jax.experimental import pallas as pl
from jax.experimental.pallas import tpu as pltpu
from jax.sharding import PartitionSpec as P

K = 4
GROUP = 256
DI = 1536
WIDTH = 64
LANES = 128
EDGE = 16
EPSILON = 1e-05
HIGHEST = lax.Precision.HIGHEST
F32 = jnp.float32
BF16 = jnp.bfloat16
FAR = -1e30
PARAMS = pltpu.CompilerParams(
    dimension_semantics=("arbitrary", "arbitrary"), vmem_limit_bytes=62 * 2**20
)


def cost(microseconds):
    return pl.CostEstimate(
        flops=int(microseconds * 1e9), bytes_accessed=int(microseconds * 1e5), transcendentals=0
    )


def rounded(tensor):
    return tensor.astype(BF16)


def dot(a, b, exact=False):
    return jnp.dot(a, b, preferred_element_type=F32, precision=HIGHEST if exact else None)


def dot_nt(a, b, exact=False):
    return lax.dot_general(
        a, b, (((1,), (1,)), ((), ())), preferred_element_type=F32,
        precision=HIGHEST if exact else None,
    )


def dot_tn(a, b, exact=False):
    return lax.dot_general(
        a, b, (((0,), (0,)), ((), ())), preferred_element_type=F32,
        precision=HIGHEST if exact else None,
    )


def iota(shape, dim):
    return lax.broadcasted_iota(jnp.int32, shape, dim)


def halves(tensor):
    high = rounded(tensor)
    return high, rounded(tensor - high.astype(F32))


def expand(tensor, channels):
    both = jnp.concatenate(halves(tensor), axis=1)
    table = iota((2 * LANES, channels), 1) // WIDTH == iota((2 * LANES, channels), 0) % LANES
    return dot(both, table.astype(F32).astype(BF16))


def collect(tensor):
    channels = tensor.shape[1]
    table = iota((channels, LANES), 0) // WIDTH == iota((channels, LANES), 1)
    table = table.astype(F32).astype(BF16)
    high, low = halves(tensor)
    return dot(high, table) + dot(low, table)


def expand_row(row, channels):
    return expand(jnp.broadcast_to(row, (8, LANES)), channels)[:1]


def collect_row(row):
    return collect(jnp.broadcast_to(row, (8, row.shape[1])))[:1]


def triangle(compare):
    return compare(iota((GROUP, GROUP), 0), iota((GROUP, GROUP), 1)).astype(F32).astype(BF16)


def running_counts(marked):
    return dot(marked.astype(BF16), triangle(lambda i, j: i <= j))


def fade_of(cum, counts):
    return jnp.exp(cum[GROUP - 1 :, :]) * (counts[:1, GROUP - 1 :] == 0).astype(F32)


def pack_state(ref, state, fade):
    ref[:LANES, :] = state
    ref[LANES:, :] = jnp.broadcast_to(fade, (8, fade.shape[1]))


def fold_states(pieces):
    state = jnp.zeros((LANES, pieces[0].shape[1]), F32)
    for piece in reversed(pieces):
        state = piece[LANES : LANES + 1, :] * state + piece[:LANES, :]
    return state


def rms_scale(tokens):
    return lax.rsqrt(jnp.mean(tokens * tokens, axis=-1, keepdims=True) + EPSILON)


def head_parts(channels):
    for start in range(0, channels, LANES):
        width = min(LANES, channels - start)
        yield start, width, [start // WIDTH + i for i in range(width // WIDTH)]


def project_kernel(tok, gain, win, wst, hp, normed, xpre, gate, spre, step, cum):
    channels = xpre.shape[-1]
    tokens = tok[...].astype(F32)
    row = rounded(tokens * rms_scale(tokens) * gain[...])
    normed[...] = row
    product = dot(row, win[...])
    xpre[...] = rounded(product[:, :channels])
    gate[...] = product[:, channels:]
    raw = dot(row, wst[...]) + hp[0:1, :]
    sizes = jax.nn.softplus(raw)
    spre[...] = raw
    step[...] = sizes
    rates = sizes * -jnp.exp(hp[1:2, :])
    lower = triangle(lambda i, j: i >= j)
    high, rest = rounded(rates), rates - rounded(rates).astype(F32)
    middle, low = halves(rest)
    cum[...] = dot(lower, high) + dot(lower, middle) + dot(lower, low)


def convolve(ext, taps, runs):
    summed = taps[K : K + 1, :] + taps[K - 1 : K, :] * ext[pl.ds(EDGE, GROUP), :]
    for lag in range(1, K):
        summed = summed + (
            taps[K - 1 - lag : K - lag, :] * ext[pl.ds(EDGE - lag, GROUP), :]
        ) * runs[lag - 1]
    return summed


def edge_rows(halo, gain, width):
    tokens = halo[:, :width].astype(F32)
    return tokens, rounded(tokens * rms_scale(tokens) * gain[...])


def forward_kernel(count, *refs):
    pieces = refs[:count]
    (
        marked, normed, xpre, step, cum, win, halo, gain, ci,
        yin, xact, bc, spre, fresh, fades, message, halo_x, halo_s, run_out, ws, cs,
        ext_x, ext_s, ext_k, state, total,
    ) = refs[count:]
    group = pl.program_id(1)
    channels = xpre.shape[-1]
    width = normed.shape[-1]
    own = pieces[0].shape[0] // 2

    @pl.when((group == 0) & (pl.program_id(0) == 0))
    def _():
        for place, piece in enumerate(pieces):
            for kind in range(2):
                row = (kind * count + place) * own
                ws[row : row + own, :] = piece[kind * own : (kind + 1) * own, :width]
        taps = jnp.concatenate(
            [p[kind * own : (kind + 1) * own, width:] for kind in range(2) for p in pieces], axis=0
        )
        cs[...] = taps.astype(F32).T[:8]

    @pl.when(group == 0)
    def _():
        _, row = edge_rows(halo, gain, width)
        edge_x = rounded(dot(row, win[:, :channels]))
        edge_s = rounded(dot_nt(row, ws[...]))
        halo_x[...] = edge_x
        halo_s[...] = edge_s
        ext_x[pl.ds(0, EDGE), :] = edge_x.astype(F32)
        ext_s[pl.ds(0, EDGE), :] = edge_s.astype(F32)
        ext_k[pl.ds(0, EDGE), :] = 1.0 - halo[:, width:].astype(F32)
        state[...] = jnp.zeros_like(state)
        total[...] = jnp.ones_like(total)

    @pl.when(group > 0)
    def _():
        ext_x[pl.ds(0, EDGE), :] = ext_x[pl.ds(GROUP, EDGE), :]
        ext_s[pl.ds(0, EDGE), :] = ext_s[pl.ds(GROUP, EDGE), :]
        ext_k[pl.ds(0, EDGE), :] = ext_k[pl.ds(GROUP, EDGE), :]

    counts = running_counts(marked[...])
    counts_column = counts.T[:, :1]
    run1 = 1.0 - marked[...].T[:, :1]
    ext_k[pl.ds(EDGE, GROUP), :] = jnp.broadcast_to(run1, (GROUP, LANES))
    run2 = run1 * ext_k[pl.ds(EDGE - 1, GROUP), :1]
    run3 = run2 * ext_k[pl.ds(EDGE - 2, GROUP), :1]
    runs = (run1, run2, run3)
    lane = iota((GROUP, LANES), 1)
    run_out[...] = jnp.where(lane == 0, run1, jnp.where(lane == 1, run2, run3))
    state_pre = rounded(dot_nt(normed[...], ws[...]))
    spre[...] = state_pre
    ext_s[pl.ds(EDGE, GROUP), :] = state_pre.astype(F32)
    ext_x[pl.ds(EDGE, GROUP), :] = xpre[...].astype(F32)
    conv_x = convolve(ext_x, ci, runs)
    conv_s = convolve(ext_s, cs, runs)
    x = rounded(conv_x * jax.nn.sigmoid(conv_x))
    both = rounded(conv_s * jax.nn.sigmoid(conv_s))
    xact[...] = x
    bc[...] = both
    half = both.shape[1] // 2
    b, c = both[:, :half], both[:, half:]
    cums = cum[...]
    causal = iota((GROUP, GROUP), 0) >= iota((GROUP, GROUP), 1)
    mask = jnp.where(causal & (counts_column == counts[:1]), 0.0, FAR)
    scores = dot_nt(c, b)
    weighted = x.astype(F32) * expand(step[...], channels)
    scaled = rounded(weighted)
    cum_rows = cums.T
    for start, size, heads in head_parts(channels):
        part = scaled[:, start : start + size]
        results = []
        for head in heads:
            decay = jnp.exp(cums[:, head : head + 1] - cum_rows[head : head + 1, :] + mask)
            results.append(dot(rounded(scores * decay), part))
        if len(results) == 2:
            results = [jnp.where(iota((GROUP, size), 1) < WIDTH, results[0], results[1])]
        yin[:, start : start + size] = results[0]
    ending = (counts_column == counts[:1, GROUP - 1 :]).astype(F32)
    reach_end = jnp.exp(cums[GROUP - 1 :, :] - cums) * ending
    new = dot_tn(b, rounded(weighted * expand(reach_end, channels)))
    fresh[...] = new
    fade = expand_row(fade_of(cums, counts), channels)
    fades[...] = jnp.broadcast_to(fade, (8, channels))
    state[...] = fade * state[...] + new
    total[...] = total[...] * fade

    @pl.when(group == pl.num_programs(1) - 1)
    def _():
        pack_state(message, state[...], total[0:1, :])


def mix_kernel(count, *refs):
    pieces = refs[:count]
    (
        yin, x, c, gate, dn, cum, marked, gain, hp, fresh, fades,
        mixer, sums, states, state,
    ) = refs[count:]
    channels = x.shape[-1]

    @pl.when(pl.program_id(1) == 0)
    def _():
        state[...] = fold_states(pieces)

    counts = running_counts(marked[...])
    living = (counts.T[:, :1] == 0).astype(F32)
    now = state[...]
    states[...] = now
    reach = expand(jnp.exp(cum[...]) * living, channels)
    skip = expand_row(hp[2:3, :], channels)
    high, low = halves(now)
    reads = c[...]
    mixed = yin[...] + reach * (dot(reads, high) + dot(reads, low)) + skip * x[...].astype(F32)
    mixer[...] = mixed
    gates = gate[...]
    gated = mixed * (gates * jax.nn.sigmoid(gates))
    square = jnp.sum(gated * gated, axis=1, keepdims=True)
    cross = jnp.sum(gated * (dn[...] * gain[...]), axis=1, keepdims=True)
    lane = iota((GROUP, LANES), 1)
    sums[...] = jnp.where(lane == 0, square, cross).T[:8]
    state[...] = fades[0:1, :] * now + fresh[...]


def gate_kernel(count, *refs):
    pieces = refs[:count]
    (
        mixer, gate, dn, x, c, cum, marked, gain, hp, fades,
        dy, dgate, normed_out, entering, message, grad_gain, grad_skip, state, total,
    ) = refs[count:]
    channels = x.shape[-1]
    last = pl.program_id(1) == 0

    @pl.when(last & (pl.program_id(0) == 0))
    def _():
        grad_gain[...] = jnp.zeros_like(grad_gain)
        grad_skip[...] = jnp.zeros_like(grad_skip)

    @pl.when(last)
    def _():
        state[...] = jnp.zeros_like(state)
        total[...] = jnp.ones_like(total)

    sums = pieces[0][...]
    for piece in pieces[1:]:
        sums = sums + piece[...]
    columns = sums.T
    scale = lax.rsqrt(columns[:, 0:1] / DI + EPSILON)
    pull = scale * scale * scale * (columns[:, 1:2] / DI)
    counts = running_counts(marked[...])
    living = (counts.T[:, :1] == 0).astype(F32)
    mixed = mixer[...]
    gates = gate[...]
    squash = jax.nn.sigmoid(gates)
    act = gates * squash
    gated = mixed * act
    norm_grad = dn[...]
    grad_gated = scale * (norm_grad * gain[...]) - gated * pull
    down = grad_gated * act
    dy[...] = down
    dgate[...] = rounded(grad_gated * mixed * (squash * (1.0 + gates * (1.0 - squash))))
    scaled = gated * scale
    normed_out[...] = rounded(scaled * gain[...])
    grad_gain[...] += jnp.sum(norm_grad * scaled, axis=0, keepdims=True)
    grad_skip[...] += jnp.sum(down * x[...].astype(F32), axis=0, keepdims=True)
    reach = expand(jnp.exp(cum[...]) * living, channels)
    new = dot_tn(c[...], rounded(reach * down))
    entering[...] = new
    fade = fades[0:1, :]
    state[...] = fade * state[...] + new
    total[...] = total[...] * fade

    @pl.when(pl.program_id(1) == pl.num_programs(1) - 1)
    def _():
        pack_state(message, state[...], total[0:1, :])


def store_parts(refs, tensor, me):
    width = tensor.shape[1]
    own = width // len(refs)
    turned = rounded(pltpu.roll(tensor, (len(refs) - me) % len(refs) * own, 1))
    blocks = [turned[:, part * own : (part + 1) * own] for part in range(len(refs))]
    if len(refs) == 4:
        odd = me % 2 == 1
        swapped = [jnp.where(odd, blocks[4 - part], blocks[part]) for part in (1, 3)]
        blocks = [blocks[0], swapped[0], blocks[2], swapped[1]]
    for block, ref in zip(blocks, refs):
        ref[...] = block


def out_kernel(parts, me, normed_out, cot, dgate, normed, wout, win, back, grads, *rest):
    channels = wout.shape[0]
    branch, total = rest[:parts], rest[parts]

    @pl.when((pl.program_id(1) == 0) & (pl.program_id(0) == 0))
    def _():
        total[...] = jnp.zeros_like(total)

    store_parts(branch, dot(normed_out[...], wout[...]), me[0])
    total[:channels, :] += dot_tn(normed_out[...], cot[...])
    total[channels : 2 * channels, :] += dot_tn(dgate[...], normed[...])

    @pl.when(
        (pl.program_id(1) == pl.num_programs(1) - 1)
        & (pl.program_id(0) == pl.num_programs(0) - 1)
    )
    def _():
        grads[...] = rounded(total[...])

    back[...] = dot_nt(dgate[...], win[:, channels:])


def token_grad(tokens, gain, down):
    scale = rms_scale(tokens)
    pulled = down * gain
    inner = jnp.mean(pulled * tokens, axis=-1, keepdims=True)
    grad = scale * pulled - tokens * (scale * scale * scale * inner)
    return grad, jnp.sum(down * tokens * scale, axis=0, keepdims=True)


def deconvolve(ext, buffers, taps, runs, grad_out, grad_taps):
    rows = GROUP + EDGE
    grad_taps[K : K + 1, :] += jnp.sum(grad_out, axis=0, keepdims=True)
    result = None
    for lag in range(K):
        masked = grad_out if lag == 0 else grad_out * runs[lag - 1]
        buffer = buffers.at[lag]
        buffer[pl.ds(EDGE, GROUP), :] = masked
        tap = K - 1 - lag
        grad_taps[tap : tap + 1, :] += jnp.sum(
            masked * ext[pl.ds(EDGE - lag, GROUP), :], axis=0, keepdims=True
        )
        piece = taps[tap : tap + 1, :] * buffer[pl.ds(lag, rows), :]
        result = piece if result is None else result + piece
        buffer[pl.ds(EDGE + GROUP, 8), :] = masked[:8]
    return rounded(result)


def swish_slope(tensor):
    squash = jax.nn.sigmoid(tensor)
    return squash * (1.0 + tensor * (1.0 - squash))


def backward_kernel(start_call, end_call, count, parts, *refs):
    pieces, refs = refs[:count], refs[count:]
    carried, refs = (refs[:0], refs) if start_call else (refs[:6], refs[6:])
    (
        me, tok, halo, marked, normed, xpre, xprev, halo_x, spre, sprev, halo_s, xact, bc, yin, dy,
        back, step, cum, raw, run_in, states, entering, fades, win, ws, wst, hp, ci, cs, gain, gain_out, skip_out,
    ), refs = refs[:32], refs[32:]
    gtok, refs = refs[:parts], refs[parts:]
    if end_call:
        (packed, *state_out), refs = refs[: 1 + parts], refs[1 + parts :]
    else:
        carry_out, refs = refs[:6], refs[6:]
    (
        ext_x, ext_s, buf_x, buf_s, state, grad_x, grad_s, grad_misc, grad_ci, grad_cs, edges,
    ) = refs
    channels = xact.shape[-1]
    width = tok.shape[-1]
    half = bc.shape[-1] // 2
    order = pl.program_id(1)
    row_id = pl.program_id(0)
    closing = order == pl.num_programs(1) - 1
    sums = (grad_x, grad_s, grad_misc, grad_ci, grad_cs)

    @pl.when((order == 0) & (row_id == 0))
    def _():
        if start_call:
            for ref in sums:
                ref[...] = jnp.zeros_like(ref)
        else:
            grad_x[...] = carried[3][:channels]
            grad_s[...] = carried[3][channels : channels + 2 * half]
            grad_misc[...] = carried[3][channels + 2 * half :]
            grad_ci[...] = carried[4][...]
            grad_cs[...] = carried[5][...]

    @pl.when(order == 0)
    def _():
        for buf in (buf_x, buf_s):
            buf[...] = jnp.zeros_like(buf)
        if start_call:
            state[...] = fold_states(pieces)
        else:
            state[...] = carried[0][...]
            buf_x[:, pl.ds(EDGE + GROUP, 8), :] = carried[1][...]
            buf_s[:, pl.ds(EDGE + GROUP, 8), :] = carried[2][...]

    first_group = closing if end_call else False
    ext_x[pl.ds(EDGE, GROUP), :] = xpre[...].astype(F32)
    ext_s[pl.ds(EDGE, GROUP), :] = spre[...].astype(F32)
    before_x, before_s = xprev[...].astype(F32), sprev[...].astype(F32)
    if end_call:
        before_x = jnp.where(first_group, halo_x[...].astype(F32), before_x)
        before_s = jnp.where(first_group, halo_s[...].astype(F32), before_s)
    ext_x[pl.ds(0, EDGE), :] = before_x
    ext_s[pl.ds(0, EDGE), :] = before_s

    counts = running_counts(marked[...])
    counts_column = counts.T[:, :1]
    runs = [run_in[:, lag : lag + 1] for lag in range(K - 1)]
    living = (counts_column == 0).astype(F32)
    x = xact[...].astype(F32)
    both = bc[...]
    b, c = both[:, :half], both[:, half:]
    cums = cum[...]
    cum_rows = cums.T
    steps = step[...]
    step_wide = expand(steps, channels)
    weighted = x * step_wide
    scaled = rounded(weighted)
    down = dy[...]
    down_low = rounded(down)
    causal = iota((GROUP, GROUP), 0) <= iota((GROUP, GROUP), 1)
    mask = jnp.where(causal & (counts_column == counts[:1]), 0.0, FAR)
    scores = dot_nt(b, c)
    grad_scores = jnp.zeros((GROUP, GROUP), F32)
    inside = []
    for start, size, heads in head_parts(channels):
        part = scaled[:, start : start + size]
        slope = down_low[:, start : start + size]
        lane = iota((GROUP, size), 1)
        results = []
        for place, head in enumerate(heads):
            decay = jnp.exp(cum_rows[head : head + 1, :] - cums[:, head : head + 1] + mask)
            results.append(dot(rounded(scores * decay), slope))
            own = part
            if len(heads) == 2:
                keep = (lane < WIDTH) if place == 0 else (lane >= WIDTH)
                own = jnp.where(keep, part, jnp.zeros_like(part))
            grad_scores = grad_scores + dot_nt(own, slope) * decay
        if len(results) == 2:
            results = [jnp.where(lane < WIDTH, results[0], results[1])]
        inside.append(results[0])
    inside = jnp.concatenate(inside, axis=1) if len(inside) > 1 else inside[0]

    later = state[...]
    later_high, later_low = halves(later)
    now = states[...]
    now_high, now_low = halves(now)
    ending = (counts_column == counts[:1, GROUP - 1 :]).astype(F32)
    reach_end = expand(jnp.exp(cums[GROUP - 1 :, :] - cums) * ending, channels)
    reach = expand(jnp.exp(cums) * living, channels)
    arriving = reach_end * (dot(b, later_high) + dot(b, later_low))
    grad_weighted = inside + arriving
    reached = reach * down
    outside = reached * (dot(c, now_high) + dot(c, now_low))
    fade = fades[0:1, :]
    fade_grad = collect_row(fade * jnp.sum(later * now, axis=0, keepdims=True))
    per_position = collect(
        down_low.astype(F32) * yin[...] - scaled.astype(F32) * inside + outside
    )
    per_ending = collect(weighted * arriving)
    direct = collect(x * grad_weighted)
    position_high, position_low = halves(per_position)
    ending_high, ending_low = halves(per_ending)
    upper = triangle(lambda i, j: i <= j)
    under = triangle(lambda i, j: i > j)
    grad_rate = (
        dot(upper, position_high) + dot(upper, position_low)
        + dot(under, ending_high) + dot(under, ending_low) + fade_grad
    )
    rate = -jnp.exp(hp[1:2, :])
    grad_pre = (direct + rate * grad_rate) * jax.nn.sigmoid(raw[...])
    grad_raw = rounded(grad_pre)
    skip = expand_row(hp[2:3, :], channels)
    grad_inputs = step_wide * grad_weighted + skip * down
    low_scores = rounded(grad_scores)
    ended = rounded(weighted * reach_end)
    reached_low = rounded(reached)
    grad_b = dot(low_scores, c) + dot_nt(ended, later_high) + dot_nt(ended, later_low)
    grad_c = dot_tn(low_scores, b) + dot_nt(reached_low, now_high) + dot_nt(reached_low, now_low)
    state[...] = fade * later + entering[...]

    conv_x = convolve(ext_x, ci, runs)
    grad_x_out = grad_inputs * swish_slope(conv_x)
    conv_s = convolve(ext_s, cs, runs)
    grad_s_out = jnp.concatenate([grad_b, grad_c], axis=1) * swish_slope(conv_s)
    back_x = deconvolve(ext_x, buf_x, ci, runs, grad_x_out, grad_ci)
    back_s = deconvolve(ext_s, buf_s, cs, runs, grad_s_out, grad_cs)
    row = normed[...]
    main_x, main_s = back_x[EDGE:], back_s[EDGE:]
    grad_x[...] += dot_tn(main_x, row)
    grad_s[...] += dot_tn(main_s, row)
    grad_normed = (
        back[...] + dot_nt(main_x, win[:, :channels]) + dot(main_s, ws[...])
        + dot_nt(grad_raw, wst[...])
    )
    grad, gain_part = token_grad(tok[...].astype(F32), gain[...], grad_normed)
    grad_misc[0:8, :] += dot_tn(grad_raw, row)[:8]
    grad_misc[8:9, :] += gain_part
    grad_misc[9:10, :LANES] += jnp.sum(grad_pre, axis=0, keepdims=True)
    grad_misc[10:11, :LANES] += rate * jnp.sum(steps * grad_rate, axis=0, keepdims=True)
    store_parts(gtok, grad, me[0])

    if not end_call:
        @pl.when(closing)
        def _():
            carry_out[0][...] = state[...]
            carry_out[1][...] = buf_x[:, pl.ds(EDGE + GROUP, 8), :]
            carry_out[2][...] = buf_s[:, pl.ds(EDGE + GROUP, 8), :]

            @pl.when(row_id == pl.num_programs(0) - 1)
            def _():
                carry_out[3][:channels] = grad_x[...]
                carry_out[3][channels : channels + 2 * half] = grad_s[...]
                carry_out[3][channels + 2 * half :] = grad_misc[...]
                carry_out[4][...] = grad_ci[...]
                carry_out[5][...] = grad_cs[...]
        return

    @pl.when(closing)
    def _():
        tokens, edge_row = edge_rows(halo, gain, width)
        edge_x, edge_s = back_x[:EDGE], back_s[:EDGE]
        grad_x[...] += dot_tn(edge_x, edge_row)
        grad_s[...] += dot_tn(edge_s, edge_row)
        edge_grad = dot_nt(edge_x, win[:, :channels]) + dot(edge_s, ws[...])
        grad, gain_part = token_grad(tokens, gain[...], edge_grad)
        grad_misc[8:9, :] += gain_part
        everything = grad_misc[8:9, :]
        high = everything.astype(BF16).astype(F32)
        place = iota((EDGE, 1), 0)
        final = row_id == pl.num_programs(0) - 1
        nothing = jnp.zeros_like(high)
        high, rest = jnp.where(final, high, nothing), jnp.where(final, everything - high, nothing)
        edge = jnp.where(place == 0, high, jnp.where(place == 1, rest, grad))
        edges[row_id] = edge

        @pl.when(final)
        def _():
            def padded(block):
                if block.shape[1] == width:
                    return block
                blank = jnp.zeros((8, width - block.shape[1]), F32)
                return jnp.concatenate([block, blank], axis=1)

            def both_halves(block):
                whole = padded(block)
                upper_half = whole.astype(BF16).astype(F32)
                return rounded(jnp.concatenate([upper_half, whole - upper_half], axis=0))

            packed[:channels, :] = rounded(grad_x[...])
            misc = grad_misc[...]
            fine = misc - misc.astype(BF16).astype(F32)
            packed[channels : channels + EDGE, :] = rounded(
                jnp.concatenate([misc[:11], fine[9:11], misc[13:]], axis=0)
            )
            grad_ci[K + 1 : K + 2, :] = gain_out[...]
            grad_ci[K + 2 : K + 3, :LANES] = collect_row(skip_out[...])
            packed[channels + EDGE : channels + 2 * EDGE, :] = both_halves(grad_ci[...])
            own = half // parts
            taps = grad_cs[...]
            for part, ref in enumerate(state_out):
                lo, hi = part * own, (part + 1) * own
                ref[:own, :] = rounded(grad_s[lo:hi, :])
                ref[own : 2 * own, :] = rounded(grad_s[half + lo : half + hi, :])
                ref[2 * own :, :] = both_halves(
                    jnp.concatenate([taps[:, lo:hi], taps[:, half + lo : half + hi]], axis=1)
                )
            own = width // parts
            for line in range(edges.shape[0]):
                shift = (parts - me[0]) % parts * own
                turned = rounded(pltpu.roll(edges[line], shift, 1))
                for part, ref in enumerate(state_out):
                    begin = (parts - part) % parts * own
                    ref[2 * (half // parts) :, LANES + line * own : LANES + (line + 1) * own] = (
                        turned[:, begin : begin + own]
                    )


def merge_kernel(own_width, packed, *refs):
    *pieces, late, edge = refs
    base = packed.shape[0]
    total = pieces[0][...].astype(F32)
    for piece in pieces[1:]:
        total = total + piece[...].astype(F32)
    body = total.shape[0] - EDGE
    rows = edge.shape[0]
    late[:base, :] = packed[...]
    late[base : base + body, :] = rounded(total[:body])
    tail = total[body:]
    for line in range(rows):
        edge[line] = tail[:, LANES + line * own_width : LANES + (line + 1) * own_width]

    def both_halves(block):
        upper_half = block.astype(BF16).astype(F32)
        return jnp.concatenate([upper_half, block - upper_half], axis=0)

    place = base + body
    late[place : place + EDGE, :] = rounded(both_halves(tail[:8] + tail[8:]))
    place += EDGE
    begin = LANES + (rows - 1) * own_width
    gain = jnp.broadcast_to(tail[0:1] + tail[1:2], (8, tail.shape[1]))
    late[place : place + EDGE, :] = jnp.zeros((EDGE, tail.shape[1]), BF16)
    late[place : place + EDGE, :own_width] = rounded(both_halves(gain))[:, begin : begin + own_width]
    if late.shape[0] > place + EDGE:
        rest = late.shape[0] - place - EDGE
        late[place + EDGE :, :] = jnp.zeros((rest, tail.shape[1]), BF16)


def unpack_kernel(
    own_width, head_count, late, early, gain, inner, state, step, conv, conv_bias, taps,
    taps_bias, step_bias, decay, skip, gain_out, out_weight,
):
    channels, width = out_weight.shape
    own = state.shape[1]
    inner[:, 0, :] = late[:channels, :].astype(F32).T
    inner[:, 1, :] = early[channels : 2 * channels, :].astype(F32).T
    base = channels
    misc = late[base : base + EDGE, :].astype(F32)
    step[...] = misc[:head_count]
    step_bias[...] = (misc[9] + misc[11])[:head_count]
    decay[...] = (misc[10] + misc[12])[:head_count]
    base += EDGE
    block = late[base : base + EDGE, :].astype(F32)
    block = block[:8] + block[8:]
    conv[...] = block[:K, :channels]
    conv_bias[...] = block[K, :channels]
    gain_out[...] = block[K + 1, :channels]
    skip[...] = block[K + 2, :head_count]
    base += EDGE
    state[0] = late[base : base + own, :].astype(F32)
    state[1] = late[base + own : base + 2 * own, :].astype(F32)
    base += 2 * own
    block = late[base : base + EDGE, :].astype(F32)
    block = block[:8] + block[8:]
    taps[:, 0, :] = block[:K, :own]
    taps[:, 1, :] = block[:K, own : 2 * own]
    taps_bias[0:1, :] = block[K : K + 1, :own]
    taps_bias[1:2, :] = block[K : K + 1, own : 2 * own]
    base += EDGE
    block = late[base : base + EDGE, :].astype(F32)
    gain[...] = (block[0] + block[8])[:own_width]
    out_weight[...] = early[:channels, :].astype(F32)


def ring(axis, distance):
    count = lax.axis_size(axis)
    return [(i, (i + distance) % count) for i in range(count)]


def shifted(block, axis, distance):
    devices = range(lax.axis_size(axis))
    return lax.ppermute(block, axis, [(i - distance, i) for i in devices if i - distance in devices])


def crossed(block, axis, mask):
    return lax.ppermute(block, axis, [(i, i ^ mask) for i in range(lax.axis_size(axis))])


def send_near(parts, axis):
    if len(parts) == 4:
        return [crossed(parts[3], axis, 1), crossed(parts[1], axis, 1)]
    return [lax.ppermute(part, axis, ring(axis, d)) for d, part in enumerate(parts[1:], 1)]


def send_far(parts, near, axis):
    if len(parts) == 4:
        return [crossed(rounded(parts[2].astype(F32) + near[0].astype(F32)), axis, 2)]
    return []


def send_all(parts, axis):
    if len(parts) == 4:
        return [crossed(part, axis, mask) for mask, part in enumerate(parts) if mask]
    return send_near(parts, axis)


def add_up(parts, near, far):
    total = parts[0].astype(F32)
    for piece in (near[1:] if far else near) + far:
        total = total + piece.astype(F32)
    return total


def ordered(*groups):
    flat, tree = jax.tree.flatten(groups)
    return jax.tree.unflatten(tree, lax.optimization_barrier(flat))


def chained(message, reverse, beside):
    count = lax.axis_size("seq")
    core = lax.axis_index("seq") % 2
    later = core == (0 if reverse else 1)
    other = crossed(message, "seq", 1)
    fade, other_fade = message[:, LANES:], other[:, LANES:]
    state, other_state = message[:, :LANES], other[:, :LANES]
    pair = jnp.where(
        later, fade[:, :1] * other_state + state, other_fade[:, :1] * state + other_state
    )
    pair = jnp.concatenate([pair, fade * other_fade], axis=1)
    neutral = (lax.broadcasted_iota(jnp.int32, message.shape, 1) >= LANES).astype(F32)
    near = jnp.where(later, other, neutral)
    sign = -2 if reverse else 2
    pair, beside = ordered(pair, beside)
    return beside, [near] + [shifted(pair, "seq", sign * d) for d in range(1, count // 2)]


def gather_sum(parts):
    total = rounded(jnp.sum(parts.astype(F32), axis=0))
    return lax.all_gather(total, "seq", axis=0, tiled=True)


def on_device(
    tokens, starts, norm_in_gain, inner_weight, state_weight, step_weight, conv_inner,
    conv_inner_bias, conv_state, conv_state_bias, step_bias, decay_log, skip_gain,
    norm_out_gain, out_weight, cotangent,
):
    rows, length, width = tokens.shape
    head_count = step_weight.shape[1]
    channels = inner_weight.shape[2]
    own_state = state_weight.shape[2]
    seq_count, head_devices = lax.axis_size("seq"), lax.axis_size("head")
    groups = length // GROUP
    grid = (rows, groups)
    states = 2 * own_state * head_devices
    own_width = width // head_devices
    me = lax.axis_index("head").reshape(1)

    def sds(shape, dtype=F32):
        return jax.ShapeDtypeStruct(shape, dtype)

    def whole(shape):
        return pl.BlockSpec(shape, lambda r, g: (0,) * len(shape))

    def place(g, reverse):
        return groups - 1 - g if reverse else g

    def block(cols, reverse=False, part=0):
        return pl.BlockSpec((None, GROUP, cols), lambda r, g: (r, place(g, reverse), part))

    def per_row(height, cols):
        return pl.BlockSpec((None, height, cols), lambda r, g: (r, 0, 0))

    def per_group(height, cols, reverse=False):
        return pl.BlockSpec(
            (None, None, height, cols), lambda r, g: (r, place(g, reverse), 0, 0)
        )

    scalar = pl.BlockSpec(memory_space=pltpu.SMEM)
    halo_width = width + LANES
    tail = jnp.concatenate(
        [
            tokens[:, length - EDGE :],
            jnp.broadcast_to(starts[:, length - EDGE :, None], (rows, EDGE, LANES)).astype(BF16),
        ],
        axis=2,
    )
    halo = shifted(tail, "seq", 1)
    state_own = jnp.concatenate(
        [
            state_weight, conv_state, conv_state_bias[None],
            jnp.zeros((LANES - K - 1, 2, own_state), BF16),
        ],
        axis=0,
    ).transpose(1, 2, 0).reshape(2 * own_state, width + LANES)
    found = [state_own] + [
        lax.ppermute(state_own, "head", ring("head", d)) for d in range(1, head_devices)
    ]

    gain_in = norm_in_gain[None]
    gain_out = norm_out_gain[None]
    win = inner_weight.reshape(width, 2 * channels)
    wst = jnp.pad(step_weight, ((0, 0), (0, LANES - head_count)))
    hp = jnp.pad(
        jnp.stack([step_bias, decay_log, skip_gain]), ((0, 5), (0, LANES - head_count))
    )
    ci = jnp.pad(
        jnp.concatenate([conv_inner, conv_inner_bias[None]], axis=0).astype(F32), ((0, 3), (0, 0))
    )
    marked = jnp.broadcast_to(
        starts.astype(F32).reshape(rows, groups, 1, GROUP), (rows, groups, 8, GROUP)
    )

    def act(cols, dtype=F32):
        return sds((rows, length, cols), dtype)

    normed, xpre, gate, raw, step, cum = pl.pallas_call(
        project_kernel,
        grid=grid,
        in_specs=[
            block(width), whole((1, width)), whole((width, 2 * channels)),
            whole((width, LANES)), whole((8, LANES)),
        ],
        out_specs=[
            block(width), block(channels), block(channels), block(LANES), block(LANES),
            block(LANES),
        ],
        out_shape=[
            act(width, BF16), act(channels, BF16), act(channels), act(LANES), act(LANES),
            act(LANES),
        ],
        compiler_params=PARAMS,
        name="project",
        cost_estimate=cost(6),
    )(tokens, gain_in, win, wst, hp)
    (
        yin, xact, bc, spre, fresh, fades, message, halo_x, halo_s, run_all, ws, cs,
    ) = pl.pallas_call(
        functools.partial(forward_kernel, len(found)),
        grid=grid,
        in_specs=[whole((2 * own_state, width + LANES))] * len(found) + [
            per_group(8, GROUP), block(width), block(channels), block(LANES), block(LANES),
            whole((width, 2 * channels)), per_row(EDGE, halo_width), whole((1, width)),
            whole((8, channels)),
        ],
        out_specs=[
            block(channels), block(channels), block(states), block(states),
            per_group(LANES, channels), per_group(8, channels), per_row(LANES + 8, channels),
            per_row(EDGE, channels), per_row(EDGE, states), block(LANES),
            whole((states, width)), whole((8, states)),
        ],
        out_shape=[
            act(channels), act(channels, BF16), act(states, BF16), act(states, BF16),
            sds((rows, groups, LANES, channels)), sds((rows, groups, 8, channels)),
            sds((rows, LANES + 8, channels)), sds((rows, EDGE, channels), BF16),
            sds((rows, EDGE, states), BF16), act(LANES), sds((states, width), BF16),
            sds((8, states)),
        ],
        scratch_shapes=[
            pltpu.VMEM((GROUP + EDGE, channels), F32), pltpu.VMEM((GROUP + EDGE, states), F32),
            pltpu.VMEM((GROUP + EDGE, LANES), F32),
            pltpu.VMEM((LANES, channels), F32), pltpu.VMEM((8, channels), F32),
        ],
        compiler_params=PARAMS,
        name="forward",
        cost_estimate=cost(10),
    )(*found, marked, normed, xpre, step, cum, win, halo, gain_in, ci)

    beside, arrived = chained(message, False, cotangent)
    dn = jnp.einsum("rsd,cd->rsc", beside, out_weight, preferred_element_type=F32)
    mixer, sums, entry_states = pl.pallas_call(
        functools.partial(mix_kernel, len(arrived)),
        grid=grid,
        in_specs=[per_row(LANES + 8, channels)] * len(arrived) + [
            block(channels), block(channels), block(states // 2, part=1), block(channels),
            block(channels), block(LANES), per_group(8, GROUP), whole((1, channels)),
            whole((8, LANES)), per_group(LANES, channels), per_group(8, channels),
        ],
        out_specs=[block(channels), per_group(8, GROUP), per_group(LANES, channels)],
        out_shape=[
            act(channels), sds((rows, groups, 8, GROUP)), sds((rows, groups, LANES, channels)),
        ],
        scratch_shapes=[pltpu.VMEM((LANES, channels), F32)],
        compiler_params=PARAMS,
        name="mix",
        cost_estimate=cost(6),
    )(*arrived, yin, xact, bc, gate, dn, cum, marked, gain_out, hp, fresh, fades)

    sums_all = [sums] + [
        lax.ppermute(sums, "head", ring("head", d)) for d in range(1, head_devices)
    ]
    dy, dgate, normed_out, entering, back_message, grad_gain_out, grad_skip = pl.pallas_call(
        functools.partial(gate_kernel, len(sums_all)),
        grid=grid,
        in_specs=[per_group(8, GROUP, True)] * len(sums_all) + [
            block(channels, True), block(channels, True), block(channels, True),
            block(channels, True), block(states // 2, True, 1), block(LANES, True),
            per_group(8, GROUP, True), whole((1, channels)), whole((8, LANES)),
            per_group(8, channels, True),
        ],
        out_specs=[
            block(channels, True), block(channels, True), block(channels, True),
            per_group(LANES, channels, True), per_row(LANES + 8, channels),
            whole((1, channels)), whole((1, channels)),
        ],
        out_shape=[
            act(channels), act(channels, BF16), act(channels, BF16),
            sds((rows, groups, LANES, channels)), sds((rows, LANES + 8, channels)),
            sds((1, channels)), sds((1, channels)),
        ],
        scratch_shapes=[pltpu.VMEM((LANES, channels), F32), pltpu.VMEM((8, channels), F32)],
        compiler_params=PARAMS,
        name="gate",
        cost_estimate=cost(6),
    )(*sums_all, mixer, gate, dn, xact, bc, cum, marked, gain_out, hp, fades)

    normed_out, returned = chained(back_message, True, normed_out)
    back, early, *branch = pl.pallas_call(
        functools.partial(out_kernel, head_devices),
        grid=grid,
        in_specs=[
            scalar, block(channels), block(width), block(channels), block(width),
            whole((channels, width)), whole((width, 2 * channels)),
        ],
        out_specs=[block(width), whole((2 * channels, width))]
        + [block(own_width)] * head_devices,
        out_shape=[act(width), sds((2 * channels, width), BF16)]
        + [act(own_width, BF16)] * head_devices,
        scratch_shapes=[pltpu.VMEM((2 * channels, width), F32)],
        compiler_params=PARAMS,
        name="out",
        cost_estimate=cost(8),
    )(me, normed_out, cotangent, dgate, normed, out_weight, win)

    column = lax.axis_index("head") * own_width
    own_tokens = lax.dynamic_slice_in_dim(tokens, column, own_width, 2).astype(F32)
    early, returned = ordered(early, returned)
    early = lax.all_to_all(early.reshape(seq_count, -1, width), "seq", 0, 0, tiled=True)
    branch_near = send_all(branch, "head")

    late_rows = channels + 3 * EDGE + 2 * own_state + EDGE
    chunk = -(-late_rows // (seq_count * EDGE)) * EDGE
    packed_rows = channels + 2 * EDGE
    piece_rows = 2 * own_state + EDGE

    def backward_call(start_call, end_call, offset, steps, carried):
        step_size = GROUP // EDGE

        def at(g):
            return offset + steps - 1 - g

        def tile(cols):
            return pl.BlockSpec((None, GROUP, cols), lambda r, g: (r, at(g), 0))

        def before(cols):
            return pl.BlockSpec(
                (None, EDGE, cols), lambda r, g: (r, jnp.maximum(at(g) * step_size - 1, 0), 0)
            )

        def group_tile(height, cols):
            return pl.BlockSpec((None, None, height, cols), lambda r, g: (r, at(g), 0, 0))

        carry_specs = [
            per_row(LANES, channels),
            pl.BlockSpec((None, K, 8, channels), lambda r, g: (r, 0, 0, 0)),
            pl.BlockSpec((None, K, 8, states), lambda r, g: (r, 0, 0, 0)),
            whole((channels + states + EDGE, width)), whole((8, channels)), whole((8, states)),
        ]
        carry_shapes = [
            sds((rows, LANES, channels)), sds((rows, K, 8, channels)), sds((rows, K, 8, states)),
            sds((channels + states + EDGE, width)), sds((8, channels)), sds((8, states)),
        ]
        local = pl.BlockSpec((None, GROUP, own_width), lambda r, g: (r, steps - 1 - g, 0))
        out_specs = [local] * head_devices
        out_shape = [sds((rows, steps * GROUP, own_width), BF16)] * head_devices
        if end_call:
            out_specs += [whole((packed_rows, width))]
            out_specs += [whole((piece_rows, width))] * head_devices
            out_shape += [sds((packed_rows, width), BF16)]
            out_shape += [sds((piece_rows, width), BF16)] * head_devices
        else:
            out_specs += carry_specs
            out_shape += carry_shapes
        lead = returned if start_call else []
        return pl.pallas_call(
            functools.partial(backward_kernel, start_call, end_call, len(lead), head_devices),
            grid=(rows, steps),
            in_specs=[per_row(LANES + 8, channels)] * len(lead)
            + ([] if start_call else carry_specs)
            + [
                scalar, tile(width), per_row(EDGE, halo_width), group_tile(8, GROUP), tile(width),
                tile(channels), before(channels), per_row(EDGE, channels), tile(states),
                before(states), per_row(EDGE, states), tile(channels), tile(states),
                tile(channels), tile(channels), tile(width), tile(LANES), tile(LANES),
                tile(LANES), tile(LANES), group_tile(LANES, channels),
                group_tile(LANES, channels), group_tile(8, channels),
                whole((width, 2 * channels)), whole((states, width)), whole((width, LANES)),
                whole((8, LANES)), whole((8, channels)), whole((8, states)), whole((1, width)),
                whole((1, channels)), whole((1, channels)),
            ],
            out_specs=out_specs,
            out_shape=out_shape,
            scratch_shapes=[
                pltpu.VMEM((GROUP + EDGE, channels), F32),
                pltpu.VMEM((GROUP + EDGE, states), F32),
                pltpu.VMEM((K, GROUP + 2 * EDGE, channels), F32),
                pltpu.VMEM((K, GROUP + 2 * EDGE, states), F32),
                pltpu.VMEM((LANES, channels), F32),
                pltpu.VMEM((channels, width), F32), pltpu.VMEM((states, width), F32),
                pltpu.VMEM((EDGE, width), F32), pltpu.VMEM((8, channels), F32),
                pltpu.VMEM((8, states), F32), pltpu.VMEM((rows, EDGE, width), F32),
            ],
            compiler_params=PARAMS,
            name="backward",
            cost_estimate=cost(15),
        )(
            *lead, *carried, me, tokens, halo, marked, normed, xpre, xpre, halo_x, spre, spre,
            halo_s, xact, bc, yin, dy, back, step, cum, raw, run_all, entry_states, entering,
            fades, win, ws, wst, hp, ci, cs, gain_in, grad_gain_out, grad_skip,
        )

    first = groups // 2
    if first:
        outs = backward_call(True, False, first, groups - first, [])
        outs, early = ordered(outs, early)
        early = gather_sum(early)
        late_parts, carried = outs[:head_devices], outs[head_devices:]
        late_near = send_near(late_parts, "head")
        outs = backward_call(False, True, 0, first, carried)
        outs, branch_near, late_near = ordered(outs, branch_near, late_near)
    else:
        outs = backward_call(True, True, 0, groups, [])
        early = gather_sum(early)
    gtok, packed = outs[:head_devices], outs[head_devices]
    state_parts = outs[head_devices + 1 :]
    state_pieces = [
        lax.ppermute(state_parts[d], "head", ring("head", -d)) for d in range(1, head_devices)
    ]
    gtok_near = send_near(gtok, "head")
    if first:
        late_far = send_far(late_parts, late_near, "head")
    late, edge = pl.pallas_call(
        functools.partial(merge_kernel, own_width),
        out_shape=[
            sds((chunk * seq_count, width), BF16), sds((rows, EDGE, own_width)),
        ],
        compiler_params=pltpu.CompilerParams(vmem_limit_bytes=62 * 2**20),
        cost_estimate=cost(2),
        name="merge",
    )(packed, state_parts[0], *state_pieces)
    late, gtok_near[0] = ordered(late, gtok_near[0])
    parts = lax.all_to_all(late.reshape(seq_count, chunk, -1), "seq", 0, 0, tiled=True)
    gtok_far = send_far(gtok, gtok_near, "head")
    parts, gtok_near = ordered(parts, gtok_near)
    output = rounded(own_tokens + add_up(branch, branch_near, []))
    from_next = shifted(edge, "seq", -1)[:, EDGE - K + 1 :]
    late = gather_sum(parts)
    late, gtok_far = ordered(late, gtok_far)
    token_sums = [add_up(gtok, gtok_near, gtok_far)]
    if first:
        token_sums.append(add_up(late_parts, late_near, late_far))
    own_cot = lax.dynamic_slice_in_dim(cotangent, column, own_width, 2).astype(F32)
    padding = jnp.zeros((rows, length - K + 1, own_width), F32)
    grad_tokens = (
        own_cot + jnp.concatenate(token_sums, axis=1)
        + jnp.concatenate([padding, from_next], axis=1)
    )
    outs = pl.pallas_call(
        functools.partial(unpack_kernel, own_width, head_count),
        out_shape=[
            sds((own_width,)), sds((width, 2, channels)), sds((2, own_state, width)),
            sds((head_count, width)), sds((K, channels)), sds((channels,)),
            sds((K, 2, own_state)), sds((2, own_state)), sds((head_count,)),
            sds((head_count,)), sds((head_count,)), sds((channels,)),
            sds((channels, width)),
        ],
        compiler_params=pltpu.CompilerParams(vmem_limit_bytes=62 * 2**20),
        cost_estimate=cost(4),
        name="unpack",
    )(late, early)
    outs = list(outs)
    outs[2] = outs[2].transpose(2, 0, 1)
    outs[3] = outs[3].T
    return (output, grad_tokens) + tuple(outs)


def solution(mesh):
    return jax.shard_map(
        on_device,
        mesh=mesh,
        in_specs=(
            P(None, "seq", None), P(None, "seq"), P(), P(None, None, "head"),
            P(None, None, "head"), P(None, "head"), P(None, "head"), P("head"),
            P(None, None, "head"), P(None, "head"), P("head"), P("head"), P("head"), P("head"),
            P("head", None), P(None, "seq", None),
        ),
        out_specs=(
            P(None, "seq", "head"), P(None, "seq", "head"), P("head"), P(None, None, "head"),
            P(None, None, "head"), P(None, "head"), P(None, "head"), P("head"),
            P(None, None, "head"), P(None, "head"), P("head"), P("head"), P("head"), P("head"),
            P("head", None),
        ),
        check_vma=False,
    )
```

```python
import functools

import jax
import jax.numpy as jnp
from jax import lax
from jax.experimental import pallas as pl
from jax.experimental.pallas import tpu as pltpu
from jax.sharding import PartitionSpec as P

K = 4
GROUP = 256
DI = 1536
WIDTH = 64
LANES = 128
EDGE = 16
EPSILON = 1e-05
HIGHEST = lax.Precision.HIGHEST
F32 = jnp.float32
BF16 = jnp.bfloat16
FAR = -1e30
PARAMS = pltpu.CompilerParams(
    dimension_semantics=("arbitrary", "arbitrary"), vmem_limit_bytes=62 * 2**20
)


def cost(microseconds):
    return pl.CostEstimate(
        flops=int(microseconds * 1e9), bytes_accessed=int(microseconds * 1e5), transcendentals=0
    )


def rounded(tensor):
    return tensor.astype(BF16)


def dot(a, b, exact=False):
    return jnp.dot(a, b, preferred_element_type=F32, precision=HIGHEST if exact else None)


def dot_nt(a, b, exact=False):
    return lax.dot_general(
        a, b, (((1,), (1,)), ((), ())), preferred_element_type=F32,
        precision=HIGHEST if exact else None,
    )


def dot_tn(a, b, exact=False):
    return lax.dot_general(
        a, b, (((0,), (0,)), ((), ())), preferred_element_type=F32,
        precision=HIGHEST if exact else None,
    )


def iota(shape, dim):
    return lax.broadcasted_iota(jnp.int32, shape, dim)


def halves(tensor):
    high = rounded(tensor)
    return high, rounded(tensor - high.astype(F32))


def expand(tensor, channels):
    both = jnp.concatenate(halves(tensor), axis=1)
    table = iota((2 * LANES, channels), 1) // WIDTH == iota((2 * LANES, channels), 0) % LANES
    return dot(both, table.astype(F32).astype(BF16))


def collect(tensor):
    channels = tensor.shape[1]
    table = iota((channels, LANES), 0) // WIDTH == iota((channels, LANES), 1)
    table = table.astype(F32).astype(BF16)
    high, low = halves(tensor)
    return dot(high, table) + dot(low, table)


def expand_row(row, channels):
    return expand(jnp.broadcast_to(row, (8, LANES)), channels)[:1]


def collect_row(row):
    return collect(jnp.broadcast_to(row, (8, row.shape[1])))[:1]


def triangle(compare):
    return compare(iota((GROUP, GROUP), 0), iota((GROUP, GROUP), 1)).astype(F32).astype(BF16)


def running_counts(marked):
    return dot(marked.astype(BF16), triangle(lambda i, j: i <= j))


def fade_of(cum, counts):
    return jnp.exp(cum[GROUP - 1 :, :]) * (counts[:1, GROUP - 1 :] == 0).astype(F32)


def pack_state(ref, state, fade):
    ref[:LANES, :] = state
    ref[LANES:, :] = jnp.broadcast_to(fade, (8, fade.shape[1]))


def fold_states(pieces):
    state = jnp.zeros((LANES, pieces[0].shape[1]), F32)
    for piece in reversed(pieces):
        state = piece[LANES : LANES + 1, :] * state + piece[:LANES, :]
    return state


def rms_scale(tokens):
    return lax.rsqrt(jnp.mean(tokens * tokens, axis=-1, keepdims=True) + EPSILON)


def head_parts(channels):
    for start in range(0, channels, LANES):
        width = min(LANES, channels - start)
        yield start, width, [start // WIDTH + i for i in range(width // WIDTH)]


def pair_kernel(later, own, other, pair, near):
    flag = later[0] == 1
    mine, theirs = own[...], other[...]
    first, second = jnp.where(flag, theirs, mine), jnp.where(flag, mine, theirs)
    fade = second[:, LANES : LANES + 1]
    pair[:, :LANES] = fade * first[:, :LANES] + second[:, :LANES]
    pair[:, LANES:] = first[:, LANES:] * second[:, LANES:]
    neutral = (iota(mine.shape, 1) >= LANES).astype(F32)
    near[...] = jnp.where(flag, theirs, neutral)


def prepare_kernel(
    tok, starts, state, conv, conv_bias, step, step_bias, decay, skip, conv_x, conv_x_bias,
    gain_in, gain_out, tail, message, norm_in, norm_out, hp, ci, wst, marked, turn,
):
    rows, length = starts.shape
    width = tok.shape[-1]
    own = state.shape[1]
    heads = step.shape[0]
    tail[:, :, :width] = tok[...]
    for line in range(rows):
        for group in range(length // GROUP):
            part = starts[line : line + 1, group * GROUP : (group + 1) * GROUP].astype(F32)
            marked[line, group] = jnp.broadcast_to(part, (8, GROUP))
        last = starts[line : line + 1, length - LANES :].astype(F32)
        column = jnp.broadcast_to(last, (LANES, LANES)).T
        tail[line, :, width:] = rounded(column[LANES - EDGE :])
    message[:, width:] = jnp.zeros((2 * own, LANES), BF16)
    taps = conv[...].astype(F32)
    for kind in range(2):
        message[kind * own : (kind + 1) * own, :width] = state[kind]
        turn[...] = jnp.zeros_like(turn)
        turn[:K, :own] = taps[:, kind, :]
        turn[K : K + 1, :own] = conv_bias[kind : kind + 1, :].astype(F32)
        message[kind * own : (kind + 1) * own, width:] = rounded(turn[...].T[:own])
    norm_in[...] = gain_in[...].reshape(1, -1)
    norm_out[...] = gain_out[...].reshape(1, -1)
    hp[...] = jnp.zeros_like(hp)
    for line, vector in enumerate((step_bias, decay, skip)):
        hp[line : line + 1, :heads] = vector[...].reshape(1, -1)
    ci[...] = jnp.zeros_like(ci)
    ci[:K, :] = conv_x[...].astype(F32)
    ci[K : K + 1, :] = conv_x_bias[...].astype(F32).reshape(1, -1)
    wst[...] = jnp.zeros_like(wst)
    wst[:heads, :] = step[...]


def project_kernel(tok, gain, win, wst, hp, normed, xpre, gate, spre, step, cum):
    channels = xpre.shape[-1]
    tokens = tok[...].astype(F32)
    row = rounded(tokens * rms_scale(tokens) * gain[...])
    normed[...] = row
    product = dot(row, win[...])
    xpre[...] = rounded(product[:, :channels])
    gate[...] = product[:, channels:]
    raw = dot_nt(row, wst[...]) + hp[0:1, :]
    sizes = jax.nn.softplus(raw)
    spre[...] = raw
    step[...] = sizes
    rates = sizes * -jnp.exp(hp[1:2, :])
    lower = triangle(lambda i, j: i >= j)
    high, rest = rounded(rates), rates - rounded(rates).astype(F32)
    middle, low = halves(rest)
    cum[...] = dot(lower, high) + dot(lower, middle) + dot(lower, low)


def convolve(ext, taps, runs):
    summed = taps[K : K + 1, :] + taps[K - 1 : K, :] * ext[pl.ds(EDGE, GROUP), :]
    for lag in range(1, K):
        summed = summed + (
            taps[K - 1 - lag : K - lag, :] * ext[pl.ds(EDGE - lag, GROUP), :]
        ) * runs[lag - 1]
    return summed


def edge_rows(halo, gain, width):
    tokens = halo[:, :width].astype(F32)
    return tokens, rounded(tokens * rms_scale(tokens) * gain[...])


def forward_kernel(count, *refs):
    pieces = refs[:count]
    (
        marked, normed, xpre, step, cum, win, halo, gain, ci,
        yin, xact, bc, spre, fresh, fades, message, halo_x, halo_s, run_out, ws, cs,
        ext_x, ext_s, ext_k, state, total,
    ) = refs[count:]
    group = pl.program_id(1)
    channels = xpre.shape[-1]
    width = normed.shape[-1]
    own = pieces[0].shape[0] // 2

    @pl.when((group == 0) & (pl.program_id(0) == 0))
    def _():
        for place, piece in enumerate(pieces):
            for kind in range(2):
                row = (kind * count + place) * own
                ws[row : row + own, :] = piece[kind * own : (kind + 1) * own, :width]
        taps = jnp.concatenate(
            [p[kind * own : (kind + 1) * own, width:] for kind in range(2) for p in pieces], axis=0
        )
        cs[...] = taps.astype(F32).T[:8]

    @pl.when(group == 0)
    def _():
        _, row = edge_rows(halo, gain, width)
        edge_x = rounded(dot(row, win[:, :channels]))
        edge_s = rounded(dot_nt(row, ws[...]))
        halo_x[...] = edge_x
        halo_s[...] = edge_s
        ext_x[pl.ds(0, EDGE), :] = edge_x.astype(F32)
        ext_s[pl.ds(0, EDGE), :] = edge_s.astype(F32)
        ext_k[pl.ds(0, EDGE), :] = 1.0 - halo[:, width:].astype(F32)
        state[...] = jnp.zeros_like(state)
        total[...] = jnp.ones_like(total)

    @pl.when(group > 0)
    def _():
        ext_x[pl.ds(0, EDGE), :] = ext_x[pl.ds(GROUP, EDGE), :]
        ext_s[pl.ds(0, EDGE), :] = ext_s[pl.ds(GROUP, EDGE), :]
        ext_k[pl.ds(0, EDGE), :] = ext_k[pl.ds(GROUP, EDGE), :]

    counts = running_counts(marked[...])
    counts_column = counts.T[:, :1]
    run1 = 1.0 - marked[...].T[:, :1]
    ext_k[pl.ds(EDGE, GROUP), :] = jnp.broadcast_to(run1, (GROUP, LANES))
    run2 = run1 * ext_k[pl.ds(EDGE - 1, GROUP), :1]
    run3 = run2 * ext_k[pl.ds(EDGE - 2, GROUP), :1]
    runs = (run1, run2, run3)
    lane = iota((GROUP, LANES), 1)
    run_out[...] = jnp.where(lane == 0, run1, jnp.where(lane == 1, run2, run3))
    state_pre = rounded(dot_nt(normed[...], ws[...]))
    spre[...] = state_pre
    ext_s[pl.ds(EDGE, GROUP), :] = state_pre.astype(F32)
    ext_x[pl.ds(EDGE, GROUP), :] = xpre[...].astype(F32)
    conv_x = convolve(ext_x, ci, runs)
    conv_s = convolve(ext_s, cs, runs)
    x = rounded(conv_x * jax.nn.sigmoid(conv_x))
    both = rounded(conv_s * jax.nn.sigmoid(conv_s))
    xact[...] = x
    bc[...] = both
    half = both.shape[1] // 2
    b, c = both[:, :half], both[:, half:]
    cums = cum[...]
    causal = iota((GROUP, GROUP), 0) >= iota((GROUP, GROUP), 1)
    mask = jnp.where(causal & (counts_column == counts[:1]), 0.0, FAR)
    scores = dot_nt(c, b)
    weighted = x.astype(F32) * expand(step[...], channels)
    scaled = rounded(weighted)
    cum_rows = cums.T
    for start, size, heads in head_parts(channels):
        part = scaled[:, start : start + size]
        results = []
        for head in heads:
            decay = jnp.exp(cums[:, head : head + 1] - cum_rows[head : head + 1, :] + mask)
            results.append(dot(rounded(scores * decay), part))
        if len(results) == 2:
            results = [jnp.where(iota((GROUP, size), 1) < WIDTH, results[0], results[1])]
        yin[:, start : start + size] = results[0]
    ending = (counts_column == counts[:1, GROUP - 1 :]).astype(F32)
    reach_end = jnp.exp(cums[GROUP - 1 :, :] - cums) * ending
    new = dot_tn(b, rounded(weighted * expand(reach_end, channels)))
    fresh[...] = new
    fade = expand_row(fade_of(cums, counts), channels)
    fades[...] = jnp.broadcast_to(fade, (8, channels))
    state[...] = fade * state[...] + new
    total[...] = total[...] * fade

    @pl.when(group == pl.num_programs(1) - 1)
    def _():
        pack_state(message, state[...], total[0:1, :])


def mix_kernel(count, *refs):
    pieces = refs[:count]
    (
        yin, x, c, gate, dn, cum, marked, gain, hp, fresh, fades,
        mixer, sums, states, state,
    ) = refs[count:]
    channels = x.shape[-1]

    @pl.when(pl.program_id(1) == 0)
    def _():
        state[...] = fold_states(pieces)

    counts = running_counts(marked[...])
    living = (counts.T[:, :1] == 0).astype(F32)
    now = state[...]
    states[...] = now
    reach = expand(jnp.exp(cum[...]) * living, channels)
    skip = expand_row(hp[2:3, :], channels)
    high, low = halves(now)
    reads = c[...]
    mixed = yin[...] + reach * (dot(reads, high) + dot(reads, low)) + skip * x[...].astype(F32)
    mixer[...] = mixed
    gates = gate[...]
    gated = mixed * (gates * jax.nn.sigmoid(gates))
    square = jnp.sum(gated * gated, axis=1, keepdims=True)
    cross = jnp.sum(gated * (dn[...] * gain[...]), axis=1, keepdims=True)
    lane = iota((GROUP, LANES), 1)
    sums[...] = jnp.where(lane == 0, square, cross).T[:8]
    state[...] = fades[0:1, :] * now + fresh[...]


def gate_kernel(count, *refs):
    pieces = refs[:count]
    (
        mixer, gate, dn, x, c, cum, marked, gain, hp, fades,
        dy, dgate, normed_out, entering, message, grad_gain, grad_skip, state, total,
    ) = refs[count:]
    channels = x.shape[-1]
    last = pl.program_id(1) == 0

    @pl.when(last & (pl.program_id(0) == 0))
    def _():
        grad_gain[...] = jnp.zeros_like(grad_gain)
        grad_skip[...] = jnp.zeros_like(grad_skip)

    @pl.when(last)
    def _():
        state[...] = jnp.zeros_like(state)
        total[...] = jnp.ones_like(total)

    sums = pieces[0][...]
    for piece in pieces[1:]:
        sums = sums + piece[...]
    columns = sums.T
    scale = lax.rsqrt(columns[:, 0:1] / DI + EPSILON)
    pull = scale * scale * scale * (columns[:, 1:2] / DI)
    counts = running_counts(marked[...])
    living = (counts.T[:, :1] == 0).astype(F32)
    mixed = mixer[...]
    gates = gate[...]
    squash = jax.nn.sigmoid(gates)
    act = gates * squash
    gated = mixed * act
    norm_grad = dn[...]
    grad_gated = scale * (norm_grad * gain[...]) - gated * pull
    down = grad_gated * act
    dy[...] = down
    dgate[...] = rounded(grad_gated * mixed * (squash * (1.0 + gates * (1.0 - squash))))
    scaled = gated * scale
    normed_out[...] = rounded(scaled * gain[...])
    grad_gain[...] += jnp.sum(norm_grad * scaled, axis=0, keepdims=True)
    grad_skip[...] += jnp.sum(down * x[...].astype(F32), axis=0, keepdims=True)
    reach = expand(jnp.exp(cum[...]) * living, channels)
    new = dot_tn(c[...], rounded(reach * down))
    entering[...] = new
    fade = fades[0:1, :]
    state[...] = fade * state[...] + new
    total[...] = total[...] * fade

    @pl.when(pl.program_id(1) == pl.num_programs(1) - 1)
    def _():
        pack_state(message, state[...], total[0:1, :])


def store_parts(refs, tensor, me):
    width = tensor.shape[1]
    own = width // len(refs)
    turned = rounded(pltpu.roll(tensor, (len(refs) - me) % len(refs) * own, 1))
    blocks = [turned[:, part * own : (part + 1) * own] for part in range(len(refs))]
    if len(refs) == 4:
        odd = me % 2 == 1
        swapped = [jnp.where(odd, blocks[4 - part], blocks[part]) for part in (1, 3)]
        blocks = [blocks[0], swapped[0], blocks[2], swapped[1]]
    for block, ref in zip(blocks, refs):
        ref[...] = block


def branch_kernel(me, normed_out, wout, *branch):
    store_parts(branch, dot(normed_out[...], wout[...]), me[0])


def out_kernel(normed_out, cot, dgate, normed, grads, total):
    channels = normed_out.shape[1]

    @pl.when((pl.program_id(1) == 0) & (pl.program_id(0) == 0))
    def _():
        total[...] = jnp.zeros_like(total)

    total[:channels, :] += dot_tn(normed_out[...], cot[...])
    total[channels : 2 * channels, :] += dot_tn(dgate[...], normed[...])

    @pl.when(
        (pl.program_id(1) == pl.num_programs(1) - 1)
        & (pl.program_id(0) == pl.num_programs(0) - 1)
    )
    def _():
        grads[...] = rounded(total[...])


def token_grad(tokens, gain, down):
    scale = rms_scale(tokens)
    pulled = down * gain
    inner = jnp.mean(pulled * tokens, axis=-1, keepdims=True)
    grad = scale * pulled - tokens * (scale * scale * scale * inner)
    return grad, jnp.sum(down * tokens * scale, axis=0, keepdims=True)


def deconvolve(ext, buffers, taps, runs, grad_out, grad_taps):
    rows = GROUP + EDGE
    grad_taps[K : K + 1, :] += jnp.sum(grad_out, axis=0, keepdims=True)
    result = None
    for lag in range(K):
        masked = grad_out if lag == 0 else grad_out * runs[lag - 1]
        buffer = buffers.at[lag]
        buffer[pl.ds(EDGE, GROUP), :] = masked
        tap = K - 1 - lag
        grad_taps[tap : tap + 1, :] += jnp.sum(
            masked * ext[pl.ds(EDGE - lag, GROUP), :], axis=0, keepdims=True
        )
        piece = taps[tap : tap + 1, :] * buffer[pl.ds(lag, rows), :]
        result = piece if result is None else result + piece
        buffer[pl.ds(EDGE + GROUP, 8), :] = masked[:8]
    return rounded(result)


def swish_slope(tensor):
    squash = jax.nn.sigmoid(tensor)
    return squash * (1.0 + tensor * (1.0 - squash))


def backward_kernel(start_call, end_call, count, parts, *refs):
    pieces, refs = refs[:count], refs[count:]
    carried, refs = (refs[:0], refs) if start_call else (refs[:6], refs[6:])
    (
        me, tok, halo, marked, normed, xpre, xprev, halo_x, spre, sprev, halo_s, xact, bc, yin, dy,
        back, step, cum, raw, run_in, states, entering, fades, win, ws, wst, hp, ci, cs, gain, gain_out, skip_out,
    ), refs = refs[:32], refs[32:]
    gtok, refs = refs[:parts], refs[parts:]
    if end_call:
        (packed, *state_out), refs = refs[: 1 + parts], refs[1 + parts :]
    else:
        carry_out, refs = refs[:6], refs[6:]
    (
        ext_x, ext_s, buf_x, buf_s, state, grad_x, grad_s, grad_misc, grad_ci, grad_cs, edges,
    ) = refs
    channels = xact.shape[-1]
    width = tok.shape[-1]
    half = bc.shape[-1] // 2
    order = pl.program_id(1)
    row_id = pl.program_id(0)
    closing = order == pl.num_programs(1) - 1
    sums = (grad_x, grad_s, grad_misc, grad_ci, grad_cs)

    @pl.when((order == 0) & (row_id == 0))
    def _():
        if start_call:
            for ref in sums:
                ref[...] = jnp.zeros_like(ref)
        else:
            grad_x[...] = carried[3][:channels]
            grad_s[...] = carried[3][channels : channels + 2 * half]
            grad_misc[...] = carried[3][channels + 2 * half :]
            grad_ci[...] = carried[4][...]
            grad_cs[...] = carried[5][...]

    @pl.when(order == 0)
    def _():
        for buf in (buf_x, buf_s):
            buf[...] = jnp.zeros_like(buf)
        if start_call:
            state[...] = fold_states(pieces)
        else:
            state[...] = carried[0][...]
            buf_x[:, pl.ds(EDGE + GROUP, 8), :] = carried[1][...]
            buf_s[:, pl.ds(EDGE + GROUP, 8), :] = carried[2][...]

    first_group = closing if end_call else False
    ext_x[pl.ds(EDGE, GROUP), :] = xpre[...].astype(F32)
    ext_s[pl.ds(EDGE, GROUP), :] = spre[...].astype(F32)
    before_x, before_s = xprev[...].astype(F32), sprev[...].astype(F32)
    if end_call:
        before_x = jnp.where(first_group, halo_x[...].astype(F32), before_x)
        before_s = jnp.where(first_group, halo_s[...].astype(F32), before_s)
    ext_x[pl.ds(0, EDGE), :] = before_x
    ext_s[pl.ds(0, EDGE), :] = before_s

    counts = running_counts(marked[...])
    counts_column = counts.T[:, :1]
    runs = [run_in[:, lag : lag + 1] for lag in range(K - 1)]
    living = (counts_column == 0).astype(F32)
    x = xact[...].astype(F32)
    both = bc[...]
    b, c = both[:, :half], both[:, half:]
    cums = cum[...]
    cum_rows = cums.T
    steps = step[...]
    step_wide = expand(steps, channels)
    weighted = x * step_wide
    scaled = rounded(weighted)
    down = dy[...]
    down_low = rounded(down)
    causal = iota((GROUP, GROUP), 0) <= iota((GROUP, GROUP), 1)
    mask = jnp.where(causal & (counts_column == counts[:1]), 0.0, FAR)
    scores = dot_nt(b, c)
    grad_scores = jnp.zeros((GROUP, GROUP), F32)
    inside = []
    for start, size, heads in head_parts(channels):
        part = scaled[:, start : start + size]
        slope = down_low[:, start : start + size]
        lane = iota((GROUP, size), 1)
        results = []
        for place, head in enumerate(heads):
            decay = jnp.exp(cum_rows[head : head + 1, :] - cums[:, head : head + 1] + mask)
            results.append(dot(rounded(scores * decay), slope))
            own = part
            if len(heads) == 2:
                keep = (lane < WIDTH) if place == 0 else (lane >= WIDTH)
                own = jnp.where(keep, part, jnp.zeros_like(part))
            grad_scores = grad_scores + dot_nt(own, slope) * decay
        if len(results) == 2:
            results = [jnp.where(lane < WIDTH, results[0], results[1])]
        inside.append(results[0])
    inside = jnp.concatenate(inside, axis=1) if len(inside) > 1 else inside[0]

    later = state[...]
    later_high, later_low = halves(later)
    now = states[...]
    now_high, now_low = halves(now)
    ending = (counts_column == counts[:1, GROUP - 1 :]).astype(F32)
    reach_end = expand(jnp.exp(cums[GROUP - 1 :, :] - cums) * ending, channels)
    reach = expand(jnp.exp(cums) * living, channels)
    arriving = reach_end * (dot(b, later_high) + dot(b, later_low))
    grad_weighted = inside + arriving
    reached = reach * down
    outside = reached * (dot(c, now_high) + dot(c, now_low))
    fade = fades[0:1, :]
    fade_grad = collect_row(fade * jnp.sum(later * now, axis=0, keepdims=True))
    per_position = collect(
        down_low.astype(F32) * yin[...] - scaled.astype(F32) * inside + outside
    )
    per_ending = collect(weighted * arriving)
    direct = collect(x * grad_weighted)
    position_high, position_low = halves(per_position)
    ending_high, ending_low = halves(per_ending)
    upper = triangle(lambda i, j: i <= j)
    under = triangle(lambda i, j: i > j)
    grad_rate = (
        dot(upper, position_high) + dot(upper, position_low)
        + dot(under, ending_high) + dot(under, ending_low) + fade_grad
    )
    rate = -jnp.exp(hp[1:2, :])
    grad_pre = (direct + rate * grad_rate) * jax.nn.sigmoid(raw[...])
    grad_raw = rounded(grad_pre)
    skip = expand_row(hp[2:3, :], channels)
    grad_inputs = step_wide * grad_weighted + skip * down
    low_scores = rounded(grad_scores)
    ended = rounded(weighted * reach_end)
    reached_low = rounded(reached)
    grad_b = dot(low_scores, c) + dot_nt(ended, later_high) + dot_nt(ended, later_low)
    grad_c = dot_tn(low_scores, b) + dot_nt(reached_low, now_high) + dot_nt(reached_low, now_low)
    state[...] = fade * later + entering[...]

    conv_x = convolve(ext_x, ci, runs)
    grad_x_out = grad_inputs * swish_slope(conv_x)
    conv_s = convolve(ext_s, cs, runs)
    grad_s_out = jnp.concatenate([grad_b, grad_c], axis=1) * swish_slope(conv_s)
    back_x = deconvolve(ext_x, buf_x, ci, runs, grad_x_out, grad_ci)
    back_s = deconvolve(ext_s, buf_s, cs, runs, grad_s_out, grad_cs)
    row = normed[...]
    main_x, main_s = back_x[EDGE:], back_s[EDGE:]
    grad_x[...] += dot_tn(main_x, row)
    grad_s[...] += dot_tn(main_s, row)
    grad_normed = (
        dot_nt(jnp.concatenate([main_x, back[...]], axis=1), win[...]) + dot(main_s, ws[...])
        + dot(grad_raw, wst[...])
    )
    grad, gain_part = token_grad(tok[...].astype(F32), gain[...], grad_normed)
    grad_misc[0:8, :] += dot_tn(grad_raw, row)[:8]
    grad_misc[8:9, :] += gain_part
    grad_misc[9:10, :LANES] += jnp.sum(grad_pre, axis=0, keepdims=True)
    grad_misc[10:11, :LANES] += rate * jnp.sum(steps * grad_rate, axis=0, keepdims=True)
    store_parts(gtok, grad, me[0])

    if not end_call:
        @pl.when(closing)
        def _():
            carry_out[0][...] = state[...]
            carry_out[1][...] = buf_x[:, pl.ds(EDGE + GROUP, 8), :]
            carry_out[2][...] = buf_s[:, pl.ds(EDGE + GROUP, 8), :]

            @pl.when(row_id == pl.num_programs(0) - 1)
            def _():
                carry_out[3][:channels] = grad_x[...]
                carry_out[3][channels : channels + 2 * half] = grad_s[...]
                carry_out[3][channels + 2 * half :] = grad_misc[...]
                carry_out[4][...] = grad_ci[...]
                carry_out[5][...] = grad_cs[...]
        return

    @pl.when(closing)
    def _():
        tokens, edge_row = edge_rows(halo, gain, width)
        edge_x, edge_s = back_x[:EDGE], back_s[:EDGE]
        grad_x[...] += dot_tn(edge_x, edge_row)
        grad_s[...] += dot_tn(edge_s, edge_row)
        edge_grad = dot_nt(edge_x, win[:, :channels]) + dot(edge_s, ws[...])
        grad, gain_part = token_grad(tokens, gain[...], edge_grad)
        grad_misc[8:9, :] += gain_part
        everything = grad_misc[8:9, :]
        high = everything.astype(BF16).astype(F32)
        place = iota((EDGE, 1), 0)
        final = row_id == pl.num_programs(0) - 1
        nothing = jnp.zeros_like(high)
        high, rest = jnp.where(final, high, nothing), jnp.where(final, everything - high, nothing)
        edge = jnp.where(place == 0, high, jnp.where(place == 1, rest, grad))
        edges[row_id] = edge

        @pl.when(final)
        def _():
            def padded(block):
                if block.shape[1] == width:
                    return block
                blank = jnp.zeros((8, width - block.shape[1]), F32)
                return jnp.concatenate([block, blank], axis=1)

            def both_halves(block):
                whole = padded(block)
                upper_half = whole.astype(BF16).astype(F32)
                return rounded(jnp.concatenate([upper_half, whole - upper_half], axis=0))

            packed[:channels, :] = rounded(grad_x[...])
            misc = grad_misc[...]
            fine = misc - misc.astype(BF16).astype(F32)
            packed[channels : channels + EDGE, :] = rounded(
                jnp.concatenate([misc[:11], fine[9:11], misc[13:]], axis=0)
            )
            grad_ci[K + 1 : K + 2, :] = gain_out[...]
            grad_ci[K + 2 : K + 3, :LANES] = collect_row(skip_out[...])
            packed[channels + EDGE : channels + 2 * EDGE, :] = both_halves(grad_ci[...])
            own = half // parts
            taps = grad_cs[...]
            for part, ref in enumerate(state_out):
                lo, hi = part * own, (part + 1) * own
                ref[:own, :] = rounded(grad_s[lo:hi, :])
                ref[own : 2 * own, :] = rounded(grad_s[half + lo : half + hi, :])
                ref[2 * own :, :] = both_halves(
                    jnp.concatenate([taps[:, lo:hi], taps[:, half + lo : half + hi]], axis=1)
                )
            own = width // parts
            for line in range(edges.shape[0]):
                shift = (parts - me[0]) % parts * own
                turned = rounded(pltpu.roll(edges[line], shift, 1))
                for part, ref in enumerate(state_out):
                    begin = (parts - part) % parts * own
                    ref[2 * (half // parts) :, LANES + line * own : LANES + (line + 1) * own] = (
                        turned[:, begin : begin + own]
                    )


def merge_kernel(own_width, packed, *refs):
    *pieces, late, edge = refs
    base = packed.shape[0]
    total = pieces[0][...].astype(F32)
    for piece in pieces[1:]:
        total = total + piece[...].astype(F32)
    body = total.shape[0] - EDGE
    rows = edge.shape[0]
    late[:base, :] = packed[...]
    late[base : base + body, :] = rounded(total[:body])
    tail = total[body:]
    for line in range(rows):
        edge[line] = tail[:, LANES + line * own_width : LANES + (line + 1) * own_width]

    def both_halves(block):
        upper_half = block.astype(BF16).astype(F32)
        return jnp.concatenate([upper_half, block - upper_half], axis=0)

    place = base + body
    late[place : place + EDGE, :] = rounded(both_halves(tail[:8] + tail[8:]))
    place += EDGE
    begin = LANES + (rows - 1) * own_width
    gain = jnp.broadcast_to(tail[0:1] + tail[1:2], (8, tail.shape[1]))
    late[place : place + EDGE, :] = jnp.zeros((EDGE, tail.shape[1]), BF16)
    late[place : place + EDGE, :own_width] = rounded(both_halves(gain))[:, begin : begin + own_width]
    if late.shape[0] > place + EDGE:
        rest = late.shape[0] - place - EDGE
        late[place + EDGE :, :] = jnp.zeros((rest, tail.shape[1]), BF16)


def unpack_kernel(
    own_width, head_count, late, early, gain, inner, state, step, conv, conv_bias, taps,
    taps_bias, step_bias, decay, skip, gain_out, out_weight,
):
    channels, width = out_weight.shape
    own = state.shape[1]
    inner[:, 0, :] = late[:channels, :].astype(F32).T
    inner[:, 1, :] = early[channels : 2 * channels, :].astype(F32).T
    base = channels
    misc = late[base : base + EDGE, :].astype(F32)
    step[...] = misc[:head_count]
    step_bias[...] = (misc[9] + misc[11])[:head_count]
    decay[...] = (misc[10] + misc[12])[:head_count]
    base += EDGE
    block = late[base : base + EDGE, :].astype(F32)
    block = block[:8] + block[8:]
    conv[...] = block[:K, :channels]
    conv_bias[...] = block[K, :channels]
    gain_out[...] = block[K + 1, :channels]
    skip[...] = block[K + 2, :head_count]
    base += EDGE
    state[0] = late[base : base + own, :].astype(F32)
    state[1] = late[base + own : base + 2 * own, :].astype(F32)
    base += 2 * own
    block = late[base : base + EDGE, :].astype(F32)
    block = block[:8] + block[8:]
    taps[:, 0, :] = block[:K, :own]
    taps[:, 1, :] = block[:K, own : 2 * own]
    taps_bias[0:1, :] = block[K : K + 1, :own]
    taps_bias[1:2, :] = block[K : K + 1, own : 2 * own]
    base += EDGE
    block = late[base : base + EDGE, :].astype(F32)
    gain[...] = (block[0] + block[8])[:own_width]
    out_weight[...] = early[:channels, :].astype(F32)


def ring(axis, distance):
    count = lax.axis_size(axis)
    return [(i, (i + distance) % count) for i in range(count)]


def shifted(block, axis, distance):
    devices = range(lax.axis_size(axis))
    return lax.ppermute(block, axis, [(i - distance, i) for i in devices if i - distance in devices])


def crossed(block, axis, mask):
    return lax.ppermute(block, axis, [(i, i ^ mask) for i in range(lax.axis_size(axis))])


def send_near(parts, axis):
    if len(parts) == 4:
        return [crossed(parts[3], axis, 1), crossed(parts[1], axis, 1)]
    return [lax.ppermute(part, axis, ring(axis, d)) for d, part in enumerate(parts[1:], 1)]


def send_far(parts, near, axis):
    if len(parts) == 4:
        return [crossed(rounded(parts[2].astype(F32) + near[0].astype(F32)), axis, 2)]
    return []


def send_all(parts, axis):
    if len(parts) == 4:
        return [crossed(part, axis, mask) for mask, part in enumerate(parts) if mask]
    return send_near(parts, axis)


def add_up(parts, near, far):
    total = parts[0].astype(F32)
    for piece in (near[1:] if far else near) + far:
        total = total + piece.astype(F32)
    return total


def ordered(*groups):
    flat, tree = jax.tree.flatten(groups)
    return jax.tree.unflatten(tree, lax.optimization_barrier(flat))


def chained(message, reverse, beside):
    count = lax.axis_size("seq")
    core = lax.axis_index("seq") % 2
    later = core == (0 if reverse else 1)
    other = crossed(message, "seq", 1)
    pair, near = pl.pallas_call(
        pair_kernel,
        in_specs=[pl.BlockSpec(memory_space=pltpu.SMEM)]
        + [pl.BlockSpec(memory_space=pltpu.VMEM)] * 2,
        out_shape=[jax.ShapeDtypeStruct(message.shape, F32)] * 2,
        compiler_params=pltpu.CompilerParams(vmem_limit_bytes=62 * 2**20),
        cost_estimate=cost(1),
        name="pair",
    )(later.astype(jnp.int32).reshape(1), message, other)
    sign = -2 if reverse else 2
    pair, beside = ordered(pair, beside)
    return beside, [near] + [shifted(pair, "seq", sign * d) for d in range(1, count // 2)]


def gather_sum(parts):
    total = rounded(jnp.sum(parts.astype(F32), axis=0))
    return lax.all_gather(total, "seq", axis=0, tiled=True)


def on_device(
    tokens, starts, norm_in_gain, inner_weight, state_weight, step_weight, conv_inner,
    conv_inner_bias, conv_state, conv_state_bias, step_bias, decay_log, skip_gain,
    norm_out_gain, out_weight, cotangent,
):
    rows, length, width = tokens.shape
    head_count = step_weight.shape[1]
    channels = inner_weight.shape[2]
    own_state = state_weight.shape[2]
    seq_count, head_devices = lax.axis_size("seq"), lax.axis_size("head")
    groups = length // GROUP
    grid = (rows, groups)
    states = 2 * own_state * head_devices
    own_width = width // head_devices
    me = lax.axis_index("head").reshape(1)

    def sds(shape, dtype=F32):
        return jax.ShapeDtypeStruct(shape, dtype)

    def whole(shape):
        return pl.BlockSpec(shape, lambda r, g: (0,) * len(shape))

    def place(g, reverse):
        return groups - 1 - g if reverse else g

    def block(cols, reverse=False, part=0):
        return pl.BlockSpec((None, GROUP, cols), lambda r, g: (r, place(g, reverse), part))

    def per_row(height, cols):
        return pl.BlockSpec((None, height, cols), lambda r, g: (r, 0, 0))

    def per_group(height, cols, reverse=False):
        return pl.BlockSpec(
            (None, None, height, cols), lambda r, g: (r, place(g, reverse), 0, 0)
        )

    scalar = pl.BlockSpec(memory_space=pltpu.SMEM)
    halo_width = width + LANES
    tail, state_own, gain_in, gain_out, hp, ci, wst, marked = pl.pallas_call(
        prepare_kernel,
        grid=(1,),
        in_specs=[
            pl.BlockSpec((rows, EDGE, width), lambda i: (0, length // EDGE - 1, 0)),
        ] + [pl.BlockSpec(memory_space=pltpu.VMEM)] * 12,
        out_specs=[pl.BlockSpec(memory_space=pltpu.VMEM)] * 8,
        out_shape=[
            sds((rows, EDGE, halo_width), BF16), sds((2 * own_state, halo_width), BF16),
            sds((1, width)), sds((1, channels)), sds((8, LANES)), sds((8, channels)),
            sds((LANES, width), BF16), sds((rows, groups, 8, GROUP)),
        ],
        scratch_shapes=[pltpu.VMEM((LANES, LANES), F32)],
        compiler_params=pltpu.CompilerParams(vmem_limit_bytes=62 * 2**20),
        cost_estimate=cost(2),
        name="prepare",
    )(
        tokens, starts, state_weight.transpose(1, 2, 0), conv_state, conv_state_bias,
        step_weight.T, step_bias, decay_log, skip_gain, conv_inner, conv_inner_bias,
        norm_in_gain, norm_out_gain,
    )
    halo = shifted(tail, "seq", 1)
    found = [state_own] + [
        lax.ppermute(state_own, "head", ring("head", d)) for d in range(1, head_devices)
    ]

    win = inner_weight.reshape(width, 2 * channels)

    def act(cols, dtype=F32):
        return sds((rows, length, cols), dtype)

    normed, xpre, gate, raw, step, cum = pl.pallas_call(
        project_kernel,
        grid=grid,
        in_specs=[
            block(width), whole((1, width)), whole((width, 2 * channels)),
            whole((LANES, width)), whole((8, LANES)),
        ],
        out_specs=[
            block(width), block(channels), block(channels), block(LANES), block(LANES),
            block(LANES),
        ],
        out_shape=[
            act(width, BF16), act(channels, BF16), act(channels), act(LANES), act(LANES),
            act(LANES),
        ],
        compiler_params=PARAMS,
        name="project",
        cost_estimate=cost(6),
    )(tokens, gain_in, win, wst, hp)
    (
        yin, xact, bc, spre, fresh, fades, message, halo_x, halo_s, run_all, ws, cs,
    ) = pl.pallas_call(
        functools.partial(forward_kernel, len(found)),
        grid=grid,
        in_specs=[whole((2 * own_state, width + LANES))] * len(found) + [
            per_group(8, GROUP), block(width), block(channels), block(LANES), block(LANES),
            whole((width, 2 * channels)), per_row(EDGE, halo_width), whole((1, width)),
            whole((8, channels)),
        ],
        out_specs=[
            block(channels), block(channels), block(states), block(states),
            per_group(LANES, channels), per_group(8, channels), per_row(LANES + 8, channels),
            per_row(EDGE, channels), per_row(EDGE, states), block(LANES),
            whole((states, width)), whole((8, states)),
        ],
        out_shape=[
            act(channels), act(channels, BF16), act(states, BF16), act(states, BF16),
            sds((rows, groups, LANES, channels)), sds((rows, groups, 8, channels)),
            sds((rows, LANES + 8, channels)), sds((rows, EDGE, channels), BF16),
            sds((rows, EDGE, states), BF16), act(LANES), sds((states, width), BF16),
            sds((8, states)),
        ],
        scratch_shapes=[
            pltpu.VMEM((GROUP + EDGE, channels), F32), pltpu.VMEM((GROUP + EDGE, states), F32),
            pltpu.VMEM((GROUP + EDGE, LANES), F32),
            pltpu.VMEM((LANES, channels), F32), pltpu.VMEM((8, channels), F32),
        ],
        compiler_params=PARAMS,
        name="forward",
        cost_estimate=cost(10),
    )(*found, marked, normed, xpre, step, cum, win, halo, gain_in, ci)

    beside, arrived = chained(message, False, cotangent)
    dn = jnp.einsum("rsd,cd->rsc", beside, out_weight, preferred_element_type=F32)
    mixer, sums, entry_states = pl.pallas_call(
        functools.partial(mix_kernel, len(arrived)),
        grid=grid,
        in_specs=[per_row(LANES + 8, channels)] * len(arrived) + [
            block(channels), block(channels), block(states // 2, part=1), block(channels),
            block(channels), block(LANES), per_group(8, GROUP), whole((1, channels)),
            whole((8, LANES)), per_group(LANES, channels), per_group(8, channels),
        ],
        out_specs=[block(channels), per_group(8, GROUP), per_group(LANES, channels)],
        out_shape=[
            act(channels), sds((rows, groups, 8, GROUP)), sds((rows, groups, LANES, channels)),
        ],
        scratch_shapes=[pltpu.VMEM((LANES, channels), F32)],
        compiler_params=PARAMS,
        name="mix",
        cost_estimate=cost(6),
    )(*arrived, yin, xact, bc, gate, dn, cum, marked, gain_out, hp, fresh, fades)

    sums_all = [sums] + [
        lax.ppermute(sums, "head", ring("head", d)) for d in range(1, head_devices)
    ]
    dy, dgate, normed_out, entering, back_message, grad_gain_out, grad_skip = pl.pallas_call(
        functools.partial(gate_kernel, len(sums_all)),
        grid=grid,
        in_specs=[per_group(8, GROUP, True)] * len(sums_all) + [
            block(channels, True), block(channels, True), block(channels, True),
            block(channels, True), block(states // 2, True, 1), block(LANES, True),
            per_group(8, GROUP, True), whole((1, channels)), whole((8, LANES)),
            per_group(8, channels, True),
        ],
        out_specs=[
            block(channels, True), block(channels, True), block(channels, True),
            per_group(LANES, channels, True), per_row(LANES + 8, channels),
            whole((1, channels)), whole((1, channels)),
        ],
        out_shape=[
            act(channels), act(channels, BF16), act(channels, BF16),
            sds((rows, groups, LANES, channels)), sds((rows, LANES + 8, channels)),
            sds((1, channels)), sds((1, channels)),
        ],
        scratch_shapes=[pltpu.VMEM((LANES, channels), F32), pltpu.VMEM((8, channels), F32)],
        compiler_params=PARAMS,
        name="gate",
        cost_estimate=cost(6),
    )(*sums_all, mixer, gate, dn, xact, bc, cum, marked, gain_out, hp, fades)

    branch = pl.pallas_call(
        branch_kernel,
        grid=grid,
        in_specs=[scalar, block(channels), whole((channels, width))],
        out_specs=[block(own_width)] * head_devices,
        out_shape=[act(own_width, BF16)] * head_devices,
        compiler_params=PARAMS,
        cost_estimate=cost(3),
        name="branch",
    )(me, normed_out, out_weight)
    branch_near = send_all(branch, "head")
    normed_out, returned = chained(back_message, True, normed_out)
    early = pl.pallas_call(
        out_kernel,
        grid=grid,
        in_specs=[block(channels), block(width), block(channels), block(width)],
        out_specs=whole((2 * channels, width)),
        out_shape=sds((2 * channels, width), BF16),
        scratch_shapes=[pltpu.VMEM((2 * channels, width), F32)],
        compiler_params=PARAMS,
        cost_estimate=cost(5),
        name="out",
    )(normed_out, cotangent, dgate, normed)

    column = lax.axis_index("head") * own_width
    own_tokens = lax.dynamic_slice_in_dim(tokens, column, own_width, 2).astype(F32)

    early = lax.all_to_all(early.reshape(seq_count, -1, width), "seq", 0, 0, tiled=True)

    late_rows = channels + 3 * EDGE + 2 * own_state + EDGE
    chunk = -(-late_rows // (seq_count * EDGE)) * EDGE
    packed_rows = channels + 2 * EDGE
    piece_rows = 2 * own_state + EDGE

    def backward_call(start_call, end_call, offset, steps, carried):
        step_size = GROUP // EDGE

        def at(g):
            return offset + steps - 1 - g

        def tile(cols):
            return pl.BlockSpec((None, GROUP, cols), lambda r, g: (r, at(g), 0))

        def before(cols):
            return pl.BlockSpec(
                (None, EDGE, cols), lambda r, g: (r, jnp.maximum(at(g) * step_size - 1, 0), 0)
            )

        def group_tile(height, cols):
            return pl.BlockSpec((None, None, height, cols), lambda r, g: (r, at(g), 0, 0))

        carry_specs = [
            per_row(LANES, channels),
            pl.BlockSpec((None, K, 8, channels), lambda r, g: (r, 0, 0, 0)),
            pl.BlockSpec((None, K, 8, states), lambda r, g: (r, 0, 0, 0)),
            whole((channels + states + EDGE, width)), whole((8, channels)), whole((8, states)),
        ]
        carry_shapes = [
            sds((rows, LANES, channels)), sds((rows, K, 8, channels)), sds((rows, K, 8, states)),
            sds((channels + states + EDGE, width)), sds((8, channels)), sds((8, states)),
        ]
        local = pl.BlockSpec((None, GROUP, own_width), lambda r, g: (r, steps - 1 - g, 0))
        out_specs = [local] * head_devices
        out_shape = [sds((rows, steps * GROUP, own_width), BF16)] * head_devices
        if end_call:
            out_specs += [whole((packed_rows, width))]
            out_specs += [whole((piece_rows, width))] * head_devices
            out_shape += [sds((packed_rows, width), BF16)]
            out_shape += [sds((piece_rows, width), BF16)] * head_devices
        else:
            out_specs += carry_specs
            out_shape += carry_shapes
        lead = returned if start_call else []
        return pl.pallas_call(
            functools.partial(backward_kernel, start_call, end_call, len(lead), head_devices),
            grid=(rows, steps),
            in_specs=[per_row(LANES + 8, channels)] * len(lead)
            + ([] if start_call else carry_specs)
            + [
                scalar, tile(width), per_row(EDGE, halo_width), group_tile(8, GROUP), tile(width),
                tile(channels), before(channels), per_row(EDGE, channels), tile(states),
                before(states), per_row(EDGE, states), tile(channels), tile(states),
                tile(channels), tile(channels), tile(channels), tile(LANES), tile(LANES),
                tile(LANES), tile(LANES), group_tile(LANES, channels),
                group_tile(LANES, channels), group_tile(8, channels),
                whole((width, 2 * channels)), whole((states, width)), whole((LANES, width)),
                whole((8, LANES)), whole((8, channels)), whole((8, states)), whole((1, width)),
                whole((1, channels)), whole((1, channels)),
            ],
            out_specs=out_specs,
            out_shape=out_shape,
            scratch_shapes=[
                pltpu.VMEM((GROUP + EDGE, channels), F32),
                pltpu.VMEM((GROUP + EDGE, states), F32),
                pltpu.VMEM((K, GROUP + 2 * EDGE, channels), F32),
                pltpu.VMEM((K, GROUP + 2 * EDGE, states), F32),
                pltpu.VMEM((LANES, channels), F32),
                pltpu.VMEM((channels, width), F32), pltpu.VMEM((states, width), F32),
                pltpu.VMEM((EDGE, width), F32), pltpu.VMEM((8, channels), F32),
                pltpu.VMEM((8, states), F32), pltpu.VMEM((rows, EDGE, width), F32),
            ],
            compiler_params=PARAMS,
            name="backward",
            cost_estimate=cost(15),
        )(
            *lead, *carried, me, tokens, halo, marked, normed, xpre, xpre, halo_x, spre, spre,
            halo_s, xact, bc, yin, dy, dgate, step, cum, raw, run_all, entry_states, entering,
            fades, win, ws, wst, hp, ci, cs, gain_in, grad_gain_out, grad_skip,
        )

    first = groups // 2
    if first:
        outs = backward_call(True, False, first, groups - first, [])
        outs, early = ordered(outs, early)
        early = gather_sum(early)
        late_parts, carried = outs[:head_devices], outs[head_devices:]
        late_near = send_near(late_parts, "head")
        outs = backward_call(False, True, 0, first, carried)
        outs, branch_near, late_near = ordered(outs, branch_near, late_near)
    else:
        outs = backward_call(True, True, 0, groups, [])
        early = gather_sum(early)
    gtok, packed = outs[:head_devices], outs[head_devices]
    state_parts = outs[head_devices + 1 :]
    state_pieces = [
        lax.ppermute(state_parts[d], "head", ring("head", -d)) for d in range(1, head_devices)
    ]
    gtok_near = send_near(gtok, "head")
    if first:
        late_far = send_far(late_parts, late_near, "head")
    late, edge = pl.pallas_call(
        functools.partial(merge_kernel, own_width),
        out_shape=[
            sds((chunk * seq_count, width), BF16), sds((rows, EDGE, own_width)),
        ],
        compiler_params=pltpu.CompilerParams(vmem_limit_bytes=62 * 2**20),
        cost_estimate=cost(2),
        name="merge",
    )(packed, state_parts[0], *state_pieces)
    late, gtok_near[0] = ordered(late, gtok_near[0])
    parts = lax.all_to_all(late.reshape(seq_count, chunk, -1), "seq", 0, 0, tiled=True)
    gtok_far = send_far(gtok, gtok_near, "head")
    parts, gtok_near = ordered(parts, gtok_near)
    output = rounded(own_tokens + add_up(branch, branch_near, []))
    from_next = shifted(edge, "seq", -1)[:, EDGE - K + 1 :]
    late = gather_sum(parts)
    late, gtok_far = ordered(late, gtok_far)
    token_sums = [add_up(gtok, gtok_near, gtok_far)]
    if first:
        token_sums.append(add_up(late_parts, late_near, late_far))
    own_cot = lax.dynamic_slice_in_dim(cotangent, column, own_width, 2).astype(F32)
    padding = jnp.zeros((rows, length - K + 1, own_width), F32)
    grad_tokens = (
        own_cot + jnp.concatenate(token_sums, axis=1)
        + jnp.concatenate([padding, from_next], axis=1)
    )
    outs = pl.pallas_call(
        functools.partial(unpack_kernel, own_width, head_count),
        out_shape=[
            sds((own_width,)), sds((width, 2, channels)), sds((2, own_state, width)),
            sds((head_count, width)), sds((K, channels)), sds((channels,)),
            sds((K, 2, own_state)), sds((2, own_state)), sds((head_count,)),
            sds((head_count,)), sds((head_count,)), sds((channels,)),
            sds((channels, width)),
        ],
        compiler_params=pltpu.CompilerParams(vmem_limit_bytes=62 * 2**20),
        cost_estimate=cost(4),
        name="unpack",
    )(late, early)
    outs = list(outs)
    outs[2] = outs[2].transpose(2, 0, 1)
    outs[3] = outs[3].T
    return (output, grad_tokens) + tuple(outs)


def solution(mesh):
    return jax.shard_map(
        on_device,
        mesh=mesh,
        in_specs=(
            P(None, "seq", None), P(None, "seq"), P(), P(None, None, "head"),
            P(None, None, "head"), P(None, "head"), P(None, "head"), P("head"),
            P(None, None, "head"), P(None, "head"), P("head"), P("head"), P("head"), P("head"),
            P("head", None), P(None, "seq", None),
        ),
        out_specs=(
            P(None, "seq", "head"), P(None, "seq", "head"), P("head"), P(None, None, "head"),
            P(None, None, "head"), P(None, "head"), P(None, "head"), P("head"),
            P(None, None, "head"), P(None, "head"), P("head"), P("head"), P("head"), P("head"),
            P("head", None),
        ),
        check_vma=False,
    )
```

```python
import functools

import jax
import jax.numpy as jnp
from jax import lax
from jax.experimental import pallas as pl
from jax.experimental.pallas import tpu as pltpu
from jax.sharding import PartitionSpec as P

K = 4
GROUP = 256
DI = 1536
WIDTH = 64
LANES = 128
EDGE = 16
EPSILON = 1e-05
HIGHEST = lax.Precision.HIGHEST
F32 = jnp.float32
BF16 = jnp.bfloat16
FAR = -1e30
PARAMS = pltpu.CompilerParams(
    dimension_semantics=("arbitrary", "arbitrary"), vmem_limit_bytes=62 * 2**20
)


def cost(microseconds):
    return pl.CostEstimate(
        flops=int(microseconds * 1e9), bytes_accessed=int(microseconds * 1e5), transcendentals=0
    )


def rounded(tensor):
    return tensor.astype(BF16)


def dot(a, b, exact=False):
    return jnp.dot(a, b, preferred_element_type=F32, precision=HIGHEST if exact else None)


def dot_nt(a, b, exact=False):
    return lax.dot_general(
        a, b, (((1,), (1,)), ((), ())), preferred_element_type=F32,
        precision=HIGHEST if exact else None,
    )


def dot_tn(a, b, exact=False):
    return lax.dot_general(
        a, b, (((0,), (0,)), ((), ())), preferred_element_type=F32,
        precision=HIGHEST if exact else None,
    )


def iota(shape, dim):
    return lax.broadcasted_iota(jnp.int32, shape, dim)


def halves(tensor):
    high = rounded(tensor)
    return high, rounded(tensor - high.astype(F32))


def expand(tensor, channels):
    both = jnp.concatenate(halves(tensor), axis=1)
    table = iota((2 * LANES, channels), 1) // WIDTH == iota((2 * LANES, channels), 0) % LANES
    return dot(both, table.astype(F32).astype(BF16))


def collect(tensor):
    channels = tensor.shape[1]
    table = iota((channels, LANES), 0) // WIDTH == iota((channels, LANES), 1)
    table = table.astype(F32).astype(BF16)
    high, low = halves(tensor)
    return dot(high, table) + dot(low, table)


def expand_row(row, channels):
    return expand(jnp.broadcast_to(row, (8, LANES)), channels)[:1]


def collect_row(row):
    return collect(jnp.broadcast_to(row, (8, row.shape[1])))[:1]


def triangle(compare):
    return compare(iota((GROUP, GROUP), 0), iota((GROUP, GROUP), 1)).astype(F32).astype(BF16)


def running_counts(marked):
    return dot(marked.astype(BF16), triangle(lambda i, j: i <= j))


def fade_of(cum, counts):
    return jnp.exp(cum[GROUP - 1 :, :]) * (counts[:1, GROUP - 1 :] == 0).astype(F32)


def pack_state(ref, state, fade):
    ref[:LANES, :] = state
    ref[LANES:, :] = jnp.broadcast_to(fade, (8, fade.shape[1]))


def fold_states(pieces):
    state = jnp.zeros((LANES, pieces[0].shape[1]), F32)
    for piece in reversed(pieces):
        state = piece[LANES : LANES + 1, :] * state + piece[:LANES, :]
    return state


def rms_scale(tokens):
    return lax.rsqrt(jnp.mean(tokens * tokens, axis=-1, keepdims=True) + EPSILON)


def head_parts(channels):
    for start in range(0, channels, LANES):
        width = min(LANES, channels - start)
        yield start, width, [start // WIDTH + i for i in range(width // WIDTH)]


def pair_kernel(later, own, other, pair, near):
    flag = later[0] == 1
    mine, theirs = own[...], other[...]
    first, second = jnp.where(flag, theirs, mine), jnp.where(flag, mine, theirs)
    fade = second[:, LANES : LANES + 1]
    pair[:, :LANES] = fade * first[:, :LANES] + second[:, :LANES]
    pair[:, LANES:] = first[:, LANES:] * second[:, LANES:]
    neutral = (iota(mine.shape, 1) >= LANES).astype(F32)
    near[...] = jnp.where(flag, theirs, neutral)


def prepare_kernel(
    tok, starts, state, conv, conv_bias, step, step_bias, decay, skip, conv_x, conv_x_bias,
    gain_in, gain_out, tail, message, norm_in, norm_out, hp, ci, wst, marked, turn,
):
    rows, length = starts.shape
    width = tok.shape[-1]
    own = state.shape[1]
    heads = step.shape[0]
    tail[:, :, :width] = tok[...]
    for line in range(rows):
        for group in range(length // GROUP):
            part = starts[line : line + 1, group * GROUP : (group + 1) * GROUP].astype(F32)
            marked[line, group] = jnp.broadcast_to(part, (8, GROUP))
        last = starts[line : line + 1, length - LANES :].astype(F32)
        column = jnp.broadcast_to(last, (LANES, LANES)).T
        tail[line, :, width:] = rounded(column[LANES - EDGE :])
    message[:, width:] = jnp.zeros((2 * own, LANES), BF16)
    taps = conv[...].astype(F32)
    for kind in range(2):
        message[kind * own : (kind + 1) * own, :width] = state[kind]
        turn[...] = jnp.zeros_like(turn)
        turn[:K, :own] = taps[:, kind, :]
        turn[K : K + 1, :own] = conv_bias[kind : kind + 1, :].astype(F32)
        message[kind * own : (kind + 1) * own, width:] = rounded(turn[...].T[:own])
    norm_in[...] = gain_in[...].reshape(1, -1)
    norm_out[...] = gain_out[...].reshape(1, -1)
    hp[...] = jnp.zeros_like(hp)
    for line, vector in enumerate((step_bias, decay, skip)):
        hp[line : line + 1, :heads] = vector[...].reshape(1, -1)
    ci[...] = jnp.zeros_like(ci)
    ci[:K, :] = conv_x[...].astype(F32)
    ci[K : K + 1, :] = conv_x_bias[...].astype(F32).reshape(1, -1)
    wst[...] = jnp.zeros_like(wst)
    wst[:heads, :] = step[...]


def project_kernel(tok, gain, win, wst, hp, normed, xpre, gate, spre, step, cum):
    channels = xpre.shape[-1]
    tokens = tok[...].astype(F32)
    row = rounded(tokens * rms_scale(tokens) * gain[...])
    normed[...] = row
    product = dot(row, win[...])
    xpre[...] = rounded(product[:, :channels])
    gate[...] = product[:, channels:]
    raw = dot_nt(row, wst[...]) + hp[0:1, :]
    sizes = jax.nn.softplus(raw)
    spre[...] = raw
    step[...] = sizes
    rates = sizes * -jnp.exp(hp[1:2, :])
    lower = triangle(lambda i, j: i >= j)
    high, rest = rounded(rates), rates - rounded(rates).astype(F32)
    middle, low = halves(rest)
    cum[...] = dot(lower, high) + dot(lower, middle) + dot(lower, low)


def convolve(ext, taps, runs):
    summed = taps[K : K + 1, :] + taps[K - 1 : K, :] * ext[pl.ds(EDGE, GROUP), :]
    for lag in range(1, K):
        summed = summed + (
            taps[K - 1 - lag : K - lag, :] * ext[pl.ds(EDGE - lag, GROUP), :]
        ) * runs[lag - 1]
    return summed


def edge_rows(halo, gain, width):
    tokens = halo[:, :width].astype(F32)
    return tokens, rounded(tokens * rms_scale(tokens) * gain[...])


def forward_kernel(count, *refs):
    pieces = refs[:count]
    (
        marked, normed, xpre, step, cum, win, halo, gain, ci,
        yin, xact, bc, spre, fresh, fades, message, halo_x, halo_s, run_out, ws, cs,
        ext_x, ext_s, ext_k, state, total,
    ) = refs[count:]
    group = pl.program_id(1)
    channels = xpre.shape[-1]
    width = normed.shape[-1]
    own = pieces[0].shape[0] // 2

    @pl.when((group == 0) & (pl.program_id(0) == 0))
    def _():
        for place, piece in enumerate(pieces):
            for kind in range(2):
                row = (kind * count + place) * own
                ws[row : row + own, :] = piece[kind * own : (kind + 1) * own, :width]
        taps = jnp.concatenate(
            [p[kind * own : (kind + 1) * own, width:] for kind in range(2) for p in pieces], axis=0
        )
        cs[...] = taps.astype(F32).T[:8]

    @pl.when(group == 0)
    def _():
        _, row = edge_rows(halo, gain, width)
        edge_x = rounded(dot(row, win[:, :channels]))
        edge_s = rounded(dot_nt(row, ws[...]))
        halo_x[...] = edge_x
        halo_s[...] = edge_s
        ext_x[pl.ds(0, EDGE), :] = edge_x.astype(F32)
        ext_s[pl.ds(0, EDGE), :] = edge_s.astype(F32)
        ext_k[pl.ds(0, EDGE), :] = 1.0 - halo[:, width:].astype(F32)
        state[...] = jnp.zeros_like(state)
        total[...] = jnp.ones_like(total)

    @pl.when(group > 0)
    def _():
        ext_x[pl.ds(0, EDGE), :] = ext_x[pl.ds(GROUP, EDGE), :]
        ext_s[pl.ds(0, EDGE), :] = ext_s[pl.ds(GROUP, EDGE), :]
        ext_k[pl.ds(0, EDGE), :] = ext_k[pl.ds(GROUP, EDGE), :]

    counts = running_counts(marked[...])
    counts_column = counts.T[:, :1]
    run1 = 1.0 - marked[...].T[:, :1]
    ext_k[pl.ds(EDGE, GROUP), :] = jnp.broadcast_to(run1, (GROUP, LANES))
    run2 = run1 * ext_k[pl.ds(EDGE - 1, GROUP), :1]
    run3 = run2 * ext_k[pl.ds(EDGE - 2, GROUP), :1]
    runs = (run1, run2, run3)
    lane = iota((GROUP, LANES), 1)
    run_out[...] = jnp.where(lane == 0, run1, jnp.where(lane == 1, run2, run3))
    state_pre = rounded(dot_nt(normed[...], ws[...]))
    spre[...] = state_pre
    ext_s[pl.ds(EDGE, GROUP), :] = state_pre.astype(F32)
    ext_x[pl.ds(EDGE, GROUP), :] = xpre[...].astype(F32)
    conv_x = convolve(ext_x, ci, runs)
    conv_s = convolve(ext_s, cs, runs)
    x = rounded(conv_x * jax.nn.sigmoid(conv_x))
    both = rounded(conv_s * jax.nn.sigmoid(conv_s))
    xact[...] = x
    bc[...] = both
    half = both.shape[1] // 2
    b, c = both[:, :half], both[:, half:]
    cums = cum[...]
    causal = iota((GROUP, GROUP), 0) >= iota((GROUP, GROUP), 1)
    mask = jnp.where(causal & (counts_column == counts[:1]), 0.0, FAR)
    scores = dot_nt(c, b)
    weighted = x.astype(F32) * expand(step[...], channels)
    scaled = rounded(weighted)
    cum_rows = cums.T
    for start, size, heads in head_parts(channels):
        part = scaled[:, start : start + size]
        results = []
        for head in heads:
            decay = jnp.exp(cums[:, head : head + 1] - cum_rows[head : head + 1, :] + mask)
            results.append(dot(rounded(scores * decay), part))
        if len(results) == 2:
            results = [jnp.where(iota((GROUP, size), 1) < WIDTH, results[0], results[1])]
        yin[:, start : start + size] = results[0]
    ending = (counts_column == counts[:1, GROUP - 1 :]).astype(F32)
    reach_end = jnp.exp(cums[GROUP - 1 :, :] - cums) * ending
    new = dot_tn(b, rounded(weighted * expand(reach_end, channels)))
    fresh[...] = new
    fade = expand_row(fade_of(cums, counts), channels)
    fades[...] = jnp.broadcast_to(fade, (8, channels))
    state[...] = fade * state[...] + new
    total[...] = total[...] * fade

    @pl.when(group == pl.num_programs(1) - 1)
    def _():
        pack_state(message, state[...], total[0:1, :])


def mix_kernel(count, *refs):
    pieces = refs[:count]
    (
        yin, x, c, gate, dn, cum, marked, gain, hp, fresh, fades,
        mixer, sums, states, state,
    ) = refs[count:]
    channels = x.shape[-1]

    @pl.when(pl.program_id(1) == 0)
    def _():
        state[...] = fold_states(pieces)

    counts = running_counts(marked[...])
    living = (counts.T[:, :1] == 0).astype(F32)
    now = state[...]
    states[...] = now
    reach = expand(jnp.exp(cum[...]) * living, channels)
    skip = expand_row(hp[2:3, :], channels)
    high, low = halves(now)
    reads = c[...]
    mixed = yin[...] + reach * (dot(reads, high) + dot(reads, low)) + skip * x[...].astype(F32)
    mixer[...] = mixed
    gates = gate[...]
    gated = mixed * (gates * jax.nn.sigmoid(gates))
    square = jnp.sum(gated * gated, axis=1, keepdims=True)
    cross = jnp.sum(gated * (dn[...] * gain[...]), axis=1, keepdims=True)
    lane = iota((GROUP, LANES), 1)
    sums[...] = jnp.where(lane == 0, square, cross).T[:8]
    state[...] = fades[0:1, :] * now + fresh[...]


def gate_kernel(count, *refs):
    pieces = refs[:count]
    (
        mixer, gate, dn, x, c, cum, marked, gain, hp, fades,
        dy, dgate, normed_out, entering, message, grad_gain, grad_skip, state, total,
    ) = refs[count:]
    channels = x.shape[-1]
    last = pl.program_id(1) == 0

    @pl.when(last & (pl.program_id(0) == 0))
    def _():
        grad_gain[...] = jnp.zeros_like(grad_gain)
        grad_skip[...] = jnp.zeros_like(grad_skip)

    @pl.when(last)
    def _():
        state[...] = jnp.zeros_like(state)
        total[...] = jnp.ones_like(total)

    sums = pieces[0][...]
    for piece in pieces[1:]:
        sums = sums + piece[...]
    columns = sums.T
    scale = lax.rsqrt(columns[:, 0:1] / DI + EPSILON)
    pull = scale * scale * scale * (columns[:, 1:2] / DI)
    counts = running_counts(marked[...])
    living = (counts.T[:, :1] == 0).astype(F32)
    mixed = mixer[...]
    gates = gate[...]
    squash = jax.nn.sigmoid(gates)
    act = gates * squash
    gated = mixed * act
    norm_grad = dn[...]
    grad_gated = scale * (norm_grad * gain[...]) - gated * pull
    down = grad_gated * act
    dy[...] = down
    dgate[...] = rounded(grad_gated * mixed * (squash * (1.0 + gates * (1.0 - squash))))
    scaled = gated * scale
    normed_out[...] = rounded(scaled * gain[...])
    grad_gain[...] += jnp.sum(norm_grad * scaled, axis=0, keepdims=True)
    grad_skip[...] += jnp.sum(down * x[...].astype(F32), axis=0, keepdims=True)
    reach = expand(jnp.exp(cum[...]) * living, channels)
    new = dot_tn(c[...], rounded(reach * down))
    entering[...] = new
    fade = fades[0:1, :]
    state[...] = fade * state[...] + new
    total[...] = total[...] * fade

    @pl.when(pl.program_id(1) == pl.num_programs(1) - 1)
    def _():
        pack_state(message, state[...], total[0:1, :])


def store_parts(refs, tensor, me):
    width = tensor.shape[1]
    own = width // len(refs)
    turned = rounded(pltpu.roll(tensor, (len(refs) - me) % len(refs) * own, 1))
    blocks = [turned[:, part * own : (part + 1) * own] for part in range(len(refs))]
    if len(refs) == 4:
        odd = me % 2 == 1
        swapped = [jnp.where(odd, blocks[4 - part], blocks[part]) for part in (1, 3)]
        blocks = [blocks[0], swapped[0], blocks[2], swapped[1]]
    for block, ref in zip(blocks, refs):
        ref[...] = block


def branch_kernel(me, normed_out, wout, *branch):
    store_parts(branch, dot(normed_out[...], wout[...]), me[0])


def out_kernel(normed_out, cot, dgate, normed, grads, total):
    channels = normed_out.shape[1]

    @pl.when((pl.program_id(1) == 0) & (pl.program_id(0) == 0))
    def _():
        total[...] = jnp.zeros_like(total)

    total[:channels, :] += dot_tn(normed_out[...], cot[...])
    total[channels : 2 * channels, :] += dot_tn(dgate[...], normed[...])

    @pl.when(
        (pl.program_id(1) == pl.num_programs(1) - 1)
        & (pl.program_id(0) == pl.num_programs(0) - 1)
    )
    def _():
        grads[...] = rounded(total[...])


def token_grad(tokens, gain, down):
    scale = rms_scale(tokens)
    pulled = down * gain
    inner = jnp.mean(pulled * tokens, axis=-1, keepdims=True)
    grad = scale * pulled - tokens * (scale * scale * scale * inner)
    return grad, jnp.sum(down * tokens * scale, axis=0, keepdims=True)


def deconvolve(ext, buffers, taps, runs, grad_out, grad_taps):
    rows = GROUP + EDGE
    grad_taps[K : K + 1, :] += jnp.sum(grad_out, axis=0, keepdims=True)
    result = None
    for lag in range(K):
        masked = grad_out if lag == 0 else grad_out * runs[lag - 1]
        buffer = buffers.at[lag]
        buffer[pl.ds(EDGE, GROUP), :] = masked
        tap = K - 1 - lag
        grad_taps[tap : tap + 1, :] += jnp.sum(
            masked * ext[pl.ds(EDGE - lag, GROUP), :], axis=0, keepdims=True
        )
        piece = taps[tap : tap + 1, :] * buffer[pl.ds(lag, rows), :]
        result = piece if result is None else result + piece
        buffer[pl.ds(EDGE + GROUP, 8), :] = masked[:8]
    return rounded(result)


def swish_slope(tensor):
    squash = jax.nn.sigmoid(tensor)
    return squash * (1.0 + tensor * (1.0 - squash))


def backward_kernel(start_call, end_call, count, parts, *refs):
    pieces, refs = refs[:count], refs[count:]
    carried, refs = (refs[:0], refs) if start_call else (refs[:6], refs[6:])
    (
        me, tok, halo, marked, normed, xpre, xprev, halo_x, spre, sprev, halo_s, xact, bc, yin, dy,
        back, step, cum, raw, run_in, states, entering, fades, win, ws, wst, hp, ci, cs, gain, gain_out, skip_out,
    ), refs = refs[:32], refs[32:]
    gtok, refs = refs[:parts], refs[parts:]
    if end_call:
        (packed, *state_out), refs = refs[: 1 + parts], refs[1 + parts :]
    else:
        carry_out, refs = refs[:6], refs[6:]
    (
        ext_x, ext_s, buf_x, buf_s, state, grad_x, grad_s, grad_misc, grad_ci, grad_cs, edges,
    ) = refs
    channels = xact.shape[-1]
    width = tok.shape[-1]
    half = bc.shape[-1] // 2
    order = pl.program_id(1)
    row_id = pl.program_id(0)
    closing = order == pl.num_programs(1) - 1
    sums = (grad_x, grad_s, grad_misc, grad_ci, grad_cs)

    @pl.when((order == 0) & (row_id == 0))
    def _():
        if start_call:
            for ref in sums:
                ref[...] = jnp.zeros_like(ref)
        else:
            grad_x[...] = carried[3][:channels]
            grad_s[...] = carried[3][channels : channels + 2 * half]
            grad_misc[...] = carried[3][channels + 2 * half :]
            grad_ci[...] = carried[4][...]
            grad_cs[...] = carried[5][...]

    @pl.when(order == 0)
    def _():
        for buf in (buf_x, buf_s):
            buf[...] = jnp.zeros_like(buf)
        if start_call:
            state[...] = fold_states(pieces)
        else:
            state[...] = carried[0][...]
            buf_x[:, pl.ds(EDGE + GROUP, 8), :] = carried[1][...]
            buf_s[:, pl.ds(EDGE + GROUP, 8), :] = carried[2][...]

    first_group = closing if end_call else False
    ext_x[pl.ds(EDGE, GROUP), :] = xpre[...].astype(F32)
    ext_s[pl.ds(EDGE, GROUP), :] = spre[...].astype(F32)
    before_x, before_s = xprev[...].astype(F32), sprev[...].astype(F32)
    if end_call:
        before_x = jnp.where(first_group, halo_x[...].astype(F32), before_x)
        before_s = jnp.where(first_group, halo_s[...].astype(F32), before_s)
    ext_x[pl.ds(0, EDGE), :] = before_x
    ext_s[pl.ds(0, EDGE), :] = before_s

    counts = running_counts(marked[...])
    counts_column = counts.T[:, :1]
    runs = [run_in[:, lag : lag + 1] for lag in range(K - 1)]
    living = (counts_column == 0).astype(F32)
    x = xact[...].astype(F32)
    both = bc[...]
    b, c = both[:, :half], both[:, half:]
    cums = cum[...]
    cum_rows = cums.T
    steps = step[...]
    step_wide = expand(steps, channels)
    weighted = x * step_wide
    scaled = rounded(weighted)
    down = dy[...]
    down_low = rounded(down)
    causal = iota((GROUP, GROUP), 0) <= iota((GROUP, GROUP), 1)
    mask = jnp.where(causal & (counts_column == counts[:1]), 0.0, FAR)
    scores = dot_nt(b, c)
    grad_scores = jnp.zeros((GROUP, GROUP), F32)
    inside = []
    for start, size, heads in head_parts(channels):
        part = scaled[:, start : start + size]
        slope = down_low[:, start : start + size]
        lane = iota((GROUP, size), 1)
        results = []
        for place, head in enumerate(heads):
            decay = jnp.exp(cum_rows[head : head + 1, :] - cums[:, head : head + 1] + mask)
            results.append(dot(rounded(scores * decay), slope))
            own = part
            if len(heads) == 2:
                keep = (lane < WIDTH) if place == 0 else (lane >= WIDTH)
                own = jnp.where(keep, part, jnp.zeros_like(part))
            grad_scores = grad_scores + dot_nt(own, slope) * decay
        if len(results) == 2:
            results = [jnp.where(lane < WIDTH, results[0], results[1])]
        inside.append(results[0])
    inside = jnp.concatenate(inside, axis=1) if len(inside) > 1 else inside[0]

    later = state[...]
    later_high, later_low = halves(later)
    now = states[...]
    now_high, now_low = halves(now)
    ending = (counts_column == counts[:1, GROUP - 1 :]).astype(F32)
    reach_end = expand(jnp.exp(cums[GROUP - 1 :, :] - cums) * ending, channels)
    reach = expand(jnp.exp(cums) * living, channels)
    arriving = reach_end * (dot(b, later_high) + dot(b, later_low))
    grad_weighted = inside + arriving
    reached = reach * down
    outside = reached * (dot(c, now_high) + dot(c, now_low))
    fade = fades[0:1, :]
    fade_grad = collect_row(fade * jnp.sum(later * now, axis=0, keepdims=True))
    per_position = collect(
        down_low.astype(F32) * yin[...] - scaled.astype(F32) * inside + outside
    )
    per_ending = collect(weighted * arriving)
    direct = collect(x * grad_weighted)
    position_high, position_low = halves(per_position)
    ending_high, ending_low = halves(per_ending)
    upper = triangle(lambda i, j: i <= j)
    under = triangle(lambda i, j: i > j)
    grad_rate = (
        dot(upper, position_high) + dot(upper, position_low)
        + dot(under, ending_high) + dot(under, ending_low) + fade_grad
    )
    rate = -jnp.exp(hp[1:2, :])
    grad_pre = (direct + rate * grad_rate) * jax.nn.sigmoid(raw[...])
    grad_raw = rounded(grad_pre)
    skip = expand_row(hp[2:3, :], channels)
    grad_inputs = step_wide * grad_weighted + skip * down
    low_scores = rounded(grad_scores)
    ended = rounded(weighted * reach_end)
    reached_low = rounded(reached)
    grad_b = dot(low_scores, c) + dot_nt(ended, later_high) + dot_nt(ended, later_low)
    grad_c = dot_tn(low_scores, b) + dot_nt(reached_low, now_high) + dot_nt(reached_low, now_low)
    state[...] = fade * later + entering[...]

    conv_x = convolve(ext_x, ci, runs)
    grad_x_out = grad_inputs * swish_slope(conv_x)
    conv_s = convolve(ext_s, cs, runs)
    grad_s_out = jnp.concatenate([grad_b, grad_c], axis=1) * swish_slope(conv_s)
    back_x = deconvolve(ext_x, buf_x, ci, runs, grad_x_out, grad_ci)
    back_s = deconvolve(ext_s, buf_s, cs, runs, grad_s_out, grad_cs)
    row = normed[...]
    main_x, main_s = back_x[EDGE:], back_s[EDGE:]
    grad_x[...] += dot_tn(main_x, row)
    grad_s[...] += dot_tn(main_s, row)
    grad_normed = (
        dot_nt(jnp.concatenate([main_x, back[...]], axis=1), win[...]) + dot(main_s, ws[...])
        + dot(grad_raw, wst[...])
    )
    grad, gain_part = token_grad(tok[...].astype(F32), gain[...], grad_normed)
    grad_misc[0:8, :] += dot_tn(grad_raw, row)[:8]
    grad_misc[8:9, :] += gain_part
    grad_misc[9:10, :LANES] += jnp.sum(grad_pre, axis=0, keepdims=True)
    grad_misc[10:11, :LANES] += rate * jnp.sum(steps * grad_rate, axis=0, keepdims=True)
    store_parts(gtok, grad, me[0])

    if not end_call:
        @pl.when(closing)
        def _():
            carry_out[0][...] = state[...]
            carry_out[1][...] = buf_x[:, pl.ds(EDGE + GROUP, 8), :]
            carry_out[2][...] = buf_s[:, pl.ds(EDGE + GROUP, 8), :]

            @pl.when(row_id == pl.num_programs(0) - 1)
            def _():
                carry_out[3][:channels] = grad_x[...]
                carry_out[3][channels : channels + 2 * half] = grad_s[...]
                carry_out[3][channels + 2 * half :] = grad_misc[...]
                carry_out[4][...] = grad_ci[...]
                carry_out[5][...] = grad_cs[...]
        return

    @pl.when(closing)
    def _():
        tokens, edge_row = edge_rows(halo, gain, width)
        edge_x, edge_s = back_x[:EDGE], back_s[:EDGE]
        grad_x[...] += dot_tn(edge_x, edge_row)
        grad_s[...] += dot_tn(edge_s, edge_row)
        edge_grad = dot_nt(edge_x, win[:, :channels]) + dot(edge_s, ws[...])
        grad, gain_part = token_grad(tokens, gain[...], edge_grad)
        grad_misc[8:9, :] += gain_part
        everything = grad_misc[8:9, :]
        high = everything.astype(BF16).astype(F32)
        place = iota((EDGE, 1), 0)
        final = row_id == pl.num_programs(0) - 1
        nothing = jnp.zeros_like(high)
        high, rest = jnp.where(final, high, nothing), jnp.where(final, everything - high, nothing)
        edge = jnp.where(place == 0, high, jnp.where(place == 1, rest, grad))
        edges[row_id] = edge

        @pl.when(final)
        def _():
            def padded(block):
                if block.shape[1] == width:
                    return block
                blank = jnp.zeros((8, width - block.shape[1]), F32)
                return jnp.concatenate([block, blank], axis=1)

            def both_halves(block):
                whole = padded(block)
                upper_half = whole.astype(BF16).astype(F32)
                return rounded(jnp.concatenate([upper_half, whole - upper_half], axis=0))

            packed[:channels, :] = rounded(grad_x[...])
            misc = grad_misc[...]
            fine = misc - misc.astype(BF16).astype(F32)
            packed[channels : channels + EDGE, :] = rounded(
                jnp.concatenate([misc[:11], fine[9:11], misc[13:]], axis=0)
            )
            grad_ci[K + 1 : K + 2, :] = gain_out[...]
            grad_ci[K + 2 : K + 3, :LANES] = collect_row(skip_out[...])
            packed[channels + EDGE : channels + 2 * EDGE, :] = both_halves(grad_ci[...])
            own = half // parts
            taps = grad_cs[...]
            for part, ref in enumerate(state_out):
                lo, hi = part * own, (part + 1) * own
                ref[:own, :] = rounded(grad_s[lo:hi, :])
                ref[own : 2 * own, :] = rounded(grad_s[half + lo : half + hi, :])
                ref[2 * own :, :] = both_halves(
                    jnp.concatenate([taps[:, lo:hi], taps[:, half + lo : half + hi]], axis=1)
                )
            own = width // parts
            for line in range(edges.shape[0]):
                shift = (parts - me[0]) % parts * own
                turned = rounded(pltpu.roll(edges[line], shift, 1))
                for part, ref in enumerate(state_out):
                    begin = (parts - part) % parts * own
                    ref[2 * (half // parts) :, LANES + line * own : LANES + (line + 1) * own] = (
                        turned[:, begin : begin + own]
                    )


def merge_kernel(own_width, packed, *refs):
    *pieces, late, edge = refs
    base = packed.shape[0]
    total = pieces[0][...].astype(F32)
    for piece in pieces[1:]:
        total = total + piece[...].astype(F32)
    body = total.shape[0] - EDGE
    rows = edge.shape[0]
    late[:base, :] = packed[...]
    late[base : base + body, :] = rounded(total[:body])
    tail = total[body:]
    for line in range(rows):
        edge[line] = tail[:, LANES + line * own_width : LANES + (line + 1) * own_width]

    def both_halves(block):
        upper_half = block.astype(BF16).astype(F32)
        return jnp.concatenate([upper_half, block - upper_half], axis=0)

    place = base + body
    late[place : place + EDGE, :] = rounded(both_halves(tail[:8] + tail[8:]))
    place += EDGE
    begin = LANES + (rows - 1) * own_width
    gain = jnp.broadcast_to(tail[0:1] + tail[1:2], (8, tail.shape[1]))
    late[place : place + EDGE, :] = jnp.zeros((EDGE, tail.shape[1]), BF16)
    late[place : place + EDGE, :own_width] = rounded(both_halves(gain))[:, begin : begin + own_width]
    if late.shape[0] > place + EDGE:
        rest = late.shape[0] - place - EDGE
        late[place + EDGE :, :] = jnp.zeros((rest, tail.shape[1]), BF16)


def unpack_kernel(
    own_width, head_count, late, early, gain, inner, state, step, conv, conv_bias, taps,
    taps_bias, step_bias, decay, skip, gain_out, out_weight,
):
    channels, width = out_weight.shape
    own = state.shape[1]
    inner[:, 0, :] = late[:channels, :].astype(F32).T
    inner[:, 1, :] = early[channels : 2 * channels, :].astype(F32).T
    base = channels
    misc = late[base : base + EDGE, :].astype(F32)
    step[...] = misc[:head_count]
    step_bias[...] = (misc[9] + misc[11])[:head_count]
    decay[...] = (misc[10] + misc[12])[:head_count]
    base += EDGE
    block = late[base : base + EDGE, :].astype(F32)
    block = block[:8] + block[8:]
    conv[...] = block[:K, :channels]
    conv_bias[...] = block[K, :channels]
    gain_out[...] = block[K + 1, :channels]
    skip[...] = block[K + 2, :head_count]
    base += EDGE
    state[0] = late[base : base + own, :].astype(F32)
    state[1] = late[base + own : base + 2 * own, :].astype(F32)
    base += 2 * own
    block = late[base : base + EDGE, :].astype(F32)
    block = block[:8] + block[8:]
    taps[:, 0, :] = block[:K, :own]
    taps[:, 1, :] = block[:K, own : 2 * own]
    taps_bias[0:1, :] = block[K : K + 1, :own]
    taps_bias[1:2, :] = block[K : K + 1, own : 2 * own]
    base += EDGE
    block = late[base : base + EDGE, :].astype(F32)
    gain[...] = (block[0] + block[8])[:own_width]
    out_weight[...] = early[:channels, :].astype(F32)


def ring(axis, distance):
    count = lax.axis_size(axis)
    return [(i, (i + distance) % count) for i in range(count)]


def shifted(block, axis, distance):
    devices = range(lax.axis_size(axis))
    return lax.ppermute(block, axis, [(i - distance, i) for i in devices if i - distance in devices])


def crossed(block, axis, mask):
    return lax.ppermute(block, axis, [(i, i ^ mask) for i in range(lax.axis_size(axis))])


def send_near(parts, axis):
    if len(parts) == 4:
        return [crossed(parts[3], axis, 1), crossed(parts[1], axis, 1)]
    return [lax.ppermute(part, axis, ring(axis, d)) for d, part in enumerate(parts[1:], 1)]


def send_far(parts, near, axis):
    if len(parts) == 4:
        return [crossed(rounded(parts[2].astype(F32) + near[0].astype(F32)), axis, 2)]
    return []


def send_all(parts, axis):
    if len(parts) == 4:
        return [crossed(part, axis, mask) for mask, part in enumerate(parts) if mask]
    return send_near(parts, axis)


def add_up(parts, near, far):
    total = parts[0].astype(F32)
    for piece in (near[1:] if far else near) + far:
        total = total + piece.astype(F32)
    return total


def ordered(*groups):
    flat, tree = jax.tree.flatten(groups)
    return jax.tree.unflatten(tree, lax.optimization_barrier(flat))


def chained(message, reverse, beside):
    count = lax.axis_size("seq")
    core = lax.axis_index("seq") % 2
    later = core == (0 if reverse else 1)
    other = crossed(message, "seq", 1)
    pair, near = pl.pallas_call(
        pair_kernel,
        in_specs=[pl.BlockSpec(memory_space=pltpu.SMEM)]
        + [pl.BlockSpec(memory_space=pltpu.VMEM)] * 2,
        out_shape=[jax.ShapeDtypeStruct(message.shape, F32)] * 2,
        compiler_params=pltpu.CompilerParams(vmem_limit_bytes=62 * 2**20),
        cost_estimate=cost(1),
        name="pair",
    )(later.astype(jnp.int32).reshape(1), message, other)
    sign = -2 if reverse else 2
    pair, beside = ordered(pair, beside)
    return beside, [near] + [shifted(pair, "seq", sign * d) for d in range(1, count // 2)]


def gather_sum(parts):
    total = rounded(jnp.sum(parts.astype(F32), axis=0))
    return lax.all_gather(total, "seq", axis=0, tiled=True)


def on_device(
    tokens, starts, norm_in_gain, inner_weight, state_weight, step_weight, conv_inner,
    conv_inner_bias, conv_state, conv_state_bias, step_bias, decay_log, skip_gain,
    norm_out_gain, out_weight, cotangent,
):
    rows, length, width = tokens.shape
    head_count = step_weight.shape[1]
    channels = inner_weight.shape[2]
    own_state = state_weight.shape[2]
    seq_count, head_devices = lax.axis_size("seq"), lax.axis_size("head")
    groups = length // GROUP
    grid = (rows, groups)
    states = 2 * own_state * head_devices
    own_width = width // head_devices
    me = lax.axis_index("head").reshape(1)

    def sds(shape, dtype=F32):
        return jax.ShapeDtypeStruct(shape, dtype)

    def whole(shape):
        return pl.BlockSpec(shape, lambda r, g: (0,) * len(shape))

    def place(g, reverse):
        return groups - 1 - g if reverse else g

    def block(cols, reverse=False, part=0):
        return pl.BlockSpec((None, GROUP, cols), lambda r, g: (r, place(g, reverse), part))

    def per_row(height, cols):
        return pl.BlockSpec((None, height, cols), lambda r, g: (r, 0, 0))

    def per_group(height, cols, reverse=False):
        return pl.BlockSpec(
            (None, None, height, cols), lambda r, g: (r, place(g, reverse), 0, 0)
        )

    scalar = pl.BlockSpec(memory_space=pltpu.SMEM)
    halo_width = width + LANES
    tail, state_own, gain_in, gain_out, hp, ci, wst, marked = pl.pallas_call(
        prepare_kernel,
        grid=(1,),
        in_specs=[
            pl.BlockSpec((rows, EDGE, width), lambda i: (0, length // EDGE - 1, 0)),
        ] + [pl.BlockSpec(memory_space=pltpu.VMEM)] * 12,
        out_specs=[pl.BlockSpec(memory_space=pltpu.VMEM)] * 8,
        out_shape=[
            sds((rows, EDGE, halo_width), BF16), sds((2 * own_state, halo_width), BF16),
            sds((1, width)), sds((1, channels)), sds((8, LANES)), sds((8, channels)),
            sds((LANES, width), BF16), sds((rows, groups, 8, GROUP)),
        ],
        scratch_shapes=[pltpu.VMEM((LANES, LANES), F32)],
        compiler_params=pltpu.CompilerParams(vmem_limit_bytes=62 * 2**20),
        cost_estimate=cost(2),
        name="prepare",
    )(
        tokens, starts, state_weight.transpose(1, 2, 0), conv_state, conv_state_bias,
        step_weight.T, step_bias, decay_log, skip_gain, conv_inner, conv_inner_bias,
        norm_in_gain, norm_out_gain,
    )
    halo = shifted(tail, "seq", 1)
    found = [state_own] + [
        lax.ppermute(state_own, "head", ring("head", d)) for d in range(1, head_devices)
    ]

    win = inner_weight.reshape(width, 2 * channels)

    def act(cols, dtype=F32):
        return sds((rows, length, cols), dtype)

    normed, xpre, gate, raw, step, cum = pl.pallas_call(
        project_kernel,
        grid=grid,
        in_specs=[
            block(width), whole((1, width)), whole((width, 2 * channels)),
            whole((LANES, width)), whole((8, LANES)),
        ],
        out_specs=[
            block(width), block(channels), block(channels), block(LANES), block(LANES),
            block(LANES),
        ],
        out_shape=[
            act(width, BF16), act(channels, BF16), act(channels), act(LANES), act(LANES),
            act(LANES),
        ],
        compiler_params=PARAMS,
        name="project",
        cost_estimate=cost(6),
    )(tokens, gain_in, win, wst, hp)
    (
        yin, xact, bc, spre, fresh, fades, message, halo_x, halo_s, run_all, ws, cs,
    ) = pl.pallas_call(
        functools.partial(forward_kernel, len(found)),
        grid=grid,
        in_specs=[whole((2 * own_state, width + LANES))] * len(found) + [
            per_group(8, GROUP), block(width), block(channels), block(LANES), block(LANES),
            whole((width, 2 * channels)), per_row(EDGE, halo_width), whole((1, width)),
            whole((8, channels)),
        ],
        out_specs=[
            block(channels), block(channels), block(states), block(states),
            per_group(LANES, channels), per_group(8, channels), per_row(LANES + 8, channels),
            per_row(EDGE, channels), per_row(EDGE, states), block(LANES),
            whole((states, width)), whole((8, states)),
        ],
        out_shape=[
            act(channels), act(channels, BF16), act(states, BF16), act(states, BF16),
            sds((rows, groups, LANES, channels)), sds((rows, groups, 8, channels)),
            sds((rows, LANES + 8, channels)), sds((rows, EDGE, channels), BF16),
            sds((rows, EDGE, states), BF16), act(LANES), sds((states, width), BF16),
            sds((8, states)),
        ],
        scratch_shapes=[
            pltpu.VMEM((GROUP + EDGE, channels), F32), pltpu.VMEM((GROUP + EDGE, states), F32),
            pltpu.VMEM((GROUP + EDGE, LANES), F32),
            pltpu.VMEM((LANES, channels), F32), pltpu.VMEM((8, channels), F32),
        ],
        compiler_params=PARAMS,
        name="forward",
        cost_estimate=cost(10),
    )(*found, marked, normed, xpre, step, cum, win, halo, gain_in, ci)

    beside, arrived = chained(message, False, cotangent)
    dn = jnp.einsum("rsd,cd->rsc", beside, out_weight, preferred_element_type=F32)
    mixer, sums, entry_states = pl.pallas_call(
        functools.partial(mix_kernel, len(arrived)),
        grid=grid,
        in_specs=[per_row(LANES + 8, channels)] * len(arrived) + [
            block(channels), block(channels), block(states // 2, part=1), block(channels),
            block(channels), block(LANES), per_group(8, GROUP), whole((1, channels)),
            whole((8, LANES)), per_group(LANES, channels), per_group(8, channels),
        ],
        out_specs=[block(channels), per_group(8, GROUP), per_group(LANES, channels)],
        out_shape=[
            act(channels), sds((rows, groups, 8, GROUP)), sds((rows, groups, LANES, channels)),
        ],
        scratch_shapes=[pltpu.VMEM((LANES, channels), F32)],
        compiler_params=PARAMS,
        name="mix",
        cost_estimate=cost(6),
    )(*arrived, yin, xact, bc, gate, dn, cum, marked, gain_out, hp, fresh, fades)

    sums_all = [sums] + [
        lax.ppermute(sums, "head", ring("head", d)) for d in range(1, head_devices)
    ]
    dy, dgate, normed_out, entering, back_message, grad_gain_out, grad_skip = pl.pallas_call(
        functools.partial(gate_kernel, len(sums_all)),
        grid=grid,
        in_specs=[per_group(8, GROUP, True)] * len(sums_all) + [
            block(channels, True), block(channels, True), block(channels, True),
            block(channels, True), block(states // 2, True, 1), block(LANES, True),
            per_group(8, GROUP, True), whole((1, channels)), whole((8, LANES)),
            per_group(8, channels, True),
        ],
        out_specs=[
            block(channels, True), block(channels, True), block(channels, True),
            per_group(LANES, channels, True), per_row(LANES + 8, channels),
            whole((1, channels)), whole((1, channels)),
        ],
        out_shape=[
            act(channels), act(channels, BF16), act(channels, BF16),
            sds((rows, groups, LANES, channels)), sds((rows, LANES + 8, channels)),
            sds((1, channels)), sds((1, channels)),
        ],
        scratch_shapes=[pltpu.VMEM((LANES, channels), F32), pltpu.VMEM((8, channels), F32)],
        compiler_params=PARAMS,
        name="gate",
        cost_estimate=cost(6),
    )(*sums_all, mixer, gate, dn, xact, bc, cum, marked, gain_out, hp, fades)

    branch = pl.pallas_call(
        branch_kernel,
        grid=grid,
        in_specs=[scalar, block(channels), whole((channels, width))],
        out_specs=[block(own_width)] * head_devices,
        out_shape=[act(own_width, BF16)] * head_devices,
        compiler_params=PARAMS,
        cost_estimate=cost(3),
        name="branch",
    )(me, normed_out, out_weight)
    branch_near = send_all(branch, "head")
    normed_out, returned = chained(back_message, True, normed_out)
    early = pl.pallas_call(
        out_kernel,
        grid=grid,
        in_specs=[block(channels), block(width), block(channels), block(width)],
        out_specs=whole((2 * channels, width)),
        out_shape=sds((2 * channels, width), BF16),
        scratch_shapes=[pltpu.VMEM((2 * channels, width), F32)],
        compiler_params=PARAMS,
        cost_estimate=cost(5),
        name="out",
    )(normed_out, cotangent, dgate, normed)

    column = lax.axis_index("head") * own_width
    own_tokens = lax.dynamic_slice_in_dim(tokens, column, own_width, 2).astype(F32)

    early = lax.all_to_all(early.reshape(seq_count, -1, width), "seq", 0, 0, tiled=True)

    late_rows = channels + 3 * EDGE + 2 * own_state + EDGE
    chunk = -(-late_rows // (seq_count * EDGE)) * EDGE
    packed_rows = channels + 2 * EDGE
    piece_rows = 2 * own_state + EDGE

    def backward_call(start_call, end_call, offset, steps, carried):
        step_size = GROUP // EDGE

        def at(g):
            return offset + steps - 1 - g

        def tile(cols):
            return pl.BlockSpec((None, GROUP, cols), lambda r, g: (r, at(g), 0))

        def before(cols):
            return pl.BlockSpec(
                (None, EDGE, cols), lambda r, g: (r, jnp.maximum(at(g) * step_size - 1, 0), 0)
            )

        def group_tile(height, cols):
            return pl.BlockSpec((None, None, height, cols), lambda r, g: (r, at(g), 0, 0))

        carry_specs = [
            per_row(LANES, channels),
            pl.BlockSpec((None, K, 8, channels), lambda r, g: (r, 0, 0, 0)),
            pl.BlockSpec((None, K, 8, states), lambda r, g: (r, 0, 0, 0)),
            whole((channels + states + EDGE, width)), whole((8, channels)), whole((8, states)),
        ]
        carry_shapes = [
            sds((rows, LANES, channels)), sds((rows, K, 8, channels)), sds((rows, K, 8, states)),
            sds((channels + states + EDGE, width)), sds((8, channels)), sds((8, states)),
        ]
        local = pl.BlockSpec((None, GROUP, own_width), lambda r, g: (r, steps - 1 - g, 0))
        out_specs = [local] * head_devices
        out_shape = [sds((rows, steps * GROUP, own_width), BF16)] * head_devices
        if end_call:
            out_specs += [whole((packed_rows, width))]
            out_specs += [whole((piece_rows, width))] * head_devices
            out_shape += [sds((packed_rows, width), BF16)]
            out_shape += [sds((piece_rows, width), BF16)] * head_devices
        else:
            out_specs += carry_specs
            out_shape += carry_shapes
        lead = returned if start_call else []
        return pl.pallas_call(
            functools.partial(backward_kernel, start_call, end_call, len(lead), head_devices),
            grid=(rows, steps),
            in_specs=[per_row(LANES + 8, channels)] * len(lead)
            + ([] if start_call else carry_specs)
            + [
                scalar, tile(width), per_row(EDGE, halo_width), group_tile(8, GROUP), tile(width),
                tile(channels), before(channels), per_row(EDGE, channels), tile(states),
                before(states), per_row(EDGE, states), tile(channels), tile(states),
                tile(channels), tile(channels), tile(channels), tile(LANES), tile(LANES),
                tile(LANES), tile(LANES), group_tile(LANES, channels),
                group_tile(LANES, channels), group_tile(8, channels),
                whole((width, 2 * channels)), whole((states, width)), whole((LANES, width)),
                whole((8, LANES)), whole((8, channels)), whole((8, states)), whole((1, width)),
                whole((1, channels)), whole((1, channels)),
            ],
            out_specs=out_specs,
            out_shape=out_shape,
            scratch_shapes=[
                pltpu.VMEM((GROUP + EDGE, channels), F32),
                pltpu.VMEM((GROUP + EDGE, states), F32),
                pltpu.VMEM((K, GROUP + 2 * EDGE, channels), F32),
                pltpu.VMEM((K, GROUP + 2 * EDGE, states), F32),
                pltpu.VMEM((LANES, channels), F32),
                pltpu.VMEM((channels, width), F32), pltpu.VMEM((states, width), F32),
                pltpu.VMEM((EDGE, width), F32), pltpu.VMEM((8, channels), F32),
                pltpu.VMEM((8, states), F32), pltpu.VMEM((rows, EDGE, width), F32),
            ],
            compiler_params=PARAMS,
            name="backward",
            cost_estimate=cost(15),
        )(
            *lead, *carried, me, tokens, halo, marked, normed, xpre, xpre, halo_x, spre, spre,
            halo_s, xact, bc, yin, dy, dgate, step, cum, raw, run_all, entry_states, entering,
            fades, win, ws, wst, hp, ci, cs, gain_in, grad_gain_out, grad_skip,
        )

    first = min(1, groups // 2)
    if first:
        outs = backward_call(True, False, first, groups - first, [])
        outs, early = ordered(outs, early)
        early = gather_sum(early)
        late_parts, carried = outs[:head_devices], outs[head_devices:]
        late_near = send_near(late_parts, "head")
        outs = backward_call(False, True, 0, first, carried)
        outs, branch_near, late_near = ordered(outs, branch_near, late_near)
    else:
        outs = backward_call(True, True, 0, groups, [])
        early = gather_sum(early)
    gtok, packed = outs[:head_devices], outs[head_devices]
    state_parts = outs[head_devices + 1 :]
    state_pieces = [
        lax.ppermute(state_parts[d], "head", ring("head", -d)) for d in range(1, head_devices)
    ]
    gtok_near = send_near(gtok, "head")
    if first:
        late_far = send_far(late_parts, late_near, "head")
    late, edge = pl.pallas_call(
        functools.partial(merge_kernel, own_width),
        out_shape=[
            sds((chunk * seq_count, width), BF16), sds((rows, EDGE, own_width)),
        ],
        compiler_params=pltpu.CompilerParams(vmem_limit_bytes=62 * 2**20),
        cost_estimate=cost(2),
        name="merge",
    )(packed, state_parts[0], *state_pieces)
    late, gtok_near[0] = ordered(late, gtok_near[0])
    parts = lax.all_to_all(late.reshape(seq_count, chunk, -1), "seq", 0, 0, tiled=True)
    gtok_far = send_far(gtok, gtok_near, "head")
    parts, gtok_near = ordered(parts, gtok_near)
    output = rounded(own_tokens + add_up(branch, branch_near, []))
    from_next = shifted(edge, "seq", -1)[:, EDGE - K + 1 :]
    late = gather_sum(parts)
    late, gtok_far = ordered(late, gtok_far)
    token_sums = [add_up(gtok, gtok_near, gtok_far)]
    if first:
        token_sums.append(add_up(late_parts, late_near, late_far))
    own_cot = lax.dynamic_slice_in_dim(cotangent, column, own_width, 2).astype(F32)
    padding = jnp.zeros((rows, length - K + 1, own_width), F32)
    grad_tokens = (
        own_cot + jnp.concatenate(token_sums, axis=1)
        + jnp.concatenate([padding, from_next], axis=1)
    )
    outs = pl.pallas_call(
        functools.partial(unpack_kernel, own_width, head_count),
        out_shape=[
            sds((own_width,)), sds((width, 2, channels)), sds((2, own_state, width)),
            sds((head_count, width)), sds((K, channels)), sds((channels,)),
            sds((K, 2, own_state)), sds((2, own_state)), sds((head_count,)),
            sds((head_count,)), sds((head_count,)), sds((channels,)),
            sds((channels, width)),
        ],
        compiler_params=pltpu.CompilerParams(vmem_limit_bytes=62 * 2**20),
        cost_estimate=cost(4),
        name="unpack",
    )(late, early)
    outs = list(outs)
    outs[2] = outs[2].transpose(2, 0, 1)
    outs[3] = outs[3].T
    return (output, grad_tokens) + tuple(outs)


def solution(mesh):
    return jax.shard_map(
        on_device,
        mesh=mesh,
        in_specs=(
            P(None, "seq", None), P(None, "seq"), P(), P(None, None, "head"),
            P(None, None, "head"), P(None, "head"), P(None, "head"), P("head"),
            P(None, None, "head"), P(None, "head"), P("head"), P("head"), P("head"), P("head"),
            P("head", None), P(None, "seq", None),
        ),
        out_specs=(
            P(None, "seq", "head"), P(None, "seq", "head"), P("head"), P(None, None, "head"),
            P(None, None, "head"), P(None, "head"), P(None, "head"), P("head"),
            P(None, None, "head"), P(None, "head"), P("head"), P("head"), P("head"), P("head"),
            P("head", None),
        ),
        check_vma=False,
    )
```
